32 devices in a mesh: parts: 2 (over x), wide: 16 (over z, y, core).
Axes of the slice: x: 2, y: 2, z: 4, core: 2. Of those that a mesh axis runs over, the one named last changes fastest.
Arguments:
- inputs: bfloat16 [3, 32768, 128], P(None, ('parts', 'wide')), parts along dimension 1, may hold values from -3 to 3
- state_init: float32 [32768, 128], P(('parts', 'wide')), parts along dimension 0, may hold values from -3 to 3
- cotangent: bfloat16 [3, 32768, 128], P(None, ('parts', 'wide')), parts along dimension 1, may hold values from -1.796875 to 1.796875
- gate_w: bfloat16 [768, 256], replicated, may hold values from -0.21875 to 0.21875
- gate_b: float32 [256], replicated, may hold values from -3 to 3
- cand_w: bfloat16 [768, 128], replicated, may hold values from -0.21875 to 0.21875
- cand_b: float32 [128], replicated, may hold values from -3 to 3
- tile_vals: bfloat16 [256, 4, 128, 128], P(('parts', 'wide')), parts along dimension 0, may hold values from -0.125 to 0.125
- tile_cols: int32 [256, 4], P(('parts', 'wide')), parts along dimension 0, may hold values from 0 to 127, as said below
- tile_counts: int32 [256], P(('parts', 'wide')), parts along dimension 0, may hold values from 3 to 4, as said below
- sector_order: int32 [32768], P(('parts', 'wide')), parts along dimension 0, may hold values from 0 to 1023, as said below
Outputs:
- grad_inputs: bfloat16 [3, 32768, 128], P(None, ('parts', 'wide')), parts along dimension 1
- grad_state_init: float32 [32768, 128], P(('parts', 'wide')), parts along dimension 0
- grad_gate_w: float32 [1536, 256], P('parts'), parts along dimension 0
- grad_gate_b: float32 [512], P('parts'), parts along dimension 0
- grad_cand_w: float32 [1536, 128], P('parts'), parts along dimension 0
- grad_cand_b: float32 [256], P('parts'), parts along dimension 0
The draws below stay inside these ranges and needn't reach their ends.
There are 2 independent parts, one for each index of `parts`. The reference program is written for one: setup_inputs(seed, part) draws one part's arguments, and reference() takes and returns one part's arrays. A program takes and returns all parts, laid end to end along the dimension named above; an argument that names none is the same for every part. Nothing has to cross between parts.
Inputs may be any that keep to these rules, and one draw needn't show every extreme that they name: `tile_cols`: slot 0 of tile row g names g; slots 1 and 2 name g - 1 and g + 1 clipped to 0 and 127; slot 3 names a tile of g // 8 * 8 - 1 to g // 8 * 8 + 8, clipped likewise. `tile_counts`: tile row 0 has 4 live slots and tile row 1 has 3; every row has one of these two counts. `sector_order`: each aligned block of 1024 entries is a permutation of 0 to 1023.
All inputs are finite; a program needn't handle non-finite values.
Results may differ from the reference program's by a relative error of at most 0.007.
Values may be sent and summed in bfloat16 or wider, within the bound.
No kernel may reach another device: no remote copies, remote signals or barrier semaphores. Data moves between devices by JAX's collectives and lax.ppermute only.
A program may use at most 128 MiB of HBM per device.

```python
import math
import jax
import jax.numpy as jnp
from jax import lax

H = 128
TILE = 128
SLOTS = 4
STEPS = 3
TILES_DEV = 8
ROWS = 1024
TILES = 128
SECTORS = 16384


def draw_tile_cols(key, part):
    tile_index = jnp.arange(TILES, dtype=jnp.int32)
    block_start = tile_index // TILES_DEV * TILES_DEV
    extra_tile = block_start - 1 + jax.random.randint(key, (TILES,), 0, TILES_DEV + 2, dtype=jnp.int32)
    column_tiles = jnp.stack([tile_index, tile_index - 1, tile_index + 1, extra_tile], axis=1)
    return jnp.clip(column_tiles, 0, TILES - 1).astype(jnp.int32)


def draw_tile_counts(key, part):
    row_counts = SLOTS - 1 + jax.random.randint(key, (TILES,), 0, 2, dtype=jnp.int32)
    row_counts = row_counts.at[0].set(SLOTS).at[1].set(SLOTS - 1)
    return row_counts.astype(jnp.int32)


def draw_sector_order(key, part):
    block_count = SECTORS // ROWS
    block_keys = jax.random.split(key, block_count)
    orders = jax.vmap(lambda block_key: jax.random.permutation(block_key, ROWS))(block_keys)
    return orders.reshape(SECTORS).astype(jnp.int32)


def block_levels(stream_key, shape, pieces, smallest, top_value):
    factor_of = 1.0
    for axis_at, parts in pieces:
        heights = jax.random.uniform(jax.random.fold_in(jax.random.fold_in(stream_key, 6), axis_at), (parts,), jnp.float32, smallest / len(pieces), top_value / len(pieces))
        factor_of = factor_of * jnp.repeat(jnp.exp(heights), shape[axis_at] // parts).reshape((-1,) + (1,) * (len(shape) - 1 - axis_at))
    return factor_of


def bell_draw(stream_key, dims, spread, limit, shards=(), kind=jnp.bfloat16):
    loudness = block_levels(stream_key, dims, shards, -0.22, 0.18) if shards else 1.0
    drawn = jax.random.normal(stream_key, dims, jnp.float32) * spread * loudness
    return jnp.minimum(jnp.maximum(drawn, -limit), limit).astype(kind)


def setup_inputs(seed: int = 0, part: int = 0) -> dict:
    splits = jax.random.split(jax.random.key(seed), 12)
    part_splits = jax.random.split(jax.random.fold_in(splits[11], part), 12)
    inputs = bell_draw(part_splits[0], (STEPS, SECTORS, H), 0.5, 3.0, ((1, 16),))
    state_init = bell_draw(part_splits[1], (SECTORS, H), 0.5, 3.0, ((0, 16),), jnp.float32)
    cotangent = bell_draw(part_splits[2], (STEPS, SECTORS, H), 0.3, 1.796875, ((1, 16),))
    gate_w = bell_draw(splits[3], (6 * H, 2 * H), (6 * H) ** -0.5, 0.21875)
    gate_b = bell_draw(splits[4], (2 * H,), 0.5, 3.0, (), jnp.float32)
    cand_w = bell_draw(splits[5], (6 * H, H), (6 * H) ** -0.5, 0.21875)
    cand_b = bell_draw(splits[6], (H,), 0.5, 3.0, (), jnp.float32)
    tile_vals = bell_draw(part_splits[7], (TILES, SLOTS, TILE, TILE), (4 * SLOTS * TILE) ** -0.5, 0.125, ((0, 16),))
    tile_cols = draw_tile_cols(jax.random.fold_in(jax.random.fold_in(splits[11], part), 71), part)
    tile_counts = draw_tile_counts(jax.random.fold_in(jax.random.fold_in(splits[11], part), 71), part)
    sector_order = draw_sector_order(jax.random.fold_in(jax.random.fold_in(splits[11], part), 71), part)
    return {"inputs": inputs, "state_init": state_init, "cotangent": cotangent, "gate_w": gate_w, "gate_b": gate_b, "cand_w": cand_w, "cand_b": cand_b, "tile_vals": tile_vals, "tile_cols": tile_cols, "tile_counts": tile_counts, "sector_order": sector_order}


def outer_sum(left, right):
    return lax.dot_general(left.astype(jnp.float32), right.astype(jnp.float32), (((0,), (0,)), ((), ())), precision=lax.Precision.HIGHEST)

def diffuse(forward, input_base):
    first_order = forward(input_base).astype(jnp.bfloat16)
    second_order = (2.0 * forward(first_order) - input_base.astype(jnp.float32)).astype(jnp.bfloat16)
    return (first_order, second_order)

def diffuse_back(backward, grad_zero, grad_one, grad_two):
    through_two = backward(grad_two.astype(jnp.bfloat16))
    grad_one_total = grad_one + 2.0 * through_two
    return grad_zero - grad_two + backward(grad_one_total.astype(jnp.bfloat16))

def reference(inputs, state_init, cotangent, gate_w, gate_b, cand_w, cand_b, tile_vals, tile_cols, tile_counts, sector_order):
    global_rows = (sector_order + jnp.arange(SECTORS, dtype=jnp.int32) // ROWS * ROWS).astype(jnp.int32)
    live_slots = (jnp.arange(SLOTS, dtype=jnp.int32)[None, :] < tile_counts[:, None]).astype(jnp.bfloat16)
    masked = (tile_vals * live_slots[:, :, None, None]).astype(jnp.float32)
    tile_spots = (tile_cols + 1).astype(jnp.int32)
    flat_spots = tile_spots.reshape(-1)

    def forward(row_block):
        feat_count = row_block.shape[1]
        tile_rows = row_block.astype(jnp.float32).reshape(TILES, TILE, feat_count)
        padded = jnp.pad(tile_rows, ((1, 1), (0, 0), (0, 0)))
        picked = padded[tile_spots]
        product = jnp.einsum('rsab,rsbf->raf', masked, picked, precision=lax.Precision.HIGHEST)
        return product.reshape(SECTORS, feat_count)

    def backward(grads):
        feat_count = grads.shape[1]
        contrib = jnp.einsum('rsab,raf->rsbf', masked, grads.astype(jnp.float32).reshape(TILES, TILE, feat_count), precision=lax.Precision.HIGHEST)
        extended = jnp.zeros((TILES + 2, TILE, feat_count), jnp.float32).at[flat_spots].add(contrib.reshape(-1, TILE, feat_count))
        return extended[1:TILES + 1].reshape(SECTORS, feat_count)
    ordered_in = inputs[:, global_rows]
    ordered_cot = cotangent[:, global_rows].astype(jnp.float32)
    carried = state_init[global_rows].astype(jnp.float32)
    saved_steps = []
    for step_index in range(STEPS):
        input_base = ordered_in[step_index]
        input_one, input_two = diffuse(forward, input_base)
        state_b = carried.astype(jnp.bfloat16)
        state_one, state_two = diffuse(forward, state_b)
        gate_feats = jnp.concatenate([input_base, input_one, input_two, state_b, state_one, state_two], axis=1)
        gate_pre = jnp.dot(gate_feats, gate_w, preferred_element_type=jnp.float32) + gate_b
        reset_gate = jax.nn.sigmoid(gate_pre[:, :H])
        update = jax.nn.sigmoid(gate_pre[:, H:])
        reset_state = (reset_gate * carried).astype(jnp.bfloat16)
        reset_one, reset_two = diffuse(forward, reset_state)
        cand_feats = jnp.concatenate([input_base, input_one, input_two, reset_state, reset_one, reset_two], axis=1)
        candidate = jnp.tanh(jnp.dot(cand_feats, cand_w, preferred_element_type=jnp.float32) + cand_b)
        saved_steps.append((carried, gate_feats, cand_feats, reset_gate, update, candidate))
        carried = update * carried + (1.0 - update) * candidate
    grad_state = jnp.zeros((SECTORS, H), jnp.float32)
    total_gw = jnp.zeros((6 * H, 2 * H), jnp.float32)
    total_gb = jnp.zeros((2 * H,), jnp.float32)
    total_cw = jnp.zeros((6 * H, H), jnp.float32)
    total_cb = jnp.zeros((H,), jnp.float32)
    input_grads = [None] * STEPS
    for step_index in reversed(range(STEPS)):
        prev_state, gate_feats, cand_feats, reset_gate, update, candidate = saved_steps[step_index]
        grad_state = grad_state + ordered_cot[step_index]
        grad_cand = grad_state * (1.0 - update)
        grad_update = grad_state * (prev_state - candidate)
        grad_prev = grad_state * update
        cand_pre_grad = grad_cand * (1.0 - candidate * candidate)
        cand_pre_b = cand_pre_grad.astype(jnp.bfloat16)
        total_cw = total_cw + outer_sum(cand_feats, cand_pre_b)
        total_cb = total_cb + lax.optimization_barrier(jnp.sum(cand_pre_grad, axis=0))
        cand_feat_grad = jnp.dot(cand_pre_b, cand_w.T, preferred_element_type=jnp.float32)
        reset_grad = diffuse_back(backward, cand_feat_grad[:, 3 * H:4 * H], cand_feat_grad[:, 4 * H:5 * H], cand_feat_grad[:, 5 * H:])
        grad_reset = reset_grad * prev_state
        grad_prev = grad_prev + reset_grad * reset_gate
        gate_pre_grad = jnp.concatenate([grad_reset * reset_gate * (1.0 - reset_gate), grad_update * update * (1.0 - update)], axis=1)
        gate_pre_b = gate_pre_grad.astype(jnp.bfloat16)
        total_gw = total_gw + outer_sum(gate_feats, gate_pre_b)
        total_gb = total_gb + lax.optimization_barrier(jnp.sum(gate_pre_grad, axis=0))
        gate_feat_grad = jnp.dot(gate_pre_b, gate_w.T, preferred_element_type=jnp.float32)
        grad_prev = grad_prev + diffuse_back(backward, gate_feat_grad[:, 3 * H:4 * H], gate_feat_grad[:, 4 * H:5 * H], gate_feat_grad[:, 5 * H:])
        input_part = cand_feat_grad[:, :3 * H] + gate_feat_grad[:, :3 * H]
        input_grads[step_index] = diffuse_back(backward, input_part[:, :H], input_part[:, H:2 * H], input_part[:, 2 * H:]).astype(jnp.bfloat16)
        grad_state = grad_prev
    stacked = jnp.stack(input_grads, axis=0)
    grad_inputs = jnp.zeros((STEPS, SECTORS, H), jnp.bfloat16).at[:, global_rows].set(stacked)
    grad_state_init = jnp.zeros((SECTORS, H), jnp.float32).at[global_rows].set(grad_state)
    scale = 1.0 / math.sqrt(SECTORS * STEPS)
    return (grad_inputs, grad_state_init, total_gw * scale, total_gb * scale, total_cw * scale, total_cb * scale)
```

```python
import functools
import math

import jax
import jax.numpy as jnp
from jax import lax
from jax.experimental import pallas as pl
from jax.experimental.pallas import tpu as pltpu
from jax.sharding import PartitionSpec as P

BF = jnp.bfloat16
F32 = jnp.float32
T = 128
NT = 8
ROWS = NT * T
VMEM_LIMIT = 40 * 1024 * 1024


def swap_in(block):
    count = lax.axis_size("wide")
    return lax.ppermute(
        block, "wide", [p for i in range(0, count - 1, 2) for p in ((i, i + 1), (i + 1, i))]
    )


def swap_out(block):
    count = lax.axis_size("wide")
    return lax.ppermute(
        block, "wide", [p for i in range(1, count - 1, 2) for p in ((i, i + 1), (i + 1, i))]
    )


def exchange_forward(pay_in, pay_out):
    got_in = swap_in(pay_in)
    got_out = swap_out(jnp.concatenate([pay_out, got_in[:1]], axis=0))
    return got_in, got_out, swap_in(got_out)


def exchange_back(pay_in, pay_out):
    got_in = swap_in(pay_in)
    got_out = swap_out(
        jnp.concatenate([pay_out[:1] + got_in[3:], pay_out[1:]], axis=0)
    )
    return got_in, got_out, swap_in(got_out)


def dot(a, b):
    return jnp.dot(a, b, preferred_element_type=F32)


def dot_nt(a, b):
    return lax.dot_general(a, b, (((1,), (1,)), ((), ())), preferred_element_type=F32)


def dot_tn(a, b):
    return lax.dot_general(a, b, (((0,), (0,)), ((), ())), preferred_element_type=F32)


def tile(ref, i):
    start = i * T if isinstance(i, int) else pl.multiple_of(i * T, T)
    return ref.at[pl.ds(start, T)]


class Place:
    def __init__(self, meta):
        self.idx = lambda r, s: meta[4 * r + s]
        core = meta[32]
        self.e_in = 7 - 7 * core
        self.n_in = 6 - 5 * core
        self.e_out = 7 * core
        self.n_out = 1 + 5 * core
        self.pos_in = 9 - 9 * core
        self.pos_out = 9 * core
        row_in = jnp.where(core == 0, meta[4 * 7 + 3], meta[3])
        row_out = jnp.where(core == 0, meta[3], meta[4 * 7 + 3])
        self.t_in = jnp.clip(row_in - 1, 0, NT - 1)
        self.t_out = jnp.clip(row_out - 1, 0, NT - 1)


def write_forward_payload(place, own, pay_in, pay_out, lanes):
    for j, i in enumerate((place.e_in, place.n_in, place.t_in)):
        pay_in[j, :, lanes] = tile(own, i)[...]
    for j, i in enumerate((place.e_out, place.n_out, place.t_out)):
        pay_out[j, :, lanes] = tile(own, i)[...]


def forward_row(place, vfg, src, r):
    low = tile(src, place.idx(0, 1))[...] if r == 0 else tile(src, r)[...]
    high = tile(src, place.idx(7, 2))[...] if r == 7 else tile(src, r + 2)[...]
    picked = jnp.concatenate(
        [low, tile(src, r + 1)[...], high, tile(src, place.idx(r, 3))[...]], axis=0
    )
    return dot(vfg[r], picked)


def lanes_of(vals):
    return jnp.concatenate([vals[k] for k in range(6)], axis=1)


def first_order(place, vfg, vin, vout, zext, d1, rin, rout, rfwd):
    tile(zext, place.pos_in)[...] = rin[0]
    tile(zext, place.pos_out)[...] = rout[0]
    for r in range(NT):
        tile(d1, r + 1)[...] = forward_row(place, vfg, zext, r).astype(BF)
    edge = tile(zext, place.e_in + 1)[...]
    picked = jnp.concatenate([rin[0], rin[1], edge, edge, rin[2], rfwd[0]], axis=0)
    tile(d1, place.pos_in)[...] = dot(lanes_of(vin), picked).astype(BF)
    edge = tile(zext, place.e_out + 1)[...]
    picked = jnp.concatenate([rout[0], rout[1], edge, edge, rout[2], rout[3]], axis=0)
    tile(d1, place.pos_out)[...] = dot(lanes_of(vout), picked).astype(BF)


def second_order(place, vfg, zext, d1, r):
    z = tile(zext, r + 1)[...].astype(F32)
    return (2.0 * forward_row(place, vfg, d1, r) - z).astype(BF)


def write_state_payload(place, st, x, pay_in, pay_out):
    for pay, tiles in (
        (pay_in, (place.e_in, place.n_in, place.t_in)),
        (pay_out, (place.e_out, place.n_out, place.t_out)),
    ):
        for j, i in enumerate(tiles):
            pay[j, :, :T] = tile(st, i)[...].astype(BF)
            pay[j, :, T:] = tile(x, i)[...]


def prepare_kernel(
    meta, counts, order, inputs, state, cot, vals,
    x0, x1, x2, c0, c1, c2, st, pay_in, pay_out, vfg, vbg, vbd, sb,
):
    place = Place(meta)
    rest = state[...]
    for k in range(3):
        part = rest.astype(BF)
        sb[k] = part
        rest = rest - part.astype(F32)
    lane = lax.broadcasted_iota(jnp.int32, (T, T), 1)
    for j in range(NT):
        wanted = jnp.broadcast_to(order[j : j + 1, :].astype(F32), (T, T)).T.astype(jnp.int32)
        pick = jnp.concatenate(
            [(wanted == lane + k * T).astype(F32).astype(BF) for k in range(NT)], axis=1
        )
        rows = slice(j * T, (j + 1) * T)
        for k, (x_out, c_out) in enumerate(((x0, c0), (x1, c1), (x2, c2))):
            x_out[rows] = dot(pick, inputs[k]).astype(BF)
            c_out[rows] = dot(pick, cot[k]).astype(BF)
        st[rows] = dot(pick, sb[0]) + dot(pick, sb[1]) + dot(pick, sb[2])
    write_state_payload(place, st, x0, pay_in, pay_out)
    for r in range(NT):
        live = (counts[r] > 3).astype(F32)
        last = (vals[r, 3].astype(F32) * live).astype(BF)
        vfg[r, :, 0:T] = vals[r, 1]
        vfg[r, :, T : 2 * T] = vals[r, 0]
        vfg[r, :, 2 * T : 3 * T] = vals[r, 2]
        vfg[r, :, 3 * T :] = last
        vbg[r, :, T : 2 * T] = vals[r, 0].T
        if r > 0:
            vbg[r - 1, :, 2 * T :] = vals[r, 1].T
        else:
            vbd[8] = vals[r, 1].T
        if r < NT - 1:
            vbg[r + 1, :, 0:T] = vals[r, 2].T
        else:
            vbd[9] = vals[r, 2].T
        vbd[r] = last.T
    vbg[0, :, 0:T] = jnp.zeros((T, T), BF)
    vbg[NT - 1, :, 2 * T :] = jnp.zeros((T, T), BF)


def transposed_kernel(vin, vout, vin_t, vout_t):
    for k in range(6):
        vin_t[k] = vin[k].T
        vout_t[k] = vout[k].T


def gate_kernel(
    meta, st, x, rin, rout, rfwd, vfg, vin, vout, gw, gb, cw, cb,
    feats, r_out, u_out, q_out, xc_out, pay_in, pay_out, zext, d1,
):
    place = Place(meta)
    zext[T : T + ROWS, :T] = st[...].astype(BF)
    zext[T : T + ROWS, T:] = x[...]
    first_order(place, vfg, vin, vout, zext, d1, rin, rout, rfwd)
    for r in range(NT):
        d2 = second_order(place, vfg, zext, d1, r)
        z = tile(zext, r + 1)[...]
        one = tile(d1, r + 1)[...]
        row = jnp.concatenate(
            [z[:, T:], one[:, T:], d2[:, T:], z[:, :T], one[:, :T], d2[:, :T]], axis=1
        )
        tile(feats, r)[...] = row
    for h in range(4):
        rows = slice(h * 256, (h + 1) * 256)
        f = feats[rows]
        pre = dot(f, gw[...]) + gb[...]
        xc_out[rows] = dot(f[:, : 3 * T], cw[: 3 * T]) + cb[...]
        reset = jax.nn.sigmoid(pre[:, :T])
        r_out[rows] = reset
        u_out[rows] = jax.nn.sigmoid(pre[:, T:])
        q_out[rows] = (reset * st[rows]).astype(BF)
    write_forward_payload(place, q_out, pay_in, pay_out, slice(0, T))


def cand_kernel(
    meta, q, rin, rout, rfwd, vfg, vin, vout, cw, xc, u, st, *rest, last
):
    if last:
        fq, c_out, zext, d1 = rest
    else:
        x_next, fq, c_out, st_out, pay_in, pay_out, zext, d1 = rest
    place = Place(meta)
    zext[T : T + ROWS] = q[...]
    first_order(place, vfg, vin, vout, zext, d1, rin, rout, rfwd)
    for r in range(NT):
        d2 = second_order(place, vfg, zext, d1, r)
        tile(fq, r)[...] = jnp.concatenate(
            [tile(zext, r + 1)[...], tile(d1, r + 1)[...], d2], axis=1
        )
    for h in range(4):
        rows = slice(h * 256, (h + 1) * 256)
        cand = jnp.tanh(dot(fq[rows], cw[3 * T :]) + xc[rows])
        c_out[rows] = cand
        if not last:
            st_out[rows] = u[rows] * st[rows] + (1.0 - u[rows]) * cand
    if not last:
        write_state_payload(place, st_out, x_next, pay_in, pay_out)


def add_received(place, acc, rin, rout, rfwd):
    for i, block in (
        (place.e_in, rin[0]),
        (place.n_in, rin[1]),
        (place.t_in, rin[2]),
        (place.e_out, rout[0]),
        (place.n_out, rout[1]),
        (place.t_out, rout[2]),
        (place.e_in, rfwd[3]),
    ):
        tile(acc, i)[...] += block.astype(F32)


def back_rows(place, vbg, vbd, y, acc, base):
    zero = jnp.zeros((T, acc.shape[1]), F32)
    tile(acc, 0)[...] = zero
    tile(acc, 9)[...] = zero
    for r in range(NT):
        lo, hi = max(r - 1, 0), min(r + 2, NT)
        lhs = vbg[r, :, (lo - r + 1) * T : (hi - r + 1) * T]
        tile(acc, r + 1)[...] = base(r, dot(lhs, y[lo * T : hi * T]))
    parts = [(place.idx(0, 1), 8, 0), (place.idx(7, 2), 9, 7)]
    parts += [(place.idx(r, 3), r, r) for r in range(NT)]
    for i, k, r in parts:
        tile(acc, i)[...] += dot(vbd[k], y[r * T : (r + 1) * T])


def diffuse_back(place, vbg, vbd, vin_t, vout_t, a, wide, y, w, acc, pay_in, pay_out):
    for r in range(NT):
        rows = slice(r * T, (r + 1) * T)
        y[rows] = a(2, rows).astype(BF)
    back_rows(
        place, vbg, vbd, y, acc, lambda r, v: a(1, slice(r * T, (r + 1) * T)) * 0.5 + v
    )
    for e in range(NT + 2):
        tile(w, e)[...] = (2.0 * tile(acc, e)[...]).astype(BF)
    own = w.at[pl.ds(T, ROWS)]

    def second(r, v):
        rows = slice(r * T, (r + 1) * T)
        return a(0, rows) - a(2, rows) + v

    back_rows(place, vbg, vbd, own, acc, second)
    for pos, edge, vals, pay in (
        (place.pos_in, place.e_in, vin_t, pay_in),
        (place.pos_out, place.e_out, vout_t, pay_out),
    ):
        got = dot(vals[...].reshape(6 * T, T), tile(w, pos)[...])
        part = [got[k * T : (k + 1) * T] for k in range(6)]
        tile(acc, edge + 1)[...] += part[2] + part[3]
        pay[0] = (tile(acc, pos)[...] + part[0]).astype(BF)
        pay[1] = part[1].astype(BF)
        pay[2] = part[4].astype(BF)
        pay[3] = part[5].astype(BF)


def cand_back_kernel(*refs, first):
    refs = list(refs)
    take = lambda n: [refs.pop(0) for _ in range(n)]
    meta, cot, u, c, st, feats, fq, cw, vbg, vbd, vin_t, vout_t = take(12)
    if not first:
        gs_part, gx_part, rin, rout, rfwd, wc_in = take(6)
    gp_out, ec_out, eu_out, gq_out, wc_out, pay_in, pay_out = take(7)
    if not first:
        (gx_out,) = take(1)
    gs, g, y, w, acc = take(5)
    place = Place(meta)
    if not first:
        gs[:, :T] = gs_part[...]
        gs[:, T:] = gx_part[...]
        add_received(place, gs, rin, rout, rfwd)
        gx_out[...] = gs[:, T:].astype(BF)
    sum_c = jnp.zeros((1, T), F32)
    sum_u = jnp.zeros((1, T), F32)
    for h in range(NT):
        rows = slice(h * T, (h + 1) * T)
        grad = cot[rows].astype(F32)
        if not first:
            grad = grad + gs[rows, :T]
        upd, cand = u[rows], c[rows]
        pre = grad * (1.0 - upd) * (1.0 - cand * cand)
        gate = grad * (st[rows] - cand) * upd * (1.0 - upd)
        gp_out[rows] = grad * upd
        ec_out[rows] = pre.astype(BF)
        eu_out[rows] = gate.astype(BF)
        sum_c = sum_c + jnp.sum(pre, axis=0, keepdims=True)
        sum_u = sum_u + jnp.sum(gate, axis=0, keepdims=True)
    ec = ec_out[...]
    g[...] = dot_nt(ec, cw[3 * T :])
    diffuse_back(
        place, vbg, vbd, vin_t, vout_t,
        lambda k, rows: g[rows, k * T : (k + 1) * T],
        T, y, w, acc, pay_in, pay_out,
    )
    gq_out[...] = acc[T : T + ROWS]
    low = dot_tn(ec, feats[:, : 3 * T])
    high = dot_tn(ec, fq[...])
    sums = jnp.concatenate([sum_c, sum_u, jnp.zeros((1, 4 * T), F32)], axis=1)
    sums = jnp.concatenate([sums, jnp.zeros((7, 6 * T), F32)], axis=0)
    if not first:
        low = low + wc_in[:T, : 3 * T]
        high = high + wc_in[:T, 3 * T :]
        sums = sums + wc_in[T:]
    wc_out[:T, : 3 * T] = low
    wc_out[:T, 3 * T :] = high
    wc_out[T:] = sums


def gate_back_kernel(*refs, first):
    refs = list(refs)
    take = lambda n: [refs.pop(0) for _ in range(n)]
    meta, gq_part, rin, rout, rfwd, gp, r_ref, st, ec, eu, feats, gw, cw = take(13)
    vbg, vbd, vin_t, vout_t = take(4)
    if not first:
        (wg_in,) = take(1)
    gs_out, gx_out, wg_out, pay_in, pay_out = take(5)
    gq, eg, gps, g, y, w, acc = take(7)
    place = Place(meta)
    gq[...] = gq_part[...]
    add_received(place, gq, rin, rout, rfwd)
    sum_r = jnp.zeros((1, T), F32)
    for h in range(NT):
        rows = slice(h * T, (h + 1) * T)
        grad, reset = gq[rows], r_ref[rows]
        gps[rows] = gp[rows] + grad * reset
        pre = grad * st[rows] * reset * (1.0 - reset)
        eg[rows, :T] = pre.astype(BF)
        eg[rows, T:] = eu[rows]
        sum_r = sum_r + jnp.sum(pre, axis=0, keepdims=True)
    e = eg[...]
    for k in range(3):
        cols = slice(2 * k * T, (2 * k + 1) * T)
        g[:, cols] = dot_nt(e, gw[(3 + k) * T : (4 + k) * T])
        cols = slice((2 * k + 1) * T, (2 * k + 2) * T)
        g[:, cols] = dot_nt(e, gw[k * T : (k + 1) * T]) + dot_nt(
            ec[...], cw[k * T : (k + 1) * T]
        )
    diffuse_back(
        place, vbg, vbd, vin_t, vout_t,
        lambda k, rows: g[rows, 2 * k * T : 2 * (k + 1) * T],
        2 * T, y, w, acc, pay_in, pay_out,
    )
    gs_out[...] = acc[T : T + ROWS, :T] + gps[...]
    gx_out[...] = acc[T : T + ROWS, T:]
    total = dot_tn(e, feats[...])
    sums = jnp.concatenate([sum_r, jnp.zeros((1, 5 * T), F32)], axis=1)
    sums = jnp.concatenate([sums, jnp.zeros((7, 6 * T), F32)], axis=0)
    if not first:
        total = total + wg_in[: 2 * T]
        sums = sums + wg_in[2 * T :]
    wg_out[: 2 * T] = total
    wg_out[2 * T :] = sums


def finish_kernel(
    meta, order, gs_part, gx_part, rin, rout, rfwd, gx1, gx2, gi_out, gs_out, gs, parts
):
    place = Place(meta)
    gs[:, :T] = gs_part[...]
    gs[:, T:] = gx_part[...]
    add_received(place, gs, rin, rout, rfwd)
    rest = gs[:, :T]
    for k in range(3):
        part = rest.astype(BF)
        parts[:, k * T : (k + 1) * T] = part
        rest = rest - part.astype(F32)
    parts[:, 3 * T : 4 * T] = gs[:, T:].astype(BF)
    parts[:, 4 * T : 5 * T] = gx1[...]
    parts[:, 5 * T :] = gx2[...]
    row = lax.broadcasted_iota(jnp.int32, (T, T), 0)
    for k in range(NT):
        put = jnp.concatenate(
            [
                (jnp.broadcast_to(order[j : j + 1, :], (T, T)) == row + k * T)
                .astype(F32)
                .astype(BF)
                for j in range(NT)
            ],
            axis=1,
        )
        rows = slice(k * T, (k + 1) * T)
        got = dot(put, parts[...])
        gs_out[rows] = got[:, :T] + got[:, T : 2 * T] + got[:, 2 * T : 3 * T]
        for t in range(3):
            gi_out[t, rows] = got[:, (3 + t) * T : (4 + t) * T].astype(BF)


SMEM = pl.BlockSpec(memory_space=pltpu.SMEM)
VMEM = pl.BlockSpec(memory_space=pltpu.VMEM)


def run(kernel, name, smem, args, outs, scratch=()):
    specs = [SMEM if i in smem else VMEM for i in range(len(args))]
    out_shape = [jax.ShapeDtypeStruct(s, d) for s, d in outs]
    return pl.pallas_call(
        kernel,
        name=name,
        in_specs=specs,
        out_specs=[VMEM] * len(outs),
        out_shape=out_shape,
        scratch_shapes=[pltpu.VMEM(s, d) for s, d in scratch],
        compiler_params=pltpu.CompilerParams(vmem_limit_bytes=VMEM_LIMIT),
    )(*args)


def edge_values(tile_vals, local_cols, tile_counts, row, low_side, pos_them, pos_far):
    vals = lax.dynamic_index_in_dim(tile_vals, row, 0, keepdims=False)
    col = lax.dynamic_index_in_dim(local_cols, row, 0, keepdims=False)[3]
    live = lax.dynamic_index_in_dim(tile_counts, row, 0, keepdims=False) > 3
    ahead = jnp.where(low_side, vals[1], vals[2])
    inside = jnp.where(low_side, vals[2], vals[1])
    them, far = col == pos_them, col == pos_far
    zero = jnp.zeros_like(vals[3])
    return jnp.stack(
        [
            vals[0],
            inside,
            ahead,
            jnp.where(live & them, vals[3], zero),
            jnp.where(live & ~them & ~far, vals[3], zero),
            jnp.where(live & far, vals[3], zero),
        ]
    )


def per_device(
    inputs, state_init, cotangent, gate_w, gate_b, cand_w, cand_b,
    tile_vals, tile_cols, tile_counts, sector_order,
):
    device = lax.axis_index("wide")
    core = device % 2
    local_cols = tile_cols - (device * NT - 1)
    meta = jnp.concatenate([local_cols.reshape(-1), core[None]]).astype(jnp.int32)
    order = sector_order.reshape(NT, T)
    gb = gate_b.reshape(1, -1)
    cb = cand_b.reshape(1, -1)
    e_in, e_out = 7 - 7 * core, 7 * core
    p_in, p_out = 9 - 9 * core, 9 * core
    vin = swap_in(
        edge_values(tile_vals, local_cols, tile_counts, e_in, core == 1, p_in, p_out)
    )
    vout = swap_out(
        edge_values(tile_vals, local_cols, tile_counts, e_out, core == 0, p_out, p_in)
    )
    big = (ROWS, T)
    x0, x1, x2, c0, c1, c2, st, pay_in, pay_out, vfg, vbg, vbd = run(
        prepare_kernel,
        "prepare",
        (0, 1),
        (meta, tile_counts, order, inputs, state_init, cotangent, tile_vals),
        [(big, BF)] * 6
        + [(big, F32), ((3, T, 2 * T), BF), ((3, T, 2 * T), BF)]
        + [((NT, T, 4 * T), BF), ((NT, T, 3 * T), BF), ((NT + 2, T, T), BF)],
        [((3,) + big, BF)],
    )
    pay = (pay_in, pay_out)
    vin_t, vout_t = run(
        transposed_kernel, "turn", (), (vin, vout), [((6, T, T), BF)] * 2
    )
    xs, cots = (x0, x1, x2), (c0, c1, c2)
    saved = []
    steps = inputs.shape[0]
    wide = ((NT + 2) * T, 2 * T)
    slim = ((NT + 2) * T, T)
    for t in range(steps):
        rin, rout, rfwd = exchange_forward(*pay)
        feats, r, u, q, xc, *pay = run(
            gate_kernel,
            "gate",
            (0,),
            (meta, st, xs[t], rin, rout, rfwd, vfg, vin, vout, gate_w, gb, cand_w, cb),
            [((ROWS, 6 * T), BF), (big, F32), (big, F32), (big, BF), (big, F32)]
            + [((3, T, T), BF)] * 2,
            [(wide, BF)] * 2,
        )
        rin, rout, rfwd = exchange_forward(*pay)
        last = t == steps - 1
        got = run(
            functools.partial(cand_kernel, last=last),
            "cand",
            (0,),
            (meta, q, rin, rout, rfwd, vfg, vin, vout, cand_w, xc, u, st)
            + (() if last else (xs[t + 1],)),
            [((ROWS, 3 * T), BF), (big, F32)]
            + ([] if last else [(big, F32)] + [((3, T, 2 * T), BF)] * 2),
            [(slim, BF)] * 2,
        )
        saved.append((st, feats, r, u, got[0], got[1]))
        if not last:
            st, pay = got[2], got[3:]
    ops = (vbg, vbd, vin_t, vout_t)
    gxs = [None] * steps
    carry = ()
    wg = ()
    for t in reversed(range(steps)):
        st, feats, r, u, fq, c = saved[t]
        first = t == steps - 1
        got = run(
            functools.partial(cand_back_kernel, first=first),
            "cand_back",
            (0,),
            (meta, cots[t], u, c, st, feats, fq, cand_w) + ops + carry,
            [(big, F32), (big, BF), (big, BF), (big, F32), ((T + 8, 6 * T), F32)]
            + [((4, T, T), BF)] * 2
            + ([] if first else [(big, BF)]),
            [((ROWS, 2 * T), F32), ((ROWS, 3 * T), F32), (big, BF), (slim, BF), (slim, F32)],
        )
        gp, ec, eu, gq, wc, *pay = got[:7]
        if not first:
            gxs[t + 1] = got[7]
        rin, rout, rfwd = exchange_back(*pay)
        gs_part, gx_part, wg_new, *pay = run(
            functools.partial(gate_back_kernel, first=first),
            "gate_back",
            (0,),
            (meta, gq, rin, rout, rfwd, gp, r, st, ec, eu, feats, gate_w, cand_w) + ops + wg,
            [(big, F32), (big, F32), ((2 * T + 8, 6 * T), F32)] + [((4, T, 2 * T), BF)] * 2,
            [
                (big, F32), ((ROWS, 2 * T), BF), (big, F32), ((ROWS, 6 * T), F32),
                ((ROWS, 2 * T), BF), (wide, BF), (wide, F32),
            ],
        )
        wg = (wg_new,)
        rin, rout, rfwd = exchange_back(*pay)
        carry = (gs_part, gx_part, rin, rout, rfwd, wc)
    grads = lax.psum(jnp.concatenate([wg[0], wc], axis=0), "wide")
    gi, gs = run(
        finish_kernel,
        "finish",
        (0,),
        (meta, order, gs_part, gx_part, rin, rout, rfwd, gxs[1], gxs[2]),
        [((steps,) + big, BF), (big, F32)],
        [((ROWS, 2 * T), F32), ((ROWS, 6 * T), BF)],
    )
    scale = 1.0 / math.sqrt(ROWS * lax.axis_size("wide") * steps)
    grads = grads * scale
    wgt, bg, wct, bc = grads[: 2 * T], grads[2 * T], grads[2 * T + 8 : 3 * T + 8], grads[3 * T + 8]
    return (
        gi,
        gs,
        wgt.T,
        jnp.concatenate([bg[:T], bc[T : 2 * T]]),
        wct.T,
        bc[:T],
    )


def solution(mesh):
    return jax.shard_map(
        per_device,
        mesh=mesh,
        in_specs=(
            P(None, ("parts", "wide"), None),
            P(("parts", "wide"), None),
            P(None, ("parts", "wide"), None),
            P(),
            P(),
            P(),
            P(),
            P(("parts", "wide"), None, None, None),
            P(("parts", "wide"), None),
            P(("parts", "wide")),
            P(("parts", "wide")),
        ),
        out_specs=(
            P(None, ("parts", "wide"), None),
            P(("parts", "wide"), None),
            P("parts", None),
            P("parts"),
            P("parts", None),
            P("parts"),
        ),
        check_vma=False,
    )
```

```python
import functools
import math

import jax
import jax.numpy as jnp
from jax import lax
from jax.experimental import pallas as pl
from jax.experimental.pallas import tpu as pltpu
from jax.sharding import PartitionSpec as P

BF = jnp.bfloat16
F32 = jnp.float32
T = 128
NT = 8
ROWS = NT * T
VMEM_LIMIT = 24 * 1024 * 1024


def swap(block, start):
    count = lax.axis_size("wide")
    return lax.ppermute(
        block, "wide", [p for i in range(start, count - 1, 2) for p in ((i, i + 1), (i + 1, i))]
    )


def swap_in(block):
    return swap(block, 0)


def swap_out(block):
    return swap(block, 1)


def exchange(pay_in, pay_out, far, middle):
    got_in = swap_in(pay_in)
    (ready,) = run(middle, "middle", (), (pay_out, got_in, far), [(pay_out.shape, BF)])
    got_out = swap_out(ready)
    return got_in, got_out, swap_in(got_out)


def dot(a, b):
    return jnp.dot(a, b, preferred_element_type=F32)


def dot_nt(a, b):
    return lax.dot_general(a, b, (((1,), (1,)), ((), ())), preferred_element_type=F32)


def dot_tn(a, b):
    return lax.dot_general(a, b, (((0,), (0,)), ((), ())), preferred_element_type=F32)


def tile(ref, i):
    start = i * T if isinstance(i, int) else pl.multiple_of(i * T, T)
    return ref.at[pl.ds(start, T)]


class Place:
    def __init__(self, meta):
        self.idx = lambda r, s: meta[4 * r + s]
        core = meta[32]
        self.core = core
        self.e_in = 7 - 7 * core
        self.n_in = 6 - 5 * core
        self.e_out = 7 * core
        self.n_out = 1 + 5 * core
        self.pos_in = 9 - 9 * core
        self.pos_out = 9 * core
        self.col_in = jnp.where(core == 0, meta[4 * 7 + 3], meta[3])
        self.col_out = jnp.where(core == 0, meta[3], meta[4 * 7 + 3])
        self.t_in = jnp.clip(self.col_in - 1, 0, NT - 1)
        self.t_out = jnp.clip(self.col_out - 1, 0, NT - 1)


def edge_kernel(meta, counts, first, last, e_in, e_out, et_in, et_out, f_out, ft_in, s_in, s_out):
    place = Place(meta)
    zero = place.core == 0
    for low, side_row, row_far, them, far in (
        (False, place.e_in, place.col_in, place.pos_in, place.pos_out),
        (True, place.e_out, place.col_out, place.pos_out, place.pos_in),
    ):
        top = zero if low else jnp.logical_not(zero)
        vals = [jnp.where(top, first[0, k].astype(F32), last[0, k].astype(F32)) for k in range(4)]
        inside = jnp.where(top, vals[2], vals[1])
        ahead = jnp.where(top, vals[1], vals[2])
        live = counts[side_row] > 3

        def third(flag):
            return vals[3] * jnp.where(jnp.logical_and(live, flag), 1.0, 0.0)

        is_them, is_far = row_far == them, row_far == far
        own = third(jnp.logical_not(jnp.logical_or(is_them, is_far)))
        e_ref, et_ref = (e_out, et_out) if low else (e_in, et_in)
        for k, v in enumerate((vals[0], inside, own)):
            e_ref[:, k * T : (k + 1) * T] = v.astype(BF)
            et_ref[k * T : (k + 1) * T] = v.T.astype(BF)
        s_ref = s_out if low else s_in
        s_ref[0] = ahead.astype(BF)
        s_ref[1] = third(is_them).astype(BF)
        if low:
            f_out[...] = third(is_far).astype(BF)
            s_in[3] = third(is_far).astype(BF)
        else:
            s_ref[2] = third(is_far).astype(BF)
            ft_in[...] = third(is_far).T.astype(BF)


def pick_rows(order, pick):
    lane = lax.broadcasted_iota(jnp.int32, (T, T), 1).astype(F32)
    for j in range(NT):
        wanted = jnp.broadcast_to(order[j : j + 1, :].astype(F32), (T, T)).T
        for k in range(NT):
            pick[j * T : (j + 1) * T, k * T : (k + 1) * T] = (
                (wanted == lane + float(k * T)).astype(F32).astype(BF)
            )


def split_f32(value, ref, start):
    for k in range(3):
        part = value.astype(BF)
        ref[:, start + k * T : start + (k + 1) * T] = part
        value = value - part.astype(F32)


def write_payload(place, own, e_in, e_out, pay_in, pay_out, lanes):
    for e_ref, pay, tiles in (
        (e_in, pay_in, (place.e_in, place.n_in, place.t_in)),
        (e_out, pay_out, (place.e_out, place.n_out, place.t_out)),
    ):
        picked = [tile(own, i)[...].astype(BF) for i in tiles]
        pay[0, :, lanes] = picked[0]
        pay[1, :, lanes] = dot(e_ref[...], jnp.concatenate(picked, axis=0)).astype(BF)


S_LANES, X_LANES = slice(0, T), slice(T, 2 * T)


def start_kernel(
    meta, order, inputs, state, e_in, e_out, x0, st, pay_in, pay_out, pick, parts
):
    place = Place(meta)
    pick_rows(order, pick)
    split_f32(state[...], parts, 0)
    parts[:, 3 * T :] = inputs[0]
    for h in range(4):
        rows = slice(h * 256, (h + 1) * 256)
        got = dot(pick[rows], parts[...])
        st[rows] = got[:, :T] + got[:, T : 2 * T] + got[:, 2 * T : 3 * T]
        x0[rows] = got[:, 3 * T :].astype(BF)
    write_payload(place, st, e_in, e_out, pay_in, pay_out, S_LANES)
    write_payload(place, x0, e_in, e_out, pay_in, pay_out, X_LANES)


def rest_kernel(order, in1, in2, cot, x1, x2, c0, c1, c2, pick, parts):
    pick_rows(order, pick)
    for k, src in enumerate((in1[0], in2[0], cot[0], cot[1], cot[2])):
        parts[:, k * T : (k + 1) * T] = src
    for h in range(4):
        rows = slice(h * 256, (h + 1) * 256)
        got = dot(pick[rows], parts[...]).astype(BF)
        for k, out in enumerate((x1, x2, c0, c1, c2)):
            out[rows] = got[:, k * T : (k + 1) * T]


def operator_kernel(counts, vals, vfg, vbg, vbd):
    for r in range(NT):
        live = jnp.where(counts[r] > 3, 1.0, 0.0)
        last = (vals[r, 3].astype(F32) * live).astype(BF)
        vfg[r, :, 0:T] = vals[r, 1]
        vfg[r, :, T : 2 * T] = vals[r, 0]
        vfg[r, :, 2 * T : 3 * T] = vals[r, 2]
        vfg[r, :, 3 * T :] = last
        vbg[r, :, T : 2 * T] = vals[r, 0].T
        if r > 0:
            vbg[r - 1, :, 2 * T :] = vals[r, 1].T
        else:
            vbd[8] = vals[r, 1].T
        if r < NT - 1:
            vbg[r + 1, :, 0:T] = vals[r, 2].T
        else:
            vbd[9] = vals[r, 2].T
        vbd[r] = last.T
    vbg[0, :, 0:T] = jnp.zeros((T, T), BF)
    vbg[NT - 1, :, 2 * T :] = jnp.zeros((T, T), BF)


def turn_kernel(vin, vout, tin, tout, tfar):
    for k in range(2):
        tin[:, k * T : (k + 1) * T] = vin[k].astype(F32).T.astype(BF)
        tout[:, k * T : (k + 1) * T] = vout[k].astype(F32).T.astype(BF)
    tfar[...] = vin[3].astype(F32).T.astype(BF)


def middle_forward(pay, got, far, out):
    out[0] = pay[0]
    out[1] = (pay[1].astype(F32) + dot(far[...], got[0])).astype(BF)


def middle_back(pay, got, far, out):
    out[0] = (pay[0].astype(F32) + dot(far[...], got[1])).astype(BF)
    out[1] = pay[1]


def forward_row(place, vfg, src, r):
    low = tile(src, place.idx(0, 1))[...] if r == 0 else tile(src, r)[...]
    high = tile(src, place.idx(7, 2))[...] if r == 7 else tile(src, r + 2)[...]
    picked = jnp.concatenate(
        [low, tile(src, r + 1)[...], high, tile(src, place.idx(r, 3))[...]], axis=0
    )
    return dot(vfg[r], picked)


def first_order(place, vfg, vin, vout, zext, d1, rin, rout, rfwd):
    tile(zext, place.pos_in)[...] = rin[0]
    tile(zext, place.pos_out)[...] = rout[0]
    for r in range(NT):
        tile(d1, r + 1)[...] = forward_row(place, vfg, zext, r).astype(BF)
    edge = tile(zext, place.e_in + 1)[...]
    lhs = jnp.concatenate([vin[0], vin[1], vin[2]], axis=1)
    total = rin[1].astype(F32) + dot(lhs, jnp.concatenate([edge, edge, rfwd[0]], axis=0))
    tile(d1, place.pos_in)[...] = total.astype(BF)
    edge = tile(zext, place.e_out + 1)[...]
    lhs = jnp.concatenate([vout[0], vout[1]], axis=1)
    total = rout[1].astype(F32) + dot(lhs, jnp.concatenate([edge, edge], axis=0))
    tile(d1, place.pos_out)[...] = total.astype(BF)


def second_order(place, vfg, zext, d1, r):
    z = tile(zext, r + 1)[...].astype(F32)
    return (2.0 * forward_row(place, vfg, d1, r) - z).astype(BF)


def gate_kernel(
    meta, st, x, rin, rout, rfwd, vfg, vin, vout, e_in, e_out, gw, gb, cw, cb,
    feats, r_out, u_out, q_out, xc_out, pay_in, pay_out, zext, d1,
):
    place = Place(meta)
    zext[T : T + ROWS, :T] = st[...].astype(BF)
    zext[T : T + ROWS, T:] = x[...]
    first_order(place, vfg, vin, vout, zext, d1, rin, rout, rfwd)
    for r in range(NT):
        d2 = second_order(place, vfg, zext, d1, r)
        z = tile(zext, r + 1)[...]
        one = tile(d1, r + 1)[...]
        row = jnp.concatenate(
            [z[:, T:], one[:, T:], d2[:, T:], z[:, :T], one[:, :T], d2[:, :T]], axis=1
        )
        tile(feats, r)[...] = row
    for h in range(4):
        rows = slice(h * 256, (h + 1) * 256)
        f = feats[rows]
        pre = dot(f, gw[...]) + gb[...]
        xc_out[rows] = dot(f[:, : 3 * T], cw[: 3 * T]) + cb[...]
        reset = jax.nn.sigmoid(pre[:, :T])
        r_out[rows] = reset
        u_out[rows] = jax.nn.sigmoid(pre[:, T:])
        q_out[rows] = (reset * st[rows]).astype(BF)
    write_payload(place, q_out, e_in, e_out, pay_in, pay_out, S_LANES)


def cand_kernel(meta, q, rin, rout, rfwd, vfg, vin, vout, e_in, e_out, cw, xc, u, st, *rest, last):
    if last:
        fq, c_out, zext, d1 = rest
    else:
        x_next, fq, c_out, st_out, pay_in, pay_out, zext, d1 = rest
    place = Place(meta)
    zext[T : T + ROWS] = q[...]
    first_order(place, vfg, vin, vout, zext, d1, rin, rout, rfwd)
    for r in range(NT):
        d2 = second_order(place, vfg, zext, d1, r)
        tile(fq, r)[...] = jnp.concatenate(
            [tile(zext, r + 1)[...], tile(d1, r + 1)[...], d2], axis=1
        )
    for h in range(4):
        rows = slice(h * 256, (h + 1) * 256)
        cand = jnp.tanh(dot(fq[rows], cw[3 * T :]) + xc[rows])
        c_out[rows] = cand
        if not last:
            st_out[rows] = u[rows] * st[rows] + (1.0 - u[rows]) * cand
    if not last:
        write_payload(place, st_out, e_in, e_out, pay_in, pay_out, S_LANES)
        write_payload(place, x_next, e_in, e_out, pay_in, pay_out, X_LANES)


def add_received(place, acc, rin, rout, rfwd, et_in, et_out, tfar):
    got_in = dot(et_in[...], rin[1])
    got_out = dot(et_out[...], rout[1])
    for i, block in (
        (place.e_in, got_in[:T] + rin[0].astype(F32) + dot(tfar[...], rfwd[1])),
        (place.n_in, got_in[T : 2 * T]),
        (place.t_in, got_in[2 * T :]),
        (place.e_out, got_out[:T] + rout[0].astype(F32)),
        (place.n_out, got_out[T : 2 * T]),
        (place.t_out, got_out[2 * T :]),
    ):
        tile(acc, i)[...] += block


def back_rows(place, vbg, vbd, y, acc, base):
    zero = jnp.zeros((T, acc.shape[1]), F32)
    tile(acc, 0)[...] = zero
    tile(acc, 9)[...] = zero
    for r in range(NT):
        lo, hi = max(r - 1, 0), min(r + 2, NT)
        lhs = vbg[r, :, (lo - r + 1) * T : (hi - r + 1) * T]
        tile(acc, r + 1)[...] = base(r, dot(lhs, y[lo * T : hi * T]))
    parts = [(place.idx(0, 1), 8, 0), (place.idx(7, 2), 9, 7)]
    parts += [(place.idx(r, 3), r, r) for r in range(NT)]
    for i, k, r in parts:
        tile(acc, i)[...] += dot(vbd[k], y[r * T : (r + 1) * T])


def diffuse_back(place, vbg, vbd, tin, tout, a, y, w, acc, pay_in, pay_out):
    for r in range(NT):
        rows = slice(r * T, (r + 1) * T)
        y[rows] = a(2, rows).astype(BF)
    back_rows(
        place, vbg, vbd, y, acc, lambda r, v: a(1, slice(r * T, (r + 1) * T)) * 0.5 + v
    )
    for e in range(NT + 2):
        tile(w, e)[...] = (2.0 * tile(acc, e)[...]).astype(BF)
    own = w.at[pl.ds(T, ROWS)]

    def second(r, v):
        rows = slice(r * T, (r + 1) * T)
        return a(0, rows) - a(2, rows) + v

    back_rows(place, vbg, vbd, own, acc, second)
    for pos, edge, vals, pay in (
        (place.pos_in, place.e_in, tin, pay_in),
        (place.pos_out, place.e_out, tout, pay_out),
    ):
        part = tile(w, pos)[...]
        tile(acc, edge + 1)[...] += dot(vals[...], jnp.concatenate([part, part], axis=0))
        pay[0] = tile(acc, pos)[...].astype(BF)
        pay[1] = part


def cand_back_kernel(*refs, first):
    refs = list(refs)
    take = lambda n: [refs.pop(0) for _ in range(n)]
    meta, cot, u, c, st, cw, vbg, vbd, tin, tout, et_in, et_out, tfar = take(13)
    if not first:
        gs_part, gx_part, rin, rout, rfwd = take(5)
    gp_out, ec_out, eu_out, gq_out, sums, pay_in, pay_out = take(7)
    if not first:
        (gx_out,) = take(1)
    gs, g, y, w, acc = take(5)
    place = Place(meta)
    if not first:
        gs[:, :T] = gs_part[...]
        gs[:, T:] = gx_part[...]
        add_received(place, gs, rin, rout, rfwd, et_in, et_out, tfar)
        gx_out[...] = gs[:, T:].astype(BF)
    sum_c = jnp.zeros((1, T), F32)
    sum_u = jnp.zeros((1, T), F32)
    for h in range(NT):
        rows = slice(h * T, (h + 1) * T)
        grad = cot[rows].astype(F32)
        if not first:
            grad = grad + gs[rows, :T]
        upd, cand = u[rows], c[rows]
        pre = grad * (1.0 - upd) * (1.0 - cand * cand)
        gate = grad * (st[rows] - cand) * upd * (1.0 - upd)
        gp_out[rows] = grad * upd
        ec_out[rows] = pre.astype(BF)
        eu_out[rows] = gate.astype(BF)
        sum_c = sum_c + jnp.sum(pre, axis=0, keepdims=True)
        sum_u = sum_u + jnp.sum(gate, axis=0, keepdims=True)
    sums[...] = jnp.broadcast_to(jnp.concatenate([sum_c, sum_u], axis=1), (8, 2 * T))
    g[...] = dot_nt(ec_out[...], cw[3 * T :])
    diffuse_back(
        place, vbg, vbd, tin, tout,
        lambda k, rows: g[rows, k * T : (k + 1) * T],
        y, w, acc, pay_in, pay_out,
    )
    gq_out[...] = acc[T : T + ROWS]


def gate_back_kernel(
    meta, gq_part, rin, rout, rfwd, gp, r_ref, st, ec, eu, gw, cw,
    vbg, vbd, tin, tout, et_in, et_out, tfar,
    gs_out, gx_out, er_out, sums, pay_in, pay_out, gq, eg, gps, g, y, w, acc,
):
    place = Place(meta)
    gq[...] = gq_part[...]
    add_received(place, gq, rin, rout, rfwd, et_in, et_out, tfar)
    sum_r = jnp.zeros((1, T), F32)
    for h in range(NT):
        rows = slice(h * T, (h + 1) * T)
        grad, reset = gq[rows], r_ref[rows]
        gps[rows] = gp[rows] + grad * reset
        pre = grad * st[rows] * reset * (1.0 - reset)
        eg[rows, :T] = pre.astype(BF)
        sum_r = sum_r + jnp.sum(pre, axis=0, keepdims=True)
    eg[:, T:] = eu[...]
    er_out[...] = eg[:, :T]
    sums[...] = jnp.broadcast_to(sum_r, (8, T))
    e = eg[...]
    for k in range(3):
        cols = slice(2 * k * T, (2 * k + 1) * T)
        g[:, cols] = dot_nt(e, gw[(3 + k) * T : (4 + k) * T])
        cols = slice((2 * k + 1) * T, (2 * k + 2) * T)
        g[:, cols] = dot_nt(e, gw[k * T : (k + 1) * T]) + dot_nt(
            ec[...], cw[k * T : (k + 1) * T]
        )
    diffuse_back(
        place, vbg, vbd, tin, tout,
        lambda k, rows: g[rows, 2 * k * T : 2 * (k + 1) * T],
        y, w, acc, pay_in, pay_out,
    )
    gs_out[...] = acc[T : T + ROWS, :T] + gps[...]
    gx_out[...] = acc[T : T + ROWS, T:]


def weight_cu_kernel(ec, eu, sums, feats, fq, *rest):
    out = rest[-1]
    x = feats[:, : 3 * T]
    out[:T, : 3 * T] = dot_tn(ec[...], x)
    out[:T, 3 * T :] = dot_tn(ec[...], fq[...])
    out[T : 2 * T] = dot_tn(eu[...], feats[...])
    row = jnp.concatenate([sums[...], jnp.zeros((8, 4 * T), F32)], axis=1)
    out[2 * T :] = jnp.concatenate([row, row], axis=0)
    if len(rest) > 1:
        out[...] += rest[0][...]


def weight_r_kernel(er, sums, feats, *rest):
    out = rest[-1]
    out[:T] = dot_tn(er[...], feats[...])
    row = jnp.concatenate([sums[...], jnp.zeros((8, 5 * T), F32)], axis=1)
    out[T:] = jnp.concatenate([row, row], axis=0)
    if len(rest) > 1:
        out[...] += rest[0][...]


def reduce_all(total, core):
    half = total.shape[1] // 2
    low, high = total[:, :half], total[:, half:]
    kept = jnp.where(core == 0, low, high)
    sent = jnp.where(core == 0, high, low).astype(BF)
    part = (kept + swap_in(sent).astype(F32)).astype(BF)
    count = lax.axis_size("wide")
    step = 2
    while step < count:
        other = lax.ppermute(part, "wide", [(i, i ^ step) for i in range(count)])
        part = (part.astype(F32) + other.astype(F32)).astype(BF)
        step *= 2
    return part, swap_in(part)


def weights_kernel(meta, cu_own, cu_other, r_own, r_other, gw, gb, cw, cb, *, scale):
    mine = meta[32] == 0

    def pick(own, other, side):
        a, b = own[...].astype(F32), other[...].astype(F32)
        return jnp.where(mine, a, b) if side == 0 else jnp.where(mine, b, a)

    for side in range(2):
        cu = pick(cu_own, cu_other, side) * scale
        r = pick(r_own, r_other, side) * scale
        for k in range(3):
            cols = slice(k * T, (k + 1) * T)
            rows = slice((3 * side + k) * T, (3 * side + k + 1) * T)
            cw[rows] = cu[:T, cols].T
            gw[rows, T:] = cu[T : 2 * T, cols].T
            gw[rows, :T] = r[:T, cols].T
        if side == 0:
            cb[...] = cu[2 * T : 2 * T + 1, :T]
            gb[:, T:] = cu[2 * T : 2 * T + 1, T : 2 * T]
            gb[:, :T] = r[T : T + 1, :T]


def finish_kernel(
    meta, order, gs_part, gx_part, rin, rout, rfwd, et_in, et_out, tfar, gx1, gx2,
    gi_out, gs_out, gs, parts,
):
    place = Place(meta)
    gs[:, :T] = gs_part[...]
    gs[:, T:] = gx_part[...]
    add_received(place, gs, rin, rout, rfwd, et_in, et_out, tfar)
    split_f32(gs[:, :T], parts, 0)
    parts[:, 3 * T : 4 * T] = gs[:, T:].astype(BF)
    parts[:, 4 * T : 5 * T] = gx1[...]
    parts[:, 5 * T :] = gx2[...]
    row = lax.broadcasted_iota(jnp.int32, (T, T), 0)
    for k in range(NT):
        put = jnp.concatenate(
            [
                (jnp.broadcast_to(order[j : j + 1, :], (T, T)) == row + k * T)
                .astype(F32)
                .astype(BF)
                for j in range(NT)
            ],
            axis=1,
        )
        rows = slice(k * T, (k + 1) * T)
        got = dot(put, parts[...])
        gs_out[rows] = got[:, :T] + got[:, T : 2 * T] + got[:, 2 * T : 3 * T]
        for t in range(3):
            gi_out[t, rows] = got[:, (3 + t) * T : (4 + t) * T].astype(BF)


SMEM = pl.BlockSpec(memory_space=pltpu.SMEM)
VMEM = pl.BlockSpec(memory_space=pltpu.VMEM)


def run(kernel, name, smem, args, outs, scratch=(), specs=None, flops=10**8):
    grid = (1,) if specs else ()
    specs = specs or [SMEM if i in smem else VMEM for i in range(len(args))]
    out_shape = [jax.ShapeDtypeStruct(s, d) for s, d in outs]
    moved = sum(x.size * x.dtype.itemsize for x in (*args, *out_shape))
    return pl.pallas_call(
        kernel,
        name=name,
        grid=grid,
        in_specs=specs,
        out_specs=[VMEM] * len(outs),
        out_shape=out_shape,
        scratch_shapes=[pltpu.VMEM(s, d) for s, d in scratch],
        cost_estimate=pl.CostEstimate(flops=flops, bytes_accessed=moved, transcendentals=0),
        compiler_params=pltpu.CompilerParams(vmem_limit_bytes=VMEM_LIMIT),
    )(*args)


def leading(block, at):
    zeros = (0,) * (len(block) - 1)
    return pl.BlockSpec(block, lambda i: (at,) + zeros, memory_space=pltpu.VMEM)


def per_device(
    inputs, state_init, cotangent, gate_w, gate_b, cand_w, cand_b,
    tile_vals, tile_cols, tile_counts, sector_order,
):
    device = lax.axis_index("wide")
    core = device % 2
    local_cols = tile_cols - (device * NT - 1)
    meta = jnp.concatenate([local_cols.reshape(-1), core[None]]).astype(jnp.int32)
    order = sector_order.reshape(NT, T)
    gb = gate_b.reshape(1, -1)
    cb = cand_b.reshape(1, -1)
    big = (ROWS, T)
    square = (T, T)
    flat, tall = ((T, 3 * T), BF), ((3 * T, T), BF)
    row_block, x_block = (1, 4, T, T), (1, ROWS, T)
    e_in, e_out, et_in, et_out, f_out, ft_in, s_in, s_out = run(
        edge_kernel, "edges", (), (meta, tile_counts, tile_vals, tile_vals),
        [flat, flat, tall, tall, (square, BF), (square, BF), ((4, T, T), BF), ((2, T, T), BF)],
        specs=[SMEM, SMEM, leading(row_block, 0), leading(row_block, NT - 1)],
    )
    vin, vout = swap_in(s_in), swap_out(s_out)
    x0, st, *pay = run(
        start_kernel, "start", (), (meta, order, inputs, state_init, e_in, e_out),
        [(big, BF), (big, F32)] + [((2, T, 2 * T), BF)] * 2,
        [((ROWS, ROWS), BF), ((ROWS, 4 * T), BF)],
        specs=[SMEM, VMEM, leading(x_block, 0), VMEM, VMEM, VMEM],
        flops=10**9,
    )
    vfg, vbg, vbd = run(
        operator_kernel, "operator", (0,), (tile_counts, tile_vals),
        [((NT, T, 4 * T), BF), ((NT, T, 3 * T), BF), ((NT + 2, T, T), BF)],
    )
    x1, x2, *cots = run(
        rest_kernel, "rest", (), (order, inputs, inputs, cotangent), [(big, BF)] * 5,
        [((ROWS, ROWS), BF), ((ROWS, 5 * T), BF)],
        specs=[VMEM, leading(x_block, 1), leading(x_block, 2), VMEM],
        flops=10**9,
    )
    tin, tout, tfar = run(
        turn_kernel, "turn", (), (vin, vout), [((T, 2 * T), BF)] * 2 + [(square, BF)]
    )
    xs = (x0, x1, x2)
    saved = []
    steps = inputs.shape[0]
    wide = ((NT + 2) * T, 2 * T)
    slim = ((NT + 2) * T, T)
    ops = (vfg, vin, vout, e_in, e_out)
    for t in range(steps):
        got = exchange(*pay, f_out, middle_forward)
        feats, r, u, q, xc, *pay = run(
            gate_kernel,
            "gate",
            (0,),
            (meta, st, xs[t], *got, *ops, gate_w, gb, cand_w, cb),
            [((ROWS, 6 * T), BF), (big, F32), (big, F32), (big, BF), (big, F32)]
            + [((2, T, T), BF)] * 2,
            [(wide, BF)] * 2,
        )
        got = exchange(*pay, f_out, middle_forward)
        last = t == steps - 1
        fq, c, *rest = run(
            functools.partial(cand_kernel, last=last),
            "cand",
            (0,),
            (meta, q, *got, *ops, cand_w, xc, u, st) + (() if last else (xs[t + 1],)),
            [((ROWS, 3 * T), BF), (big, F32)]
            + ([] if last else [(big, F32)] + [((2, T, 2 * T), BF)] * 2),
            [(slim, BF)] * 2,
        )
        saved.append((st, feats, r, u, fq, c))
        if not last:
            st, *pay = rest
    ops = (vbg, vbd, tin, tout, et_in, et_out, tfar)
    gxs = [None] * steps
    carry, cu_sum, r_sum = (), (), ()
    for t in reversed(range(steps)):
        st, feats, r, u, fq, c = saved[t]
        first = t == steps - 1
        gp, ec, eu, gq, sums, *rest = run(
            functools.partial(cand_back_kernel, first=first),
            "cand_back",
            (0,),
            (meta, cots[t], u, c, st, cand_w) + ops + carry,
            [(big, F32), (big, BF), (big, BF), (big, F32), ((8, 2 * T), F32)]
            + [((2, T, T), BF)] * 2
            + ([] if first else [(big, BF)]),
            [((ROWS, 2 * T), F32), ((ROWS, 3 * T), F32), (big, BF), (slim, BF), (slim, F32)],
        )
        if not first:
            gxs[t + 1] = rest[2]
        got = exchange(*rest[:2], ft_in, middle_back)
        cu_sum = run(
            weight_cu_kernel, "weight_cu", (), (ec, eu, sums, feats, fq, *cu_sum),
            [((2 * T + 16, 6 * T), F32)], flops=4 * 10**8,
        )
        gs_part, gx_part, er, sums, *rest = run(
            gate_back_kernel,
            "gate_back",
            (0,),
            (meta, gq, *got, gp, r, st, ec, eu, gate_w, cand_w) + ops,
            [(big, F32), (big, F32), (big, BF), ((8, T), F32)] + [((2, T, 2 * T), BF)] * 2,
            [
                (big, F32), ((ROWS, 2 * T), BF), (big, F32), ((ROWS, 6 * T), F32),
                ((ROWS, 2 * T), BF), (wide, BF), (wide, F32),
            ],
        )
        r_sum = run(
            weight_r_kernel, "weight_r", (), (er, sums, feats, *r_sum),
            [((T + 16, 6 * T), F32)], flops=2 * 10**8,
        )
        got = exchange(*rest, ft_in, middle_back)
        carry = (gs_part, gx_part, *got)
    cu = reduce_all(cu_sum[0], core)
    rr = reduce_all(r_sum[0], core)
    gi, gs = run(
        finish_kernel,
        "finish",
        (0,),
        (meta, order, *carry, et_in, et_out, tfar, gxs[1], gxs[2]),
        [((steps,) + big, BF), (big, F32)],
        [((ROWS, 2 * T), F32), ((ROWS, 6 * T), BF)],
    )
    scale = 1.0 / math.sqrt(ROWS * lax.axis_size("wide") * steps)
    gw, gb, cw, cb = run(
        functools.partial(weights_kernel, scale=scale),
        "weights",
        (0,),
        (meta, *cu, *rr),
        [((6 * T, 2 * T), F32), ((1, 2 * T), F32), ((6 * T, T), F32), ((1, T), F32)],
    )
    return gi, gs, gw, gb.reshape(-1), cw, cb.reshape(-1)


def solution(mesh):
    return jax.shard_map(
        per_device,
        mesh=mesh,
        in_specs=(
            P(None, ("parts", "wide"), None),
            P(("parts", "wide"), None),
            P(None, ("parts", "wide"), None),
            P(),
            P(),
            P(),
            P(),
            P(("parts", "wide"), None, None, None),
            P(("parts", "wide"), None),
            P(("parts", "wide")),
            P(("parts", "wide")),
        ),
        out_specs=(
            P(None, ("parts", "wide"), None),
            P(("parts", "wide"), None),
            P("parts", None),
            P("parts"),
            P("parts", None),
            P("parts"),
        ),
        check_vma=False,
    )
```

```python
import functools
import math

import jax
import jax.numpy as jnp
from jax import lax
from jax.experimental import pallas as pl
from jax.experimental.pallas import tpu as pltpu
from jax.sharding import PartitionSpec as P

BF = jnp.bfloat16
F32 = jnp.float32
T = 128
NT = 8
ROWS = NT * T
COUNTS = 34
VMEM_LIMIT = 14 * 1024 * 1024


def swap(block, start):
    count = lax.axis_size("wide")
    return lax.ppermute(
        block, "wide", [p for i in range(start, count - 1, 2) for p in ((i, i + 1), (i + 1, i))]
    )


def swap_in(block):
    return swap(block, 0)


def swap_out(block):
    return swap(block, 1)


def exchange(pay_in, pay_out, far, middle, beside=()):
    got_in = swap_in(pay_in)
    (ready,) = run(middle, "middle", (), (pay_out, got_in, far), [(pay_out.shape, BF)])
    got_out = swap_out(ready)
    got_out, beside = lax.optimization_barrier((got_out, tuple(beside)))
    return (got_in, got_out, swap_in(got_out)), beside


def dot(a, b):
    return jnp.dot(a, b, preferred_element_type=F32)


def dot_nt(a, b):
    return lax.dot_general(a, b, (((1,), (1,)), ((), ())), preferred_element_type=F32)


def dot_tn(a, b):
    return lax.dot_general(a, b, (((0,), (0,)), ((), ())), preferred_element_type=F32)


def tile(ref, i):
    start = i * T if isinstance(i, int) else pl.multiple_of(i * T, T)
    return ref.at[pl.ds(start, T)]


class Place:
    def __init__(self, meta):
        self.idx = lambda r, s: meta[4 * r + s]
        core = meta[32]
        self.core = core
        self.e_in = 7 - 7 * core
        self.n_in = 6 - 5 * core
        self.e_out = 7 * core
        self.n_out = 1 + 5 * core
        self.pos_in = 9 - 9 * core
        self.pos_out = 9 * core
        self.col_in = jnp.where(core == 0, meta[4 * 7 + 3], meta[3])
        self.col_out = jnp.where(core == 0, meta[3], meta[4 * 7 + 3])
        self.t_in = jnp.clip(self.col_in - 1, 0, NT - 1)
        self.t_out = jnp.clip(self.col_out - 1, 0, NT - 1)


def copies(sems, *pairs):
    started = [pltpu.make_async_copy(a, b, sems.at[k]) for k, (a, b) in enumerate(pairs)]
    for copy in started:
        copy.start()

    def wait():
        for copy in started:
            copy.wait()

    return wait


def edge_kernel(
    cols, counts, vals_hbm, meta, e_in, e_out, et_in, et_out, f_out, ft_in, s_in, s_out, first, last, sems
):
    wait = copies(sems, (vals_hbm.at[0], first), (vals_hbm.at[NT - 1], last))
    device = lax.axis_index("wide")
    for r in range(NT):
        for k in range(4):
            meta[4 * r + k] = cols[k, r] - (device * NT - 1)
        meta[COUNTS + r] = counts[r]
    meta[32] = device % 2
    meta[33] = device // 2 % 2
    place = Place(meta)
    wait()
    zero = place.core == 0
    for low, side_row, row_far, them, far in (
        (False, place.e_in, place.col_in, place.pos_in, place.pos_out),
        (True, place.e_out, place.col_out, place.pos_out, place.pos_in),
    ):
        top = zero if low else jnp.logical_not(zero)
        vals = [jnp.where(top, first[k].astype(F32), last[k].astype(F32)) for k in range(4)]
        inside = jnp.where(top, vals[2], vals[1])
        ahead = jnp.where(top, vals[1], vals[2])
        live = meta[COUNTS + side_row] > 3

        def third(flag):
            return vals[3] * jnp.where(jnp.logical_and(live, flag), 1.0, 0.0)

        is_them, is_far = row_far == them, row_far == far
        own = third(jnp.logical_not(jnp.logical_or(is_them, is_far)))
        e_ref, et_ref = (e_out, et_out) if low else (e_in, et_in)
        for k, v in enumerate((vals[0], inside, own)):
            e_ref[:, k * T : (k + 1) * T] = v.astype(BF)
            et_ref[k * T : (k + 1) * T] = v.T.astype(BF)
        s_ref = s_out if low else s_in
        s_ref[0] = ahead.astype(BF)
        s_ref[1] = third(is_them).astype(BF)
        if low:
            f_out[...] = third(is_far).astype(BF)
            s_in[3] = third(is_far).astype(BF)
        else:
            s_ref[2] = third(is_far).astype(BF)
            ft_in[...] = third(is_far).T.astype(BF)


def pick_rows(order, pick):
    lane = lax.broadcasted_iota(jnp.int32, (T, T), 1).astype(F32)
    for j in range(NT):
        wanted = jnp.broadcast_to(order[j : j + 1, :].astype(F32), (T, T)).T
        for k in range(NT):
            pick[j * T : (j + 1) * T, k * T : (k + 1) * T] = (
                (wanted == lane + float(k * T)).astype(F32).astype(BF)
            )


def split_f32(value, ref, start):
    for k in range(3):
        part = value.astype(BF)
        ref[:, start + k * T : start + (k + 1) * T] = part
        value = value - part.astype(F32)


def write_payload(place, own, e_in, e_out, pay_in, pay_out, lanes):
    for e_ref, pay, tiles in (
        (e_in, pay_in, (place.e_in, place.n_in, place.t_in)),
        (e_out, pay_out, (place.e_out, place.n_out, place.t_out)),
    ):
        picked = [tile(own, i)[...].astype(BF) for i in tiles]
        pay[0, :, lanes] = picked[0]
        pay[1, :, lanes] = dot(e_ref[...], jnp.concatenate(picked, axis=0)).astype(BF)


S_LANES, X_LANES = slice(0, T), slice(T, 2 * T)


def start_kernel(
    meta, order, inputs, state, e_in, e_out, x0, st, pay_in, pay_out, pick, parts, given, sems
):
    place = Place(meta)
    wait = copies(sems, (inputs.at[0], given))
    pick_rows(order, pick)
    split_f32(state[...], parts, 0)
    wait()
    parts[:, 3 * T :] = given[...]
    for h in range(4):
        rows = slice(h * 256, (h + 1) * 256)
        got = dot(pick[rows], parts[...])
        st[rows] = got[:, :T] + got[:, T : 2 * T] + got[:, 2 * T : 3 * T]
        x0[rows] = got[:, 3 * T :].astype(BF)
    write_payload(place, st, e_in, e_out, pay_in, pay_out, S_LANES)
    write_payload(place, x0, e_in, e_out, pay_in, pay_out, X_LANES)


def rest_kernel(order, in1, in2, cot, x1, x2, c0, c1, c2, pick, parts):
    pick_rows(order, pick)
    for k, src in enumerate((in1[0], in2[0], cot[0], cot[1], cot[2])):
        parts[:, k * T : (k + 1) * T] = src
    for h in range(4):
        rows = slice(h * 256, (h + 1) * 256)
        got = dot(pick[rows], parts[...]).astype(BF)
        for k, out in enumerate((x1, x2, c0, c1, c2)):
            out[rows] = got[:, k * T : (k + 1) * T]


def operator_kernel(meta, vals, vfg, vbg, vbd):
    for r in range(NT):
        live = jnp.where(meta[COUNTS + r] > 3, 1.0, 0.0)
        last = (vals[r, 3].astype(F32) * live).astype(BF)
        vfg[r, :, 0:T] = vals[r, 1]
        vfg[r, :, T : 2 * T] = vals[r, 0]
        vfg[r, :, 2 * T : 3 * T] = vals[r, 2]
        vfg[r, :, 3 * T :] = last
        vbg[r, :, T : 2 * T] = vals[r, 0].T
        if r > 0:
            vbg[r - 1, :, 2 * T :] = vals[r, 1].T
        else:
            vbd[8] = vals[r, 1].T
        if r < NT - 1:
            vbg[r + 1, :, 0:T] = vals[r, 2].T
        else:
            vbd[9] = vals[r, 2].T
        vbd[r] = last.T
    vbg[0, :, 0:T] = jnp.zeros((T, T), BF)
    vbg[NT - 1, :, 2 * T :] = jnp.zeros((T, T), BF)


def turn_kernel(vin, vout, tin, tout, tfar):
    for k in range(2):
        tin[:, k * T : (k + 1) * T] = vin[k].astype(F32).T.astype(BF)
        tout[:, k * T : (k + 1) * T] = vout[k].astype(F32).T.astype(BF)
    tfar[...] = vin[3].astype(F32).T.astype(BF)


def middle_forward(pay, got, far, out):
    out[0] = pay[0]
    out[1] = (pay[1].astype(F32) + dot(far[...], got[0])).astype(BF)


def middle_back(pay, got, far, out):
    out[0] = (pay[0].astype(F32) + dot(far[...], got[1])).astype(BF)
    out[1] = pay[1]


def forward_row(place, vfg, src, r):
    low = tile(src, place.idx(0, 1))[...] if r == 0 else tile(src, r)[...]
    high = tile(src, place.idx(7, 2))[...] if r == 7 else tile(src, r + 2)[...]
    picked = jnp.concatenate(
        [low, tile(src, r + 1)[...], high, tile(src, place.idx(r, 3))[...]], axis=0
    )
    return dot(vfg[r], picked)


def first_order(place, vfg, vin, vout, zext, d1, rin, rout, rfwd):
    tile(zext, place.pos_in)[...] = rin[0]
    tile(zext, place.pos_out)[...] = rout[0]
    for r in range(NT):
        tile(d1, r + 1)[...] = forward_row(place, vfg, zext, r).astype(BF)
    edge = tile(zext, place.e_in + 1)[...]
    lhs = jnp.concatenate([vin[0], vin[1], vin[2]], axis=1)
    total = rin[1].astype(F32) + dot(lhs, jnp.concatenate([edge, edge, rfwd[0]], axis=0))
    tile(d1, place.pos_in)[...] = total.astype(BF)
    edge = tile(zext, place.e_out + 1)[...]
    lhs = jnp.concatenate([vout[0], vout[1]], axis=1)
    total = rout[1].astype(F32) + dot(lhs, jnp.concatenate([edge, edge], axis=0))
    tile(d1, place.pos_out)[...] = total.astype(BF)


def second_order(place, vfg, zext, d1, r):
    z = tile(zext, r + 1)[...].astype(F32)
    return (2.0 * forward_row(place, vfg, d1, r) - z).astype(BF)


def gate_kernel(
    meta, st, x, rin, rout, rfwd, vfg, vin, vout, e_in, e_out, gw, gb,
    feats, r_out, q_out, pay_in, pay_out, zext, d1,
):
    place = Place(meta)
    zext[T : T + ROWS, :T] = st[...].astype(BF)
    zext[T : T + ROWS, T:] = x[...]
    first_order(place, vfg, vin, vout, zext, d1, rin, rout, rfwd)
    for r in range(NT):
        d2 = second_order(place, vfg, zext, d1, r)
        z = tile(zext, r + 1)[...]
        one = tile(d1, r + 1)[...]
        row = jnp.concatenate(
            [z[:, T:], one[:, T:], d2[:, T:], z[:, :T], one[:, :T], d2[:, :T]], axis=1
        )
        tile(feats, r)[...] = row
    for h in range(4):
        rows = slice(h * 256, (h + 1) * 256)
        reset = jax.nn.sigmoid(dot(feats[rows], gw[:, :T]) + gb[:, :T])
        r_out[rows] = reset
        q_out[rows] = (reset * st[rows]).astype(BF)
    write_payload(place, q_out, e_in, e_out, pay_in, pay_out, S_LANES)


def update_kernel(feats, gw, gb, cw, cb, u_out, xc_out):
    for h in range(4):
        rows = slice(h * 256, (h + 1) * 256)
        f = feats[rows]
        u_out[rows] = jax.nn.sigmoid(dot(f, gw[:, T:]) + gb[:, T:])
        xc_out[rows] = dot(f[:, : 3 * T], cw[: 3 * T]) + cb[...]


def cand_kernel(meta, q, rin, rout, rfwd, vfg, vin, vout, e_in, e_out, cw, xc, u, st, *rest, last):
    if last:
        fq, c_out, zext, d1 = rest
    else:
        x_next, fq, c_out, st_out, pay_in, pay_out, zext, d1 = rest
    place = Place(meta)
    zext[T : T + ROWS] = q[...]
    first_order(place, vfg, vin, vout, zext, d1, rin, rout, rfwd)
    for r in range(NT):
        d2 = second_order(place, vfg, zext, d1, r)
        tile(fq, r)[...] = jnp.concatenate(
            [tile(zext, r + 1)[...], tile(d1, r + 1)[...], d2], axis=1
        )
    for h in range(4):
        rows = slice(h * 256, (h + 1) * 256)
        cand = jnp.tanh(dot(fq[rows], cw[3 * T :]) + xc[rows])
        c_out[rows] = cand
        if not last:
            st_out[rows] = u[rows] * st[rows] + (1.0 - u[rows]) * cand
    if not last:
        write_payload(place, st_out, e_in, e_out, pay_in, pay_out, S_LANES)
        write_payload(place, x_next, e_in, e_out, pay_in, pay_out, X_LANES)


def add_received(place, acc, rin, rout, rfwd, et_in, et_out, tfar):
    got_in = dot(et_in[...], rin[1])
    got_out = dot(et_out[...], rout[1])
    for i, block in (
        (place.e_in, got_in[:T] + rin[0].astype(F32) + dot(tfar[...], rfwd[1])),
        (place.n_in, got_in[T : 2 * T]),
        (place.t_in, got_in[2 * T :]),
        (place.e_out, got_out[:T] + rout[0].astype(F32)),
        (place.n_out, got_out[T : 2 * T]),
        (place.t_out, got_out[2 * T :]),
    ):
        tile(acc, i)[...] += block


def back_rows(place, vbg, vbd, y, acc, base):
    zero = jnp.zeros((T, acc.shape[1]), F32)
    tile(acc, 0)[...] = zero
    tile(acc, 9)[...] = zero
    for r in range(NT):
        lo, hi = max(r - 1, 0), min(r + 2, NT)
        lhs = vbg[r, :, (lo - r + 1) * T : (hi - r + 1) * T]
        tile(acc, r + 1)[...] = base(r, dot(lhs, y[lo * T : hi * T]))
    parts = [(place.idx(0, 1), 8, 0), (place.idx(7, 2), 9, 7)]
    parts += [(place.idx(r, 3), r, r) for r in range(NT)]
    for i, k, r in parts:
        tile(acc, i)[...] += dot(vbd[k], y[r * T : (r + 1) * T])


def diffuse_back(place, vbg, vbd, tin, tout, a, y, w, acc, pay_in, pay_out):
    for r in range(NT):
        rows = slice(r * T, (r + 1) * T)
        y[rows] = a(2, rows).astype(BF)
    back_rows(
        place, vbg, vbd, y, acc, lambda r, v: a(1, slice(r * T, (r + 1) * T)) * 0.5 + v
    )
    for e in range(NT + 2):
        tile(w, e)[...] = (2.0 * tile(acc, e)[...]).astype(BF)
    own = w.at[pl.ds(T, ROWS)]

    def second(r, v):
        rows = slice(r * T, (r + 1) * T)
        return a(0, rows) - a(2, rows) + v

    back_rows(place, vbg, vbd, own, acc, second)
    for pos, edge, vals, pay in (
        (place.pos_in, place.e_in, tin, pay_in),
        (place.pos_out, place.e_out, tout, pay_out),
    ):
        part = tile(w, pos)[...]
        tile(acc, edge + 1)[...] += dot(vals[...], jnp.concatenate([part, part], axis=0))
        pay[0] = tile(acc, pos)[...].astype(BF)
        pay[1] = part


def cand_back_kernel(*refs, first):
    refs = list(refs)
    take = lambda n: [refs.pop(0) for _ in range(n)]
    meta, cot, u, c, st, cw, vbg, vbd, tin, tout, et_in, et_out, tfar = take(13)
    if not first:
        gs_part, gx_part, rin, rout, rfwd = take(5)
    gp_out, ec_out, eu_out, gq_out, sums, pay_in, pay_out = take(7)
    if not first:
        (gx_out,) = take(1)
    gs, g, y, w, acc = take(5)
    place = Place(meta)
    if not first:
        gs[:, :T] = gs_part[...]
        gs[:, T:] = gx_part[...]
        add_received(place, gs, rin, rout, rfwd, et_in, et_out, tfar)
        gx_out[...] = gs[:, T:].astype(BF)
    sum_c = jnp.zeros((1, T), F32)
    sum_u = jnp.zeros((1, T), F32)
    for h in range(NT):
        rows = slice(h * T, (h + 1) * T)
        grad = cot[rows].astype(F32)
        if not first:
            grad = grad + gs[rows, :T]
        upd, cand = u[rows], c[rows]
        pre = grad * (1.0 - upd) * (1.0 - cand * cand)
        gate = grad * (st[rows] - cand) * upd * (1.0 - upd)
        gp_out[rows] = grad * upd
        ec_out[rows] = pre.astype(BF)
        eu_out[rows] = gate.astype(BF)
        sum_c = sum_c + jnp.sum(pre, axis=0, keepdims=True)
        sum_u = sum_u + jnp.sum(gate, axis=0, keepdims=True)
    sums[...] = jnp.broadcast_to(jnp.concatenate([sum_c, sum_u], axis=1), (8, 2 * T))
    g[...] = dot_nt(ec_out[...], cw[3 * T :])
    diffuse_back(
        place, vbg, vbd, tin, tout,
        lambda k, rows: g[rows, k * T : (k + 1) * T],
        y, w, acc, pay_in, pay_out,
    )
    gq_out[...] = acc[T : T + ROWS]


def gate_back_kernel(
    meta, gq_part, rin, rout, rfwd, gp, r_ref, st, ec, eu, gw, cw,
    vbg, vbd, tin, tout, et_in, et_out, tfar,
    gs_out, gx_out, er_out, sums, pay_in, pay_out, gq, eg, gps, g, y, w, acc,
):
    place = Place(meta)
    gq[...] = gq_part[...]
    add_received(place, gq, rin, rout, rfwd, et_in, et_out, tfar)
    sum_r = jnp.zeros((1, T), F32)
    for h in range(NT):
        rows = slice(h * T, (h + 1) * T)
        grad, reset = gq[rows], r_ref[rows]
        gps[rows] = gp[rows] + grad * reset
        pre = grad * st[rows] * reset * (1.0 - reset)
        eg[rows, :T] = pre.astype(BF)
        sum_r = sum_r + jnp.sum(pre, axis=0, keepdims=True)
    eg[:, T:] = eu[...]
    er_out[...] = eg[:, :T]
    sums[...] = jnp.broadcast_to(sum_r, (8, T))
    e = eg[...]
    for k in range(3):
        cols = slice(2 * k * T, (2 * k + 1) * T)
        g[:, cols] = dot_nt(e, gw[(3 + k) * T : (4 + k) * T])
        cols = slice((2 * k + 1) * T, (2 * k + 2) * T)
        g[:, cols] = dot_nt(e, gw[k * T : (k + 1) * T]) + dot_nt(
            ec[...], cw[k * T : (k + 1) * T]
        )
    diffuse_back(
        place, vbg, vbd, tin, tout,
        lambda k, rows: g[rows, 2 * k * T : 2 * (k + 1) * T],
        y, w, acc, pay_in, pay_out,
    )
    gs_out[...] = acc[T : T + ROWS, :T] + gps[...]
    gx_out[...] = acc[T : T + ROWS, T:]


def add_rows(out, value, rest, rows):
    out[rows] = value + rest[0][rows] if rest else value


def split_columns(meta, total, kept, sent):
    half = total.shape[1] // 2
    mine = meta[32] == 0
    low, high = total[:, :half], total[:, half:]
    kept[...] = jnp.where(mine, low, high)
    sent[...] = jnp.where(mine, high, low).astype(BF)


def weight_cu_kernel(meta, ec, eu, sums, feats, fq, *rest):
    *rest, out = rest
    x = feats[:, : 3 * T]
    both = jnp.concatenate([dot_tn(ec[...], x), dot_tn(ec[...], fq[...])], axis=1)
    add_rows(out, both, rest, slice(0, T))
    add_rows(out, dot_tn(eu[...], feats[...]), rest, slice(T, 2 * T))
    row = jnp.concatenate([sums[...], jnp.zeros((8, 4 * T), F32)], axis=1)
    add_rows(out, jnp.concatenate([row] * 4, axis=0), rest, slice(2 * T, 2 * T + 32))


def weight_cu_last_kernel(meta, ec, eu, sums, feats, fq, before, kept, sent, out):
    weight_cu_kernel(meta, ec, eu, sums, feats, fq, before, out)
    split_columns(meta, out, kept, sent)


def weight_r_kernel(meta, er, sums, feats, *rest):
    *rest, out = rest
    add_rows(out, dot_tn(er[...], feats[...]), rest, slice(0, T))
    row = jnp.concatenate([sums[...], jnp.zeros((8, 5 * T), F32)], axis=1)
    add_rows(out, jnp.concatenate([row, row], axis=0), rest, slice(T, T + 16))


def weight_r_last_kernel(meta, er, sums, feats, before, kept, sent, out):
    weight_r_kernel(meta, er, sums, feats, before, out)
    split_columns(meta, out, kept, sent)


def add_kernel(a, b, out):
    out[...] = (a[...].astype(F32) + b[...].astype(F32)).astype(BF)


def add_split_kernel(meta, a, b, kept, sent):
    total = (a[...].astype(F32) + b[...].astype(F32)).astype(BF)
    half = total.shape[0] // 2
    upper = meta[33] == 1
    top, bottom = total[:half].astype(F32), total[half:].astype(F32)
    kept[...] = jnp.where(upper, bottom, top).astype(BF)
    sent[...] = jnp.where(upper, top, bottom).astype(BF)


def sum_of(a, b):
    return run(add_kernel, "add", (), (a, b), [(a.shape, BF)])[0]


def reduce_step(part, step):
    count = lax.axis_size("wide")
    other = lax.ppermute(part, "wide", [(i, i ^ step) for i in range(count)])
    return sum_of(part, other)


def reduce_rows(kept, sent):
    count = lax.axis_size("wide")
    route = [(i, i ^ 2) for i in range(count)]
    part = sum_of(kept, lax.ppermute(sent, "wide", route))
    step = 4
    while step < count:
        part = reduce_step(part, step)
        step *= 2
    return part, lax.ppermute(part, "wide", route)


def reduce_rest(part, step):
    while step < lax.axis_size("wide"):
        part = reduce_step(part, step)
        step *= 2
    return part, swap_in(part)


def weights_kernel(
    meta, cu_a, cu_b, cu_a_other, cu_b_other, r_own, r_other, gw, gb, cw, cb, *, scale
):
    mine = meta[32] == 0
    upper = meta[33] == 1

    def pick(own, other, side):
        a, b = own[...].astype(F32), other[...].astype(F32)
        return jnp.where(mine, a, b) if side == 0 else jnp.where(mine, b, a)

    def rows_of(a, b):
        low, high = jnp.where(upper, b, a), jnp.where(upper, a, b)
        return jnp.concatenate([low, high], axis=0)

    for side in range(2):
        cu = rows_of(pick(cu_a, cu_a_other, side), pick(cu_b, cu_b_other, side)) * scale
        r = pick(r_own, r_other, side) * scale
        for k in range(3):
            cols = slice(k * T, (k + 1) * T)
            rows = slice((3 * side + k) * T, (3 * side + k + 1) * T)
            cw[rows] = cu[:T, cols].T
            gw[rows, T:] = cu[T : 2 * T, cols].T
            gw[rows, :T] = r[:T, cols].T
        if side == 0:
            cb[...] = cu[2 * T : 2 * T + 1, :T]
            gb[:, T:] = cu[2 * T : 2 * T + 1, T : 2 * T]
            gb[:, :T] = r[T : T + 1, :T]


def finish_kernel(
    meta, order, gs_part, gx_part, rin, rout, rfwd, et_in, et_out, tfar, gx1, gx2,
    gi_out, gs_out, gs, parts,
):
    place = Place(meta)
    gs[:, :T] = gs_part[...]
    gs[:, T:] = gx_part[...]
    add_received(place, gs, rin, rout, rfwd, et_in, et_out, tfar)
    split_f32(gs[:, :T], parts, 0)
    parts[:, 3 * T : 4 * T] = gs[:, T:].astype(BF)
    parts[:, 4 * T : 5 * T] = gx1[...]
    parts[:, 5 * T :] = gx2[...]
    row = lax.broadcasted_iota(jnp.int32, (T, T), 0)
    for k in range(NT):
        put = jnp.concatenate(
            [
                (jnp.broadcast_to(order[j : j + 1, :], (T, T)) == row + k * T)
                .astype(F32)
                .astype(BF)
                for j in range(NT)
            ],
            axis=1,
        )
        rows = slice(k * T, (k + 1) * T)
        got = dot(put, parts[...])
        gs_out[rows] = got[:, :T] + got[:, T : 2 * T] + got[:, 2 * T : 3 * T]
        for t in range(3):
            gi_out[t, rows] = got[:, (3 + t) * T : (4 + t) * T].astype(BF)


SMEM = pl.BlockSpec(memory_space=pltpu.SMEM)
VMEM = pl.BlockSpec(memory_space=pltpu.VMEM)


HBM = pl.BlockSpec(memory_space=pltpu.HBM)


def run(
    kernel, name, smem, args, outs, scratch=(), specs=None, flops=10**8,
    hbm=(), smem_outs=(), sems=0,
):
    grid = (1,) if specs else ()
    specs = specs or [
        SMEM if i in smem else HBM if i in hbm else VMEM for i in range(len(args))
    ]
    out_shape = [jax.ShapeDtypeStruct(s, d) for s, d in outs]
    args = [
        pltpu.with_memory_space_constraint(x, pltpu.HBM) if i in hbm else x
        for i, x in enumerate(args)
    ]
    moved = sum(math.prod(x.shape) * x.dtype.itemsize for x in (*args, *out_shape))
    return pl.pallas_call(
        kernel,
        name=name,
        grid=grid,
        in_specs=specs,
        out_specs=[SMEM if i in smem_outs else VMEM for i in range(len(outs))],
        out_shape=out_shape,
        scratch_shapes=[pltpu.VMEM(s, d) for s, d in scratch]
        + ([pltpu.SemaphoreType.DMA((sems,))] if sems else []),
        cost_estimate=pl.CostEstimate(flops=flops, bytes_accessed=moved, transcendentals=0),
        compiler_params=pltpu.CompilerParams(vmem_limit_bytes=VMEM_LIMIT),
    )(*args)


def leading(block, at):
    zeros = (0,) * (len(block) - 1)
    return pl.BlockSpec(block, lambda i: (at,) + zeros, memory_space=pltpu.VMEM)


def per_device(
    inputs, state_init, cotangent, gate_w, gate_b, cand_w, cand_b,
    tile_vals, tile_cols, tile_counts, sector_order,
):
    order = sector_order.reshape(NT, T)
    gb = gate_b.reshape(1, -1)
    cb = cand_b.reshape(1, -1)
    big = (ROWS, T)
    square = (T, T)
    flat, tall = ((T, 3 * T), BF), ((3 * T, T), BF)
    x_block = (1, ROWS, T)
    meta, e_in, e_out, et_in, et_out, f_out, ft_in, s_in, s_out = run(
        edge_kernel, "edges", (0, 1), (tile_cols.T, tile_counts, tile_vals),
        [((COUNTS + NT,), jnp.int32), flat, flat, tall, tall, (square, BF), (square, BF), ((4, T, T), BF), ((2, T, T), BF)],
        [((4, T, T), BF)] * 2, hbm=(2,), sems=2, smem_outs=(0,),
    )
    vin, vout = swap_in(s_in), swap_out(s_out)
    x0, st, *pay = run(
        start_kernel, "start", (0,), (meta, order, inputs, state_init, e_in, e_out),
        [(big, BF), (big, F32)] + [((2, T, 2 * T), BF)] * 2,
        [((ROWS, ROWS), BF), ((ROWS, 4 * T), BF), (big, BF)],
        hbm=(2,), sems=1,
        flops=10**9,
    )
    vfg, vbg, vbd = run(
        operator_kernel, "operator", (0,), (meta, tile_vals),
        [((NT, T, 4 * T), BF), ((NT, T, 3 * T), BF), ((NT + 2, T, T), BF)],
    )
    x1, x2, *cots = run(
        rest_kernel, "rest", (), (order, inputs, inputs, cotangent), [(big, BF)] * 5,
        [((ROWS, ROWS), BF), ((ROWS, 5 * T), BF)],
        specs=[VMEM, leading(x_block, 1), leading(x_block, 2), VMEM],
        flops=10**9,
    )
    tin, tout, tfar = run(
        turn_kernel, "turn", (), (vin, vout), [((T, 2 * T), BF)] * 2 + [(square, BF)]
    )
    saved = []
    steps = inputs.shape[0]
    wide = ((NT + 2) * T, 2 * T)
    slim = ((NT + 2) * T, T)
    beside = (x1, x2, *cots, vfg, vbg, vbd, tin, tout, tfar)
    for t in range(steps):
        last = t == steps - 1
        got, beside = exchange(*pay, f_out, middle_forward, beside)
        if t == 0:
            x1, x2, *cots, vfg, vbg, vbd, tin, tout, tfar = beside
            xs = (x0, x1, x2)
            ops = (vfg, vin, vout, e_in, e_out)
        feats, r, q, *pay = run(
            gate_kernel,
            "gate",
            (0,),
            (meta, st, xs[t], *got, *ops, gate_w, gb),
            [((ROWS, 6 * T), BF), (big, F32), (big, BF)] + [((2, T, T), BF)] * 2,
            [(wide, BF)] * 2,
        )
        beside = run(
            update_kernel,
            "update",
            (),
            (feats, gate_w, gb, cand_w, cb),
            [(big, F32)] * 2,
            flops=5 * 10**8,
        )
        got, (u, xc) = exchange(*pay, f_out, middle_forward, beside)
        fq, c, *rest = run(
            functools.partial(cand_kernel, last=last),
            "cand",
            (0,),
            (meta, q, *got, *ops, cand_w, xc, u, st) + (() if last else (xs[t + 1],)),
            [((ROWS, 3 * T), BF), (big, F32)]
            + ([] if last else [(big, F32)] + [((2, T, 2 * T), BF)] * 2),
            [(slim, BF)] * 2,
        )
        saved.append((st, r, u, c, feats, fq))
        if not last:
            st, *pay = rest
            beside = ()
    ops = (vbg, vbd, tin, tout, et_in, et_out, tfar)
    gxs = [None] * steps
    carry, cu_sum, r_sum = (), (), ()
    for t in reversed(range(steps)):
        st, r, u, c, feats, fq = saved[t]
        first = t == steps - 1
        gp, ec, eu, gq, sums, *rest = run(
            functools.partial(cand_back_kernel, first=first),
            "cand_back",
            (0,),
            (meta, cots[t], u, c, st, cand_w) + ops + carry,
            [(big, F32), (big, BF), (big, BF), (big, F32), ((8, 2 * T), F32)]
            + [((2, T, T), BF)] * 2
            + ([] if first else [(big, BF)]),
            [((ROWS, 2 * T), F32), ((ROWS, 3 * T), F32), (big, BF), (slim, BF), (slim, F32)],
        )
        if not first:
            gxs[t + 1] = rest[2]
        last = t == 0
        rows, columns = 2 * T + 32, 6 * T
        args = (meta, ec, eu, sums, feats, fq, *cu_sum)
        if not last:
            cu_sum = run(
                weight_cu_kernel, "weight_cu", (0,), args, [((rows, columns), F32)],
                flops=4 * 10**8,
            )
        else:
            kept, sent = run(
                weight_cu_last_kernel, "weight_cu", (0,), args,
                [((rows, columns // 2), F32), ((rows, columns // 2), BF)],
                [((rows, columns), F32)], flops=4 * 10**8,
            )
            cu_sum = run(
                add_split_kernel, "add_split", (0,), (meta, kept, swap_in(sent)),
                [((rows // 2, columns // 2), BF)] * 2,
            )
        got, cu_sum = exchange(*rest[:2], ft_in, middle_back, cu_sum)
        gs_part, gx_part, er, sums, *rest = run(
            gate_back_kernel,
            "gate_back",
            (0,),
            (meta, gq, *got, gp, r, st, ec, eu, gate_w, cand_w) + ops,
            [(big, F32), (big, F32), (big, BF), ((8, T), F32)] + [((2, T, 2 * T), BF)] * 2,
            [
                (big, F32), ((ROWS, 2 * T), BF), (big, F32), ((ROWS, 6 * T), F32),
                ((ROWS, 2 * T), BF), (wide, BF), (wide, F32),
            ],
        )
        args = (meta, er, sums, feats, *r_sum)
        rows = T + 16
        if not last:
            r_sum = run(
                weight_r_kernel, "weight_r", (0,), args, [((rows, columns), F32)],
                flops=2 * 10**8,
            )
            got, r_sum = exchange(*rest, ft_in, middle_back, r_sum)
        else:
            kept, sent = run(
                weight_r_last_kernel, "weight_r", (0,), args,
                [((rows, columns // 2), F32), ((rows, columns // 2), BF)],
                [((rows, columns), F32)], flops=2 * 10**8,
            )
            r_part = sum_of(kept, swap_in(sent))
            got, _ = exchange(*rest, ft_in, middle_back)
        carry = (gs_part, gx_part, *got)
    cu = reduce_rows(*cu_sum)
    rr = reduce_rest(r_part, 2)
    gi, gs = run(
        finish_kernel,
        "finish",
        (0,),
        (meta, order, *carry, et_in, et_out, tfar, gxs[1], gxs[2]),
        [((steps,) + big, BF), (big, F32)],
        [((ROWS, 2 * T), F32), ((ROWS, 6 * T), BF)],
    )
    gi, gs, cu = lax.optimization_barrier((gi, gs, cu))
    cu = (*cu, *[swap_in(x) for x in cu])
    scale = 1.0 / math.sqrt(ROWS * lax.axis_size("wide") * steps)
    gw, gb, cw, cb = run(
        functools.partial(weights_kernel, scale=scale),
        "weights",
        (0,),
        (meta, *cu, *rr),
        [((6 * T, 2 * T), F32), ((1, 2 * T), F32), ((6 * T, T), F32), ((1, T), F32)],
    )
    return gi, gs, gw, gb.reshape(-1), cw, cb.reshape(-1)


def solution(mesh):
    return jax.shard_map(
        per_device,
        mesh=mesh,
        in_specs=(
            P(None, ("parts", "wide"), None),
            P(("parts", "wide"), None),
            P(None, ("parts", "wide"), None),
            P(),
            P(),
            P(),
            P(),
            P(("parts", "wide"), None, None, None),
            P(("parts", "wide"), None),
            P(("parts", "wide")),
            P(("parts", "wide")),
        ),
        out_specs=(
            P(None, ("parts", "wide"), None),
            P(("parts", "wide"), None),
            P("parts", None),
            P("parts"),
            P("parts", None),
            P("parts"),
        ),
        check_vma=False,
    )
```

```python
import functools
import math

import jax
import jax.numpy as jnp
from jax import lax
from jax.experimental import pallas as pl
from jax.experimental.pallas import tpu as pltpu
from jax.sharding import PartitionSpec as P

BF = jnp.bfloat16
F32 = jnp.float32
T = 128
NT = 8
ROWS = NT * T
COUNTS = 34
VMEM_LIMIT = 14 * 1024 * 1024


def swap(block, start):
    count = lax.axis_size("wide")
    return lax.ppermute(
        block, "wide", [p for i in range(start, count - 1, 2) for p in ((i, i + 1), (i + 1, i))]
    )


def swap_in(block):
    return swap(block, 0)


def swap_out(block):
    return swap(block, 1)


def exchange(pay_in, pay_out, far, middle, beside=()):
    got_in = swap_in(pay_in)
    (ready,) = run(middle, "middle", (), (pay_out, got_in, far), [(pay_out.shape, BF)])
    got_out = swap_out(ready)
    got_out, beside = lax.optimization_barrier((got_out, tuple(beside)))
    return (got_in, got_out, swap_in(got_out)), beside


def dot(a, b):
    return jnp.dot(a, b, preferred_element_type=F32)


def dot_nt(a, b):
    return lax.dot_general(a, b, (((1,), (1,)), ((), ())), preferred_element_type=F32)


def dot_tn(a, b):
    return lax.dot_general(a, b, (((0,), (0,)), ((), ())), preferred_element_type=F32)


def tile(ref, i):
    start = i * T if isinstance(i, int) else pl.multiple_of(i * T, T)
    return ref.at[pl.ds(start, T)]


class Place:
    def __init__(self, meta):
        self.idx = lambda r, s: meta[4 * r + s]
        core = meta[32]
        self.core = core
        self.e_in = 7 - 7 * core
        self.n_in = 6 - 5 * core
        self.e_out = 7 * core
        self.n_out = 1 + 5 * core
        self.pos_in = 9 - 9 * core
        self.pos_out = 9 * core
        self.col_in = jnp.where(core == 0, meta[4 * 7 + 3], meta[3])
        self.col_out = jnp.where(core == 0, meta[3], meta[4 * 7 + 3])
        self.t_in = jnp.clip(self.col_in - 1, 0, NT - 1)
        self.t_out = jnp.clip(self.col_out - 1, 0, NT - 1)


def copies(sems, *pairs):
    started = [pltpu.make_async_copy(a, b, sems.at[k]) for k, (a, b) in enumerate(pairs)]
    for copy in started:
        copy.start()

    def wait():
        for copy in started:
            copy.wait()

    return wait


def start_kernel(
    device, cols_hbm, counts_hbm, vals_hbm, order_hbm, inputs_hbm, state_hbm,
    meta, e_in, e_out, et_in, et_out, f_out, ft_in, x0, st, pay_in, pay_out,
    cols, counts, first, last, order, given, state, pick, parts, sems,
):
    small = copies(sems.at[pl.ds(0, 2)], (cols_hbm, cols), (counts_hbm, counts))
    wait_order = copies(sems.at[pl.ds(2, 1)], (order_hbm, order))
    wait_rows = copies(
        sems.at[pl.ds(3, 2)], (inputs_hbm.at[0], given), (state_hbm, state)
    )
    wait_vals = copies(
        sems.at[pl.ds(5, 2)], (vals_hbm.at[0], first), (vals_hbm.at[NT - 1], last)
    )
    wait_order()
    pick_rows(order, pick)
    small()
    for r in range(NT):
        for k in range(4):
            meta[4 * r + k] = cols[k, r] - (device[0] * NT - 1)
        meta[COUNTS + r] = counts[r]
    meta[32] = lax.rem(device[0], 2)
    meta[33] = lax.rem(lax.div(device[0], 2), 2)
    place = Place(meta)
    wait_rows()
    split_f32(state[...], parts, 0)
    parts[:, 3 * T :] = given[...]
    for h in range(4):
        rows = slice(h * 256, (h + 1) * 256)
        got = dot(pick[rows], parts[...])
        st[rows] = got[:, :T] + got[:, T : 2 * T] + got[:, 2 * T : 3 * T]
        x0[rows] = got[:, 3 * T :].astype(BF)
    wait_vals()
    edge_tiles(place, meta, first, last, e_in, e_out, et_in, et_out, f_out, ft_in, pay_in, pay_out)
    write_payload(place, st, e_in, e_out, pay_in, pay_out, S_LANES)
    write_payload(place, x0, e_in, e_out, pay_in, pay_out, X_LANES)


def edge_tiles(place, meta, first, last, e_in, e_out, et_in, et_out, f_out, ft_in, pay_in, pay_out):
    zero = place.core == 0
    for low, side_row, row_far, them, far in (
        (False, place.e_in, place.col_in, place.pos_in, place.pos_out),
        (True, place.e_out, place.col_out, place.pos_out, place.pos_in),
    ):
        top = zero if low else jnp.logical_not(zero)
        vals = [jnp.where(top, first[k].astype(F32), last[k].astype(F32)) for k in range(4)]
        inside = jnp.where(top, vals[2], vals[1])
        ahead = jnp.where(top, vals[1], vals[2])
        live = meta[COUNTS + side_row] > 3

        def third(flag):
            return vals[3] * jnp.where(jnp.logical_and(live, flag), 1.0, 0.0)

        is_them, is_far = row_far == them, row_far == far
        own = third(jnp.logical_not(jnp.logical_or(is_them, is_far)))
        e_ref, et_ref = (e_out, et_out) if low else (e_in, et_in)
        for k, v in enumerate((vals[0], inside, own)):
            e_ref[:, k * T : (k + 1) * T] = v.astype(BF)
            et_ref[k * T : (k + 1) * T] = v.T.astype(BF)
        pay = pay_out if low else pay_in
        pay[2, :, :T] = ahead.astype(BF)
        pay[2, :, T:] = third(is_them).astype(BF)
        if low:
            f_out[...] = third(is_far).astype(BF)
            pay_in[3, :, T:] = third(is_far).astype(BF)
        else:
            pay_in[3, :, :T] = third(is_far).astype(BF)
            ft_in[...] = third(is_far).T.astype(BF)


def pick_rows(order, pick):
    lane = lax.broadcasted_iota(jnp.int32, (T, T), 1).astype(F32)
    for j in range(NT):
        wanted = jnp.broadcast_to(order[j : j + 1, :].astype(F32), (T, T)).T
        for k in range(NT):
            pick[j * T : (j + 1) * T, k * T : (k + 1) * T] = (
                (wanted == lane + float(k * T)).astype(F32).astype(BF)
            )


def split_f32(value, ref, start):
    for k in range(3):
        part = value.astype(BF)
        ref[:, start + k * T : start + (k + 1) * T] = part
        value = value - part.astype(F32)


def write_payload(place, own, e_in, e_out, pay_in, pay_out, lanes):
    for e_ref, pay, tiles in (
        (e_in, pay_in, (place.e_in, place.n_in, place.t_in)),
        (e_out, pay_out, (place.e_out, place.n_out, place.t_out)),
    ):
        picked = [tile(own, i)[...].astype(BF) for i in tiles]
        pay[0, :, lanes] = picked[0]
        pay[1, :, lanes] = dot(e_ref[...], jnp.concatenate(picked, axis=0)).astype(BF)


S_LANES, X_LANES = slice(0, T), slice(T, 2 * T)


def rest_kernel(order, in1, in2, cot, x1, x2, c0, c1, c2, pick, parts):
    pick_rows(order, pick)
    for k, src in enumerate((in1[0], in2[0], cot[0], cot[1], cot[2])):
        parts[:, k * T : (k + 1) * T] = src
    for h in range(4):
        rows = slice(h * 256, (h + 1) * 256)
        got = dot(pick[rows], parts[...]).astype(BF)
        for k, out in enumerate((x1, x2, c0, c1, c2)):
            out[rows] = got[:, k * T : (k + 1) * T]


def operator_kernel(meta, vals, vfg, vbg, vbd):
    for r in range(NT):
        live = jnp.where(meta[COUNTS + r] > 3, 1.0, 0.0)
        last = (vals[r, 3].astype(F32) * live).astype(BF)
        vfg[r, :, 0:T] = vals[r, 1]
        vfg[r, :, T : 2 * T] = vals[r, 0]
        vfg[r, :, 2 * T : 3 * T] = vals[r, 2]
        vfg[r, :, 3 * T :] = last
        vbg[r, :, T : 2 * T] = vals[r, 0].T
        if r > 0:
            vbg[r - 1, :, 2 * T :] = vals[r, 1].T
        else:
            vbd[8] = vals[r, 1].T
        if r < NT - 1:
            vbg[r + 1, :, 0:T] = vals[r, 2].T
        else:
            vbd[9] = vals[r, 2].T
        vbd[r] = last.T
    vbg[0, :, 0:T] = jnp.zeros((T, T), BF)
    vbg[NT - 1, :, 2 * T :] = jnp.zeros((T, T), BF)


def turn_kernel(rin, rout, vin, vout, tin, tout, tfar):
    vin[...] = rin[2:]
    vout[...] = rout[2:]
    for k in range(2):
        lanes = slice(k * T, (k + 1) * T)
        tin[:, lanes] = rin[2, :, lanes].astype(F32).T.astype(BF)
        tout[:, lanes] = rout[2, :, lanes].astype(F32).T.astype(BF)
    tfar[...] = rin[3, :, T:].astype(F32).T.astype(BF)


def middle_forward(pay, got, far, out):
    out[0] = pay[0]
    out[1] = (pay[1].astype(F32) + dot(far[...], got[0])).astype(BF)
    if pay.shape[0] > 2:
        out[2] = pay[2]


def middle_back(pay, got, far, out):
    out[0] = (pay[0].astype(F32) + dot(far[...], got[1])).astype(BF)
    out[1] = pay[1]


def forward_row(place, vfg, src, r):
    low = tile(src, place.idx(0, 1))[...] if r == 0 else tile(src, r)[...]
    high = tile(src, place.idx(7, 2))[...] if r == 7 else tile(src, r + 2)[...]
    picked = jnp.concatenate(
        [low, tile(src, r + 1)[...], high, tile(src, place.idx(r, 3))[...]], axis=0
    )
    return dot(vfg[r], picked)


def first_order(place, vfg, vin, vout, zext, d1, rin, rout, rfwd):
    tile(zext, place.pos_in)[...] = rin[0]
    tile(zext, place.pos_out)[...] = rout[0]
    for r in range(NT):
        tile(d1, r + 1)[...] = forward_row(place, vfg, zext, r).astype(BF)
    edge = tile(zext, place.e_in + 1)[...]
    lhs = jnp.concatenate([vin[0], vin[1, :, :T]], axis=1)
    total = rin[1].astype(F32) + dot(lhs, jnp.concatenate([edge, edge, rfwd[0]], axis=0))
    tile(d1, place.pos_in)[...] = total.astype(BF)
    edge = tile(zext, place.e_out + 1)[...]
    total = rout[1].astype(F32) + dot(vout[0], jnp.concatenate([edge, edge], axis=0))
    tile(d1, place.pos_out)[...] = total.astype(BF)


def second_order(place, vfg, zext, d1, r):
    z = tile(zext, r + 1)[...].astype(F32)
    return (2.0 * forward_row(place, vfg, d1, r) - z).astype(BF)


def gate_kernel(
    meta, st, x, rin, rout, rfwd, vfg, *rest, first
):
    if first:
        vin, vout = rin.at[pl.ds(2, 2)], rout.at[pl.ds(2, 1)]
    else:
        vin, vout, *rest = rest
    e_in, e_out, gw, gb, feats, r_out, q_out, pay_in, pay_out, zext, d1 = rest
    place = Place(meta)
    zext[T : T + ROWS, :T] = st[...].astype(BF)
    zext[T : T + ROWS, T:] = x[...]
    first_order(place, vfg, vin, vout, zext, d1, rin, rout, rfwd)
    for r in range(NT):
        d2 = second_order(place, vfg, zext, d1, r)
        z = tile(zext, r + 1)[...]
        one = tile(d1, r + 1)[...]
        row = jnp.concatenate(
            [z[:, T:], one[:, T:], d2[:, T:], z[:, :T], one[:, :T], d2[:, :T]], axis=1
        )
        tile(feats, r)[...] = row
    for h in range(4):
        rows = slice(h * 256, (h + 1) * 256)
        reset = jax.nn.sigmoid(dot(feats[rows], gw[:, :T]) + gb[:, :T])
        r_out[rows] = reset
        q_out[rows] = (reset * st[rows]).astype(BF)
    write_payload(place, q_out, e_in, e_out, pay_in, pay_out, S_LANES)


def update_kernel(feats, gw, gb, cw, cb, u_out, xc_out):
    for h in range(4):
        rows = slice(h * 256, (h + 1) * 256)
        f = feats[rows]
        u_out[rows] = jax.nn.sigmoid(dot(f, gw[:, T:]) + gb[:, T:])
        xc_out[rows] = dot(f[:, : 3 * T], cw[: 3 * T]) + cb[...]


def cand_kernel(meta, q, rin, rout, rfwd, vfg, vin, vout, e_in, e_out, cw, xc, u, st, *rest, last):
    if last:
        fq, c_out, zext, d1 = rest
    else:
        x_next, fq, c_out, st_out, pay_in, pay_out, zext, d1 = rest
    place = Place(meta)
    zext[T : T + ROWS] = q[...]
    first_order(place, vfg, vin, vout, zext, d1, rin, rout, rfwd)
    for r in range(NT):
        d2 = second_order(place, vfg, zext, d1, r)
        tile(fq, r)[...] = jnp.concatenate(
            [tile(zext, r + 1)[...], tile(d1, r + 1)[...], d2], axis=1
        )
    for h in range(4):
        rows = slice(h * 256, (h + 1) * 256)
        cand = jnp.tanh(dot(fq[rows], cw[3 * T :]) + xc[rows])
        c_out[rows] = cand
        if not last:
            st_out[rows] = u[rows] * st[rows] + (1.0 - u[rows]) * cand
    if not last:
        write_payload(place, st_out, e_in, e_out, pay_in, pay_out, S_LANES)
        write_payload(place, x_next, e_in, e_out, pay_in, pay_out, X_LANES)


def add_received(place, acc, rin, rout, rfwd, et_in, et_out, tfar):
    got_in = dot(et_in[...], rin[1])
    got_out = dot(et_out[...], rout[1])
    for i, block in (
        (place.e_in, got_in[:T] + rin[0].astype(F32) + dot(tfar[...], rfwd[1])),
        (place.n_in, got_in[T : 2 * T]),
        (place.t_in, got_in[2 * T :]),
        (place.e_out, got_out[:T] + rout[0].astype(F32)),
        (place.n_out, got_out[T : 2 * T]),
        (place.t_out, got_out[2 * T :]),
    ):
        tile(acc, i)[...] += block


def back_rows(place, vbg, vbd, y, acc, base):
    zero = jnp.zeros((T, acc.shape[1]), F32)
    tile(acc, 0)[...] = zero
    tile(acc, 9)[...] = zero
    for r in range(NT):
        lo, hi = max(r - 1, 0), min(r + 2, NT)
        lhs = vbg[r, :, (lo - r + 1) * T : (hi - r + 1) * T]
        tile(acc, r + 1)[...] = base(r, dot(lhs, y[lo * T : hi * T]))
    parts = [(place.idx(0, 1), 8, 0), (place.idx(7, 2), 9, 7)]
    parts += [(place.idx(r, 3), r, r) for r in range(NT)]
    for i, k, r in parts:
        tile(acc, i)[...] += dot(vbd[k], y[r * T : (r + 1) * T])


def diffuse_back(place, vbg, vbd, tin, tout, a, y, w, acc, pay_in, pay_out):
    for r in range(NT):
        rows = slice(r * T, (r + 1) * T)
        y[rows] = a(2, rows).astype(BF)
    back_rows(
        place, vbg, vbd, y, acc, lambda r, v: a(1, slice(r * T, (r + 1) * T)) * 0.5 + v
    )
    for e in range(NT + 2):
        tile(w, e)[...] = (2.0 * tile(acc, e)[...]).astype(BF)
    own = w.at[pl.ds(T, ROWS)]

    def second(r, v):
        rows = slice(r * T, (r + 1) * T)
        return a(0, rows) - a(2, rows) + v

    back_rows(place, vbg, vbd, own, acc, second)
    for pos, edge, vals, pay in (
        (place.pos_in, place.e_in, tin, pay_in),
        (place.pos_out, place.e_out, tout, pay_out),
    ):
        part = tile(w, pos)[...]
        tile(acc, edge + 1)[...] += dot(vals[...], jnp.concatenate([part, part], axis=0))
        pay[0] = tile(acc, pos)[...].astype(BF)
        pay[1] = part


def cand_back_kernel(*refs, first):
    refs = list(refs)
    take = lambda n: [refs.pop(0) for _ in range(n)]
    meta, cot, u, c, st, cw, vbg, vbd, tin, tout, et_in, et_out, tfar = take(13)
    if not first:
        gs_part, gx_part, rin, rout, rfwd = take(5)
    gp_out, ec_out, eu_out, gq_out, sums, pay_in, pay_out = take(7)
    if not first:
        (gx_out,) = take(1)
    gs, g, y, w, acc = take(5)
    place = Place(meta)
    if not first:
        gs[:, :T] = gs_part[...]
        gs[:, T:] = gx_part[...]
        add_received(place, gs, rin, rout, rfwd, et_in, et_out, tfar)
        gx_out[...] = gs[:, T:].astype(BF)
    sum_c = jnp.zeros((1, T), F32)
    sum_u = jnp.zeros((1, T), F32)
    for h in range(NT):
        rows = slice(h * T, (h + 1) * T)
        grad = cot[rows].astype(F32)
        if not first:
            grad = grad + gs[rows, :T]
        upd, cand = u[rows], c[rows]
        pre = grad * (1.0 - upd) * (1.0 - cand * cand)
        gate = grad * (st[rows] - cand) * upd * (1.0 - upd)
        gp_out[rows] = grad * upd
        ec_out[rows] = pre.astype(BF)
        eu_out[rows] = gate.astype(BF)
        sum_c = sum_c + jnp.sum(pre, axis=0, keepdims=True)
        sum_u = sum_u + jnp.sum(gate, axis=0, keepdims=True)
    sums[...] = jnp.broadcast_to(jnp.concatenate([sum_c, sum_u], axis=1), (8, 2 * T))
    g[...] = dot_nt(ec_out[...], cw[3 * T :])
    diffuse_back(
        place, vbg, vbd, tin, tout,
        lambda k, rows: g[rows, k * T : (k + 1) * T],
        y, w, acc, pay_in, pay_out,
    )
    gq_out[...] = acc[T : T + ROWS]


def gate_back_kernel(
    meta, gq_part, rin, rout, rfwd, gp, r_ref, st, ec, eu, gw, cw,
    vbg, vbd, tin, tout, et_in, et_out, tfar,
    gs_out, gx_out, er_out, sums, pay_in, pay_out, gq, eg, gps, g, y, w, acc,
):
    place = Place(meta)
    gq[...] = gq_part[...]
    add_received(place, gq, rin, rout, rfwd, et_in, et_out, tfar)
    sum_r = jnp.zeros((1, T), F32)
    for h in range(NT):
        rows = slice(h * T, (h + 1) * T)
        grad, reset = gq[rows], r_ref[rows]
        gps[rows] = gp[rows] + grad * reset
        pre = grad * st[rows] * reset * (1.0 - reset)
        eg[rows, :T] = pre.astype(BF)
        sum_r = sum_r + jnp.sum(pre, axis=0, keepdims=True)
    eg[:, T:] = eu[...]
    er_out[...] = eg[:, :T]
    sums[...] = jnp.broadcast_to(sum_r, (8, T))
    e = eg[...]
    for k in range(3):
        cols = slice(2 * k * T, (2 * k + 1) * T)
        g[:, cols] = dot_nt(e, gw[(3 + k) * T : (4 + k) * T])
        cols = slice((2 * k + 1) * T, (2 * k + 2) * T)
        g[:, cols] = dot_nt(e, gw[k * T : (k + 1) * T]) + dot_nt(
            ec[...], cw[k * T : (k + 1) * T]
        )
    diffuse_back(
        place, vbg, vbd, tin, tout,
        lambda k, rows: g[rows, 2 * k * T : 2 * (k + 1) * T],
        y, w, acc, pay_in, pay_out,
    )
    gs_out[...] = acc[T : T + ROWS, :T] + gps[...]
    gx_out[...] = acc[T : T + ROWS, T:]


def add_rows(out, value, rest, rows):
    out[rows] = value + rest[0][rows] if rest else value


def split_columns(meta, total, kept, sent):
    half = total.shape[1] // 2
    mine = meta[32] == 0
    low, high = total[:, :half], total[:, half:]
    kept[...] = jnp.where(mine, low, high)
    sent[...] = jnp.where(mine, high, low).astype(BF)


def weight_cu_kernel(meta, ec, eu, sums, feats, fq, *rest):
    *rest, out = rest
    x = feats[:, : 3 * T]
    both = jnp.concatenate([dot_tn(ec[...], x), dot_tn(ec[...], fq[...])], axis=1)
    add_rows(out, both, rest, slice(0, T))
    add_rows(out, dot_tn(eu[...], feats[...]), rest, slice(T, 2 * T))
    row = jnp.concatenate([sums[...], jnp.zeros((8, 4 * T), F32)], axis=1)
    add_rows(out, jnp.concatenate([row] * 4, axis=0), rest, slice(2 * T, 2 * T + 32))


def weight_cu_last_kernel(meta, ec, eu, sums, feats, fq, before, kept, sent, out):
    weight_cu_kernel(meta, ec, eu, sums, feats, fq, before, out)
    split_columns(meta, out, kept, sent)


def weight_r_kernel(meta, er, sums, feats, *rest):
    *rest, out = rest
    add_rows(out, dot_tn(er[...], feats[...]), rest, slice(0, T))
    row = jnp.concatenate([sums[...], jnp.zeros((8, 5 * T), F32)], axis=1)
    add_rows(out, jnp.concatenate([row, row], axis=0), rest, slice(T, T + 16))


def weight_r_last_kernel(meta, er, sums, feats, before, kept, sent, out):
    weight_r_kernel(meta, er, sums, feats, before, out)
    split_columns(meta, out, kept, sent)


def add_kernel(a, b, out):
    out[...] = (a[...].astype(F32) + b[...].astype(F32)).astype(BF)


def add_split_kernel(meta, a, b, kept, sent):
    total = (a[...].astype(F32) + b[...].astype(F32)).astype(BF)
    half = total.shape[0] // 2
    upper = meta[33] == 1
    top, bottom = total[:half].astype(F32), total[half:].astype(F32)
    kept[...] = jnp.where(upper, bottom, top).astype(BF)
    sent[...] = jnp.where(upper, top, bottom).astype(BF)


def sum_of(a, b):
    return run(add_kernel, "add", (), (a, b), [(a.shape, BF)])[0]


def reduce_step(part, step):
    count = lax.axis_size("wide")
    other = lax.ppermute(part, "wide", [(i, i ^ step) for i in range(count)])
    return sum_of(part, other)


def reduce_rows(kept, sent):
    count = lax.axis_size("wide")
    route = [(i, i ^ 2) for i in range(count)]
    part = sum_of(kept, lax.ppermute(sent, "wide", route))
    step = 4
    while step < count:
        part = reduce_step(part, step)
        step *= 2
    return part, lax.ppermute(part, "wide", route)


def reduce_rest(part, step):
    while step < lax.axis_size("wide"):
        part = reduce_step(part, step)
        step *= 2
    return part, swap_in(part)


def weights_kernel(
    meta, cu_a, cu_b, cu_a_other, cu_b_other, r_own, r_other, gw, gb, cw, cb, *, scale
):
    mine = meta[32] == 0
    upper = meta[33] == 1

    def pick(own, other, side):
        a, b = own[...].astype(F32), other[...].astype(F32)
        return jnp.where(mine, a, b) if side == 0 else jnp.where(mine, b, a)

    def rows_of(a, b):
        low, high = jnp.where(upper, b, a), jnp.where(upper, a, b)
        return jnp.concatenate([low, high], axis=0)

    for side in range(2):
        cu = rows_of(pick(cu_a, cu_a_other, side), pick(cu_b, cu_b_other, side)) * scale
        r = pick(r_own, r_other, side) * scale
        for k in range(3):
            cols = slice(k * T, (k + 1) * T)
            rows = slice((3 * side + k) * T, (3 * side + k + 1) * T)
            cw[rows] = cu[:T, cols].T
            gw[rows, T:] = cu[T : 2 * T, cols].T
            gw[rows, :T] = r[:T, cols].T
        if side == 0:
            cb[...] = cu[2 * T : 2 * T + 1, :T]
            gb[:, T:] = cu[2 * T : 2 * T + 1, T : 2 * T]
            gb[:, :T] = r[T : T + 1, :T]


def finish_kernel(
    meta, order, gs_part, gx_part, rin, rout, rfwd, et_in, et_out, tfar, gx1, gx2,
    gi_out, gs_out, gs, parts,
):
    place = Place(meta)
    gs[:, :T] = gs_part[...]
    gs[:, T:] = gx_part[...]
    add_received(place, gs, rin, rout, rfwd, et_in, et_out, tfar)
    split_f32(gs[:, :T], parts, 0)
    parts[:, 3 * T : 4 * T] = gs[:, T:].astype(BF)
    parts[:, 4 * T : 5 * T] = gx1[...]
    parts[:, 5 * T :] = gx2[...]
    row = lax.broadcasted_iota(jnp.int32, (T, T), 0)
    for k in range(NT):
        put = jnp.concatenate(
            [
                (jnp.broadcast_to(order[j : j + 1, :], (T, T)) == row + k * T)
                .astype(F32)
                .astype(BF)
                for j in range(NT)
            ],
            axis=1,
        )
        rows = slice(k * T, (k + 1) * T)
        got = dot(put, parts[...])
        gs_out[rows] = got[:, :T] + got[:, T : 2 * T] + got[:, 2 * T : 3 * T]
        for t in range(3):
            gi_out[t, rows] = got[:, (3 + t) * T : (4 + t) * T].astype(BF)


SMEM = pl.BlockSpec(memory_space=pltpu.SMEM)
VMEM = pl.BlockSpec(memory_space=pltpu.VMEM)


HBM = pl.BlockSpec(memory_space=pltpu.HBM)


def run(
    kernel, name, smem, args, outs, scratch=(), specs=None, flops=10**8,
    hbm=(), smem_outs=(), sems=0,
):
    grid = (1,) if specs else ()
    specs = specs or [
        SMEM if i in smem else HBM if i in hbm else VMEM for i in range(len(args))
    ]
    out_shape = [jax.ShapeDtypeStruct(s, d) for s, d in outs]
    args = [
        pltpu.with_memory_space_constraint(x, pltpu.HBM) if i in hbm else x
        for i, x in enumerate(args)
    ]
    moved = sum(math.prod(x.shape) * x.dtype.itemsize for x in (*args, *out_shape))
    return pl.pallas_call(
        kernel,
        name=name,
        grid=grid,
        in_specs=specs,
        out_specs=[SMEM if i in smem_outs else VMEM for i in range(len(outs))],
        out_shape=out_shape,
        scratch_shapes=[pltpu.VMEM(*s) if isinstance(s, tuple) else s for s in scratch]
        + ([pltpu.SemaphoreType.DMA((sems,))] if sems else []),
        cost_estimate=pl.CostEstimate(flops=flops, bytes_accessed=moved, transcendentals=0),
        compiler_params=pltpu.CompilerParams(vmem_limit_bytes=VMEM_LIMIT),
    )(*args)


def leading(block, at):
    zeros = (0,) * (len(block) - 1)
    return pl.BlockSpec(block, lambda i: (at,) + zeros, memory_space=pltpu.VMEM)


def per_device(
    inputs, state_init, cotangent, gate_w, gate_b, cand_w, cand_b,
    tile_vals, tile_cols, tile_counts, sector_order,
):
    order = sector_order.reshape(NT, T)
    gb = gate_b.reshape(1, -1)
    cb = cand_b.reshape(1, -1)
    big = (ROWS, T)
    square = (T, T)
    flat, tall = ((T, 3 * T), BF), ((3 * T, T), BF)
    x_block = (1, ROWS, T)
    device = lax.axis_index("wide").astype(jnp.int32).reshape(1)
    meta, e_in, e_out, et_in, et_out, f_out, ft_in, x0, st, *pay = run(
        start_kernel, "start", (0,),
        (device, tile_cols.T, tile_counts, tile_vals, order, inputs, state_init),
        [((COUNTS + NT,), jnp.int32), flat, flat, tall, tall, (square, BF), (square, BF)]
        + [(big, BF), (big, F32), ((4, T, 2 * T), BF), ((3, T, 2 * T), BF)],
        [
            pltpu.SMEM((4, NT), jnp.int32), pltpu.SMEM((NT,), jnp.int32),
            ((4, T, T), BF), ((4, T, T), BF), ((NT, T), jnp.int32), (big, BF), (big, F32),
            ((ROWS, ROWS), BF), ((ROWS, 4 * T), BF),
        ],
        hbm=(1, 2, 3, 4, 5, 6), sems=7, smem_outs=(0,), flops=10**9,
    )
    vfg, vbg, vbd = run(
        operator_kernel, "operator", (0,), (meta, tile_vals),
        [((NT, T, 4 * T), BF), ((NT, T, 3 * T), BF), ((NT + 2, T, T), BF)],
    )
    x1, x2, *cots = run(
        rest_kernel, "rest", (), (order, inputs, inputs, cotangent), [(big, BF)] * 5,
        [((ROWS, ROWS), BF), ((ROWS, 5 * T), BF)],
        specs=[VMEM, leading(x_block, 1), leading(x_block, 2), VMEM],
        flops=10**9,
    )
    saved = []
    steps = inputs.shape[0]
    wide = ((NT + 2) * T, 2 * T)
    slim = ((NT + 2) * T, T)
    beside = (vfg, vbg, vbd)
    for t in range(steps):
        last = t == steps - 1
        got, beside = exchange(*pay, f_out, middle_forward, beside)
        if t == 0:
            vfg, vbg, vbd = beside
            turned = run(
                turn_kernel, "turn", (), got[:2],
                [((2, T, 2 * T), BF), ((1, T, 2 * T), BF)] + [((T, 2 * T), BF)] * 2
                + [(square, BF)],
            )
            xs, ops = (x0,), (vfg, e_in, e_out)
        feats, r, q, *pay = run(
            functools.partial(gate_kernel, first=t == 0),
            "gate",
            (0,),
            (meta, st, xs[t], *got, *ops, gate_w, gb),
            [((ROWS, 6 * T), BF), (big, F32), (big, BF)] + [((2, T, T), BF)] * 2,
            [(wide, BF)] * 2,
        )
        beside = tuple(run(
            update_kernel,
            "update",
            (),
            (feats, gate_w, gb, cand_w, cb),
            [(big, F32)] * 2,
            flops=5 * 10**8,
        ))
        if t == 0:
            beside += (x1, x2, *cots, *turned)
        got, (u, xc, *beside) = exchange(*pay, f_out, middle_forward, beside)
        if t == 0:
            xs += tuple(beside[:2])
            cots = beside[2:5]
            vin, vout, tin, tout, tfar = beside[5:]
            ops = (vfg, vin, vout, e_in, e_out)
        fq, c, *rest = run(
            functools.partial(cand_kernel, last=last),
            "cand",
            (0,),
            (meta, q, *got, *ops, cand_w, xc, u, st) + (() if last else (xs[t + 1],)),
            [((ROWS, 3 * T), BF), (big, F32)]
            + ([] if last else [(big, F32)] + [((2, T, 2 * T), BF)] * 2),
            [(slim, BF)] * 2,
        )
        saved.append((st, r, u, c, feats, fq))
        if not last:
            st, *pay = rest
            beside = ()
    ops = (vbg, vbd, tin, tout, et_in, et_out, tfar)
    gxs = [None] * steps
    carry, cu_sum, r_sum = (), (), ()
    for t in reversed(range(steps)):
        st, r, u, c, feats, fq = saved[t]
        first = t == steps - 1
        gp, ec, eu, gq, sums, *rest = run(
            functools.partial(cand_back_kernel, first=first),
            "cand_back",
            (0,),
            (meta, cots[t], u, c, st, cand_w) + ops + carry,
            [(big, F32), (big, BF), (big, BF), (big, F32), ((8, 2 * T), F32)]
            + [((2, T, T), BF)] * 2
            + ([] if first else [(big, BF)]),
            [((ROWS, 2 * T), F32), ((ROWS, 3 * T), F32), (big, BF), (slim, BF), (slim, F32)],
        )
        if not first:
            gxs[t + 1] = rest[2]
        last = t == 0
        rows, columns = 2 * T + 32, 6 * T
        args = (meta, ec, eu, sums, feats, fq, *cu_sum)
        if not last:
            cu_sum = run(
                weight_cu_kernel, "weight_cu", (0,), args, [((rows, columns), F32)],
                flops=4 * 10**8,
            )
        else:
            kept, sent = run(
                weight_cu_last_kernel, "weight_cu", (0,), args,
                [((rows, columns // 2), F32), ((rows, columns // 2), BF)],
                [((rows, columns), F32)], flops=4 * 10**8,
            )
            cu_sum = run(
                add_split_kernel, "add_split", (0,), (meta, kept, swap_in(sent)),
                [((rows // 2, columns // 2), BF)] * 2,
            )
        got, cu_sum = exchange(*rest[:2], ft_in, middle_back, cu_sum)
        gs_part, gx_part, er, sums, *rest = run(
            gate_back_kernel,
            "gate_back",
            (0,),
            (meta, gq, *got, gp, r, st, ec, eu, gate_w, cand_w) + ops,
            [(big, F32), (big, F32), (big, BF), ((8, T), F32)] + [((2, T, 2 * T), BF)] * 2,
            [
                (big, F32), ((ROWS, 2 * T), BF), (big, F32), ((ROWS, 6 * T), F32),
                ((ROWS, 2 * T), BF), (wide, BF), (wide, F32),
            ],
        )
        args = (meta, er, sums, feats, *r_sum)
        rows = T + 16
        if not last:
            r_sum = run(
                weight_r_kernel, "weight_r", (0,), args, [((rows, columns), F32)],
                flops=2 * 10**8,
            )
            got, r_sum = exchange(*rest, ft_in, middle_back, r_sum)
        else:
            kept, sent = run(
                weight_r_last_kernel, "weight_r", (0,), args,
                [((rows, columns // 2), F32), ((rows, columns // 2), BF)],
                [((rows, columns), F32)], flops=2 * 10**8,
            )
            r_part = sum_of(kept, swap_in(sent))
            got, _ = exchange(*rest, ft_in, middle_back)
        carry = (gs_part, gx_part, *got)
    cu = reduce_rows(*cu_sum)
    rr = reduce_rest(r_part, 2)
    gi, gs = run(
        finish_kernel,
        "finish",
        (0,),
        (meta, order, *carry, et_in, et_out, tfar, gxs[1], gxs[2]),
        [((steps,) + big, BF), (big, F32)],
        [((ROWS, 2 * T), F32), ((ROWS, 6 * T), BF)],
    )
    gi, gs, cu = lax.optimization_barrier((gi, gs, cu))
    cu = (*cu, *[swap_in(x) for x in cu])
    scale = 1.0 / math.sqrt(ROWS * lax.axis_size("wide") * steps)
    gw, gb, cw, cb = run(
        functools.partial(weights_kernel, scale=scale),
        "weights",
        (0,),
        (meta, *cu, *rr),
        [((6 * T, 2 * T), F32), ((1, 2 * T), F32), ((6 * T, T), F32), ((1, T), F32)],
    )
    return gi, gs, gw, gb.reshape(-1), cw, cb.reshape(-1)


def solution(mesh):
    return jax.shard_map(
        per_device,
        mesh=mesh,
        in_specs=(
            P(None, ("parts", "wide"), None),
            P(("parts", "wide"), None),
            P(None, ("parts", "wide"), None),
            P(),
            P(),
            P(),
            P(),
            P(("parts", "wide"), None, None, None),
            P(("parts", "wide"), None),
            P(("parts", "wide")),
            P(("parts", "wide")),
        ),
        out_specs=(
            P(None, ("parts", "wide"), None),
            P(("parts", "wide"), None),
            P("parts", None),
            P("parts"),
            P("parts", None),
            P("parts"),
        ),
        check_vma=False,
    )
```

```python
import functools
import math

import jax
import jax.numpy as jnp
from jax import lax
from jax.experimental import pallas as pl
from jax.experimental.pallas import tpu as pltpu
from jax.sharding import PartitionSpec as P

BF = jnp.bfloat16
F32 = jnp.float32
T = 128
NT = 8
ROWS = NT * T
COUNTS = 34
VMEM_LIMIT = 14 * 1024 * 1024


def swap(block, start):
    count = lax.axis_size("wide")
    return lax.ppermute(
        block, "wide", [p for i in range(start, count - 1, 2) for p in ((i, i + 1), (i + 1, i))]
    )


def swap_in(block):
    return swap(block, 0)


def swap_out(block):
    return swap(block, 1)


def exchange(pay_in, pay_out, far, middle, beside=()):
    got_in = swap_in(pay_in)
    (ready,) = run(middle, "middle", (), (pay_out, got_in, far), [(pay_out.shape, BF)])
    got_out = swap_out(ready)
    got_out, beside = lax.optimization_barrier((got_out, tuple(beside)))
    return (got_in, got_out, swap_in(got_out)), beside


def dot(a, b):
    return jnp.dot(a, b, preferred_element_type=F32)


def dot_nt(a, b):
    return lax.dot_general(a, b, (((1,), (1,)), ((), ())), preferred_element_type=F32)


def dot_tn(a, b):
    return lax.dot_general(a, b, (((0,), (0,)), ((), ())), preferred_element_type=F32)


def tile(ref, i):
    start = i * T if isinstance(i, int) else pl.multiple_of(i * T, T)
    return ref.at[pl.ds(start, T)]


class Place:
    def __init__(self, meta):
        self.idx = lambda r, s: meta[4 * r + s]
        core = meta[32]
        self.core = core
        self.e_in = 7 - 7 * core
        self.n_in = 6 - 5 * core
        self.e_out = 7 * core
        self.n_out = 1 + 5 * core
        self.pos_in = 9 - 9 * core
        self.pos_out = 9 * core
        self.col_in = jnp.where(core == 0, meta[4 * 7 + 3], meta[3])
        self.col_out = jnp.where(core == 0, meta[3], meta[4 * 7 + 3])
        self.t_in = jnp.clip(self.col_in - 1, 0, NT - 1)
        self.t_out = jnp.clip(self.col_out - 1, 0, NT - 1)


def copies(sems, *pairs):
    started = [pltpu.make_async_copy(a, b, sems.at[k]) for k, (a, b) in enumerate(pairs)]
    for copy in started:
        copy.start()

    def wait():
        for copy in started:
            copy.wait()

    return wait


def start_kernel(
    device, cols_hbm, counts_hbm, vals_hbm, order_hbm, inputs_hbm, state_hbm,
    meta, e_in, e_out, et_in, et_out, f_out, ft_in, x0, st, pay_in, pay_out,
    cols, counts, first, last, order, given, state, pick, parts, sems,
):
    small = copies(sems.at[pl.ds(0, 2)], (cols_hbm, cols), (counts_hbm, counts))
    wait_order = copies(sems.at[pl.ds(2, 1)], (order_hbm, order))
    wait_rows = copies(
        sems.at[pl.ds(3, 2)], (inputs_hbm.at[0], given), (state_hbm, state)
    )
    wait_vals = copies(
        sems.at[pl.ds(5, 2)], (vals_hbm.at[0], first), (vals_hbm.at[NT - 1], last)
    )
    wait_order()
    pick_rows(order, pick)
    small()
    for r in range(NT):
        for k in range(4):
            meta[4 * r + k] = cols[k, r] - (device[0] * NT - 1)
        meta[COUNTS + r] = counts[r]
    meta[32] = lax.rem(device[0], 2)
    meta[33] = lax.rem(lax.div(device[0], 2), 2)
    place = Place(meta)
    wait_rows()
    split_f32(state[...], parts, 0)
    parts[:, 3 * T :] = given[...]
    for h in range(4):
        rows = slice(h * 256, (h + 1) * 256)
        got = dot(pick[rows], parts[...])
        st[rows] = got[:, :T] + got[:, T : 2 * T] + got[:, 2 * T : 3 * T]
        x0[rows] = got[:, 3 * T :].astype(BF)
    wait_vals()
    edge_tiles(place, meta, first, last, e_in, e_out, et_in, et_out, f_out, ft_in, pay_in, pay_out)
    write_payload(place, st, e_in, e_out, pay_in, pay_out, S_LANES)
    write_payload(place, x0, e_in, e_out, pay_in, pay_out, X_LANES)


def edge_tiles(place, meta, first, last, e_in, e_out, et_in, et_out, f_out, ft_in, pay_in, pay_out):
    zero = place.core == 0
    for low, side_row, row_far, them, far in (
        (False, place.e_in, place.col_in, place.pos_in, place.pos_out),
        (True, place.e_out, place.col_out, place.pos_out, place.pos_in),
    ):
        top = zero if low else jnp.logical_not(zero)
        vals = [jnp.where(top, first[k].astype(F32), last[k].astype(F32)) for k in range(4)]
        inside = jnp.where(top, vals[2], vals[1])
        ahead = jnp.where(top, vals[1], vals[2])
        live = meta[COUNTS + side_row] > 3

        def third(flag):
            return vals[3] * jnp.where(jnp.logical_and(live, flag), 1.0, 0.0)

        is_them, is_far = row_far == them, row_far == far
        own = third(jnp.logical_not(jnp.logical_or(is_them, is_far)))
        e_ref, et_ref = (e_out, et_out) if low else (e_in, et_in)
        for k, v in enumerate((vals[0], inside, own)):
            e_ref[:, k * T : (k + 1) * T] = v.astype(BF)
            et_ref[k * T : (k + 1) * T] = v.T.astype(BF)
        pay = pay_out if low else pay_in
        pay[2, :, :T] = ahead.astype(BF)
        pay[2, :, T:] = third(is_them).astype(BF)
        if low:
            f_out[...] = third(is_far).astype(BF)
            pay_in[3, :, T:] = third(is_far).astype(BF)
        else:
            pay_in[3, :, :T] = third(is_far).astype(BF)
            ft_in[...] = third(is_far).T.astype(BF)


def pick_rows(order, pick):
    lane = lax.broadcasted_iota(jnp.int32, (T, T), 1).astype(F32)
    for j in range(NT):
        wanted = jnp.broadcast_to(order[j : j + 1, :].astype(F32), (T, T)).T
        for k in range(NT):
            pick[j * T : (j + 1) * T, k * T : (k + 1) * T] = (
                (wanted == lane + float(k * T)).astype(F32).astype(BF)
            )


def split_f32(value, ref, start):
    for k in range(3):
        part = value.astype(BF)
        ref[:, start + k * T : start + (k + 1) * T] = part
        value = value - part.astype(F32)


def write_payload(place, own, e_in, e_out, pay_in, pay_out, lanes):
    for e_ref, pay, tiles in (
        (e_in, pay_in, (place.e_in, place.n_in, place.t_in)),
        (e_out, pay_out, (place.e_out, place.n_out, place.t_out)),
    ):
        picked = [tile(own, i)[...].astype(BF) for i in tiles]
        pay[0, :, lanes] = picked[0]
        pay[1, :, lanes] = dot(e_ref[...], jnp.concatenate(picked, axis=0)).astype(BF)


S_LANES, X_LANES = slice(0, T), slice(T, 2 * T)


def rest_kernel(order, in1, in2, cot, x1, x2, c0, c1, c2, pick, parts):
    pick_rows(order, pick)
    for k, src in enumerate((in1[0], in2[0], cot[0], cot[1], cot[2])):
        parts[:, k * T : (k + 1) * T] = src
    for h in range(4):
        rows = slice(h * 256, (h + 1) * 256)
        got = dot(pick[rows], parts[...]).astype(BF)
        for k, out in enumerate((x1, x2, c0, c1, c2)):
            out[rows] = got[:, k * T : (k + 1) * T]


def operator_kernel(meta, vals, vfg, vbg, vbd):
    for r in range(NT):
        live = jnp.where(meta[COUNTS + r] > 3, 1.0, 0.0)
        last = (vals[r, 3].astype(F32) * live).astype(BF)
        vfg[r, :, 0:T] = vals[r, 1]
        vfg[r, :, T : 2 * T] = vals[r, 0]
        vfg[r, :, 2 * T : 3 * T] = vals[r, 2]
        vfg[r, :, 3 * T :] = last
        vbg[r, :, T : 2 * T] = vals[r, 0].T
        if r > 0:
            vbg[r - 1, :, 2 * T :] = vals[r, 1].T
        else:
            vbd[8] = vals[r, 1].T
        if r < NT - 1:
            vbg[r + 1, :, 0:T] = vals[r, 2].T
        else:
            vbd[9] = vals[r, 2].T
        vbd[r] = last.T
    vbg[0, :, 0:T] = jnp.zeros((T, T), BF)
    vbg[NT - 1, :, 2 * T :] = jnp.zeros((T, T), BF)


def turn_kernel(rin, rout, vin, vout, tin, tout, tfar):
    vin[...] = rin[2:]
    vout[...] = rout[2:]
    for k in range(2):
        lanes = slice(k * T, (k + 1) * T)
        tin[:, lanes] = rin[2, :, lanes].astype(F32).T.astype(BF)
        tout[:, lanes] = rout[2, :, lanes].astype(F32).T.astype(BF)
    tfar[...] = rin[3, :, T:].astype(F32).T.astype(BF)


def middle_forward(pay, got, far, out):
    out[0] = pay[0]
    out[1] = (pay[1].astype(F32) + dot(far[...], got[0])).astype(BF)
    if pay.shape[0] > 2:
        out[2] = pay[2]


def middle_back(pay, got, far, out):
    out[0] = (pay[0].astype(F32) + dot(far[...], got[1])).astype(BF)
    out[1] = pay[1]


def forward_row(place, vfg, src, r):
    low = tile(src, place.idx(0, 1))[...] if r == 0 else tile(src, r)[...]
    high = tile(src, place.idx(7, 2))[...] if r == 7 else tile(src, r + 2)[...]
    picked = jnp.concatenate(
        [low, tile(src, r + 1)[...], high, tile(src, place.idx(r, 3))[...]], axis=0
    )
    return dot(vfg[r], picked)


def first_order(place, vfg, vin, vout, zext, d1, rin, rout, rfwd):
    tile(zext, place.pos_in)[...] = rin[0]
    tile(zext, place.pos_out)[...] = rout[0]
    for r in range(NT):
        tile(d1, r + 1)[...] = forward_row(place, vfg, zext, r).astype(BF)
    edge = tile(zext, place.e_in + 1)[...]
    lhs = jnp.concatenate([vin[0], vin[1, :, :T]], axis=1)
    total = rin[1].astype(F32) + dot(lhs, jnp.concatenate([edge, edge, rfwd[0]], axis=0))
    tile(d1, place.pos_in)[...] = total.astype(BF)
    edge = tile(zext, place.e_out + 1)[...]
    total = rout[1].astype(F32) + dot(vout[0], jnp.concatenate([edge, edge], axis=0))
    tile(d1, place.pos_out)[...] = total.astype(BF)


def second_order(place, vfg, zext, d1, r):
    z = tile(zext, r + 1)[...].astype(F32)
    return (2.0 * forward_row(place, vfg, d1, r) - z).astype(BF)


def gate_kernel(
    meta, st, x, rin, rout, rfwd, vfg, *rest, first
):
    if first:
        vin, vout = rin.at[pl.ds(2, 2)], rout.at[pl.ds(2, 1)]
    else:
        vin, vout, *rest = rest
    e_in, e_out, gw, gb, feats, r_out, q_out, pay_in, pay_out, zext, d1 = rest
    place = Place(meta)
    zext[T : T + ROWS, :T] = st[...].astype(BF)
    zext[T : T + ROWS, T:] = x[...]
    first_order(place, vfg, vin, vout, zext, d1, rin, rout, rfwd)
    for r in range(NT):
        d2 = second_order(place, vfg, zext, d1, r)
        z = tile(zext, r + 1)[...]
        one = tile(d1, r + 1)[...]
        row = jnp.concatenate(
            [z[:, T:], one[:, T:], d2[:, T:], z[:, :T], one[:, :T], d2[:, :T]], axis=1
        )
        tile(feats, r)[...] = row
    for h in range(4):
        rows = slice(h * 256, (h + 1) * 256)
        reset = jax.nn.sigmoid(dot(feats[rows], gw[:, :T]) + gb[:, :T])
        r_out[rows] = reset
        q_out[rows] = (reset * st[rows]).astype(BF)
    write_payload(place, q_out, e_in, e_out, pay_in, pay_out, S_LANES)


def update_kernel(feats, gw, gb, cw, cb, u_out, xc_out):
    for h in range(4):
        rows = slice(h * 256, (h + 1) * 256)
        f = feats[rows]
        u_out[rows] = jax.nn.sigmoid(dot(f, gw[:, T:]) + gb[:, T:])
        xc_out[rows] = dot(f[:, : 3 * T], cw[: 3 * T]) + cb[...]


def cand_kernel(meta, q, rin, rout, rfwd, vfg, vin, vout, e_in, e_out, cw, xc, u, st, *rest, last):
    if last:
        fq, c_out, zext, d1 = rest
    else:
        x_next, fq, c_out, st_out, pay_in, pay_out, zext, d1 = rest
    place = Place(meta)
    zext[T : T + ROWS] = q[...]
    first_order(place, vfg, vin, vout, zext, d1, rin, rout, rfwd)
    for r in range(NT):
        d2 = second_order(place, vfg, zext, d1, r)
        tile(fq, r)[...] = jnp.concatenate(
            [tile(zext, r + 1)[...], tile(d1, r + 1)[...], d2], axis=1
        )
    for h in range(4):
        rows = slice(h * 256, (h + 1) * 256)
        cand = jnp.tanh(dot(fq[rows], cw[3 * T :]) + xc[rows])
        c_out[rows] = cand
        if not last:
            st_out[rows] = u[rows] * st[rows] + (1.0 - u[rows]) * cand
    if not last:
        write_payload(place, st_out, e_in, e_out, pay_in, pay_out, S_LANES)
        write_payload(place, x_next, e_in, e_out, pay_in, pay_out, X_LANES)


def add_received(place, acc, rin, rout, rfwd, et_in, et_out, tfar):
    got_in = dot(et_in[...], rin[1])
    got_out = dot(et_out[...], rout[1])
    for i, block in (
        (place.e_in, got_in[:T] + rin[0].astype(F32) + dot(tfar[...], rfwd[1])),
        (place.n_in, got_in[T : 2 * T]),
        (place.t_in, got_in[2 * T :]),
        (place.e_out, got_out[:T] + rout[0].astype(F32)),
        (place.n_out, got_out[T : 2 * T]),
        (place.t_out, got_out[2 * T :]),
    ):
        tile(acc, i)[...] += block


def back_rows(place, vbg, vbd, y, acc, base):
    zero = jnp.zeros((T, acc.shape[1]), F32)
    tile(acc, 0)[...] = zero
    tile(acc, 9)[...] = zero
    for r in range(NT):
        lo, hi = max(r - 1, 0), min(r + 2, NT)
        lhs = vbg[r, :, (lo - r + 1) * T : (hi - r + 1) * T]
        tile(acc, r + 1)[...] = base(r, dot(lhs, y[lo * T : hi * T]))
    parts = [(place.idx(0, 1), 8, 0), (place.idx(7, 2), 9, 7)]
    parts += [(place.idx(r, 3), r, r) for r in range(NT)]
    for i, k, r in parts:
        tile(acc, i)[...] += dot(vbd[k], y[r * T : (r + 1) * T])


def diffuse_back(place, vbg, vbd, tin, tout, a, y, w, acc, pay_in, pay_out):
    for r in range(NT):
        rows = slice(r * T, (r + 1) * T)
        y[rows] = a(2, rows).astype(BF)
    back_rows(
        place, vbg, vbd, y, acc, lambda r, v: a(1, slice(r * T, (r + 1) * T)) * 0.5 + v
    )
    for e in range(NT + 2):
        tile(w, e)[...] = (2.0 * tile(acc, e)[...]).astype(BF)
    own = w.at[pl.ds(T, ROWS)]

    def second(r, v):
        rows = slice(r * T, (r + 1) * T)
        return a(0, rows) - a(2, rows) + v

    back_rows(place, vbg, vbd, own, acc, second)
    for pos, edge, vals, pay in (
        (place.pos_in, place.e_in, tin, pay_in),
        (place.pos_out, place.e_out, tout, pay_out),
    ):
        part = tile(w, pos)[...]
        tile(acc, edge + 1)[...] += dot(vals[...], jnp.concatenate([part, part], axis=0))
        pay[0] = tile(acc, pos)[...].astype(BF)
        pay[1] = part


def cand_back_kernel(*refs, first):
    refs = list(refs)
    take = lambda n: [refs.pop(0) for _ in range(n)]
    meta, cot, u, c, st, cw, vbg, vbd, tin, tout, et_in, et_out, tfar = take(13)
    if not first:
        gs_part, gx_part, rin, rout, rfwd = take(5)
    gp_out, ec_out, eu_out, gq_out, sums, pay_in, pay_out = take(7)
    if not first:
        (gx_out,) = take(1)
    gs, g, y, w, acc = take(5)
    place = Place(meta)
    if not first:
        gs[:, :T] = gs_part[...]
        gs[:, T:] = gx_part[...]
        add_received(place, gs, rin, rout, rfwd, et_in, et_out, tfar)
        gx_out[...] = gs[:, T:].astype(BF)
    sum_c = jnp.zeros((1, T), F32)
    sum_u = jnp.zeros((1, T), F32)
    for h in range(NT):
        rows = slice(h * T, (h + 1) * T)
        grad = cot[rows].astype(F32)
        if not first:
            grad = grad + gs[rows, :T]
        upd, cand = u[rows], c[rows]
        pre = grad * (1.0 - upd) * (1.0 - cand * cand)
        gate = grad * (st[rows] - cand) * upd * (1.0 - upd)
        gp_out[rows] = grad * upd
        ec_out[rows] = pre.astype(BF)
        eu_out[rows] = gate.astype(BF)
        sum_c = sum_c + jnp.sum(pre, axis=0, keepdims=True)
        sum_u = sum_u + jnp.sum(gate, axis=0, keepdims=True)
    sums[...] = jnp.broadcast_to(jnp.concatenate([sum_c, sum_u], axis=1), (8, 2 * T))
    g[...] = dot_nt(ec_out[...], cw[3 * T :])
    diffuse_back(
        place, vbg, vbd, tin, tout,
        lambda k, rows: g[rows, k * T : (k + 1) * T],
        y, w, acc, pay_in, pay_out,
    )
    gq_out[...] = acc[T : T + ROWS]


def gate_back_kernel(
    meta, gq_part, rin, rout, rfwd, gp, r_ref, st, ec, eu, gw, cw,
    vbg, vbd, tin, tout, et_in, et_out, tfar,
    gs_out, gx_out, er_out, sums, pay_in, pay_out, gq, eg, gps, g, y, w, acc,
):
    place = Place(meta)
    gq[...] = gq_part[...]
    add_received(place, gq, rin, rout, rfwd, et_in, et_out, tfar)
    sum_r = jnp.zeros((1, T), F32)
    for h in range(NT):
        rows = slice(h * T, (h + 1) * T)
        grad, reset = gq[rows], r_ref[rows]
        gps[rows] = gp[rows] + grad * reset
        pre = grad * st[rows] * reset * (1.0 - reset)
        eg[rows, :T] = pre.astype(BF)
        sum_r = sum_r + jnp.sum(pre, axis=0, keepdims=True)
    eg[:, T:] = eu[...]
    er_out[...] = eg[:, :T]
    sums[...] = jnp.broadcast_to(sum_r, (8, T))
    e = eg[...]
    for k in range(3):
        cols = slice(2 * k * T, (2 * k + 1) * T)
        g[:, cols] = dot_nt(e, gw[(3 + k) * T : (4 + k) * T])
        cols = slice((2 * k + 1) * T, (2 * k + 2) * T)
        g[:, cols] = dot_nt(e, gw[k * T : (k + 1) * T]) + dot_nt(
            ec[...], cw[k * T : (k + 1) * T]
        )
    diffuse_back(
        place, vbg, vbd, tin, tout,
        lambda k, rows: g[rows, 2 * k * T : 2 * (k + 1) * T],
        y, w, acc, pay_in, pay_out,
    )
    gs_out[...] = acc[T : T + ROWS, :T] + gps[...]
    gx_out[...] = acc[T : T + ROWS, T:]


def add_rows(out, value, rest, rows):
    out[rows] = value + rest[0][rows] if rest else value


def split_columns(meta, total, kept, sent):
    half = total.shape[1] // 2
    mine = meta[32] == 0
    low, high = total[:, :half], total[:, half:]
    kept[...] = jnp.where(mine, low, high)
    sent[...] = jnp.where(mine, high, low).astype(BF)


def weight_cu_kernel(meta, ec, eu, sums, feats, fq, *rest):
    *rest, out = rest
    x = feats[:, : 3 * T]
    both = jnp.concatenate([dot_tn(ec[...], x), dot_tn(ec[...], fq[...])], axis=1)
    add_rows(out, both, rest, slice(0, T))
    add_rows(out, dot_tn(eu[...], feats[...]), rest, slice(T, 2 * T))
    row = jnp.concatenate([sums[...], jnp.zeros((8, 4 * T), F32)], axis=1)
    add_rows(out, jnp.concatenate([row] * 4, axis=0), rest, slice(2 * T, 2 * T + 32))


def weight_cu_last_kernel(meta, ec, eu, sums, feats, fq, before, kept, sent, out):
    weight_cu_kernel(meta, ec, eu, sums, feats, fq, before, out)
    split_columns(meta, out, kept, sent)


def weight_r_kernel(meta, er, sums, feats, *rest):
    *rest, out = rest
    add_rows(out, dot_tn(er[...], feats[...]), rest, slice(0, T))
    row = jnp.concatenate([sums[...], jnp.zeros((8, 5 * T), F32)], axis=1)
    add_rows(out, jnp.concatenate([row, row], axis=0), rest, slice(T, T + 16))


def weight_r_last_kernel(meta, er, sums, feats, before, kept, sent, out):
    weight_r_kernel(meta, er, sums, feats, before, out)
    split_columns(meta, out, kept, sent)


def add_kernel(a, b, out):
    out[...] = (a[...].astype(F32) + b[...].astype(F32)).astype(BF)


def add_split_kernel(meta, a, b, kept, sent):
    total = (a[...].astype(F32) + b[...].astype(F32)).astype(BF)
    half = total.shape[0] // 2
    upper = meta[33] == 1
    top, bottom = total[:half].astype(F32), total[half:].astype(F32)
    kept[...] = jnp.where(upper, bottom, top).astype(BF)
    sent[...] = jnp.where(upper, top, bottom).astype(BF)


def sum_of(a, b):
    return run(add_kernel, "add", (), (a, b), [(a.shape, BF)])[0]


def reduce_step(part, step):
    count = lax.axis_size("wide")
    other = lax.ppermute(part, "wide", [(i, i ^ step) for i in range(count)])
    return sum_of(part, other)


def reduce_rows(kept, sent):
    count = lax.axis_size("wide")
    route = [(i, i ^ 2) for i in range(count)]
    part = sum_of(kept, lax.ppermute(sent, "wide", route))
    step = 4
    while step < count:
        part = reduce_step(part, step)
        step *= 2
    return part, lax.ppermute(part, "wide", route)


def reduce_rest(part, step):
    while step < lax.axis_size("wide"):
        part = reduce_step(part, step)
        step *= 2
    return part, swap_in(part)


def weights_kernel(
    meta, cu_a, cu_b, cu_a_other, cu_b_other, r_own, r_other, gw, gb, cw, cb, *, scale
):
    mine = meta[32] == 0
    upper = meta[33] == 1

    def pick(own, other, side):
        a, b = own[...].astype(F32), other[...].astype(F32)
        return jnp.where(mine, a, b) if side == 0 else jnp.where(mine, b, a)

    def rows_of(a, b):
        low, high = jnp.where(upper, b, a), jnp.where(upper, a, b)
        return jnp.concatenate([low, high], axis=0)

    for side in range(2):
        cu = rows_of(pick(cu_a, cu_a_other, side), pick(cu_b, cu_b_other, side)) * scale
        r = pick(r_own, r_other, side) * scale
        for k in range(3):
            cols = slice(k * T, (k + 1) * T)
            rows = slice((3 * side + k) * T, (3 * side + k + 1) * T)
            cw[rows] = cu[:T, cols].T
            gw[rows, T:] = cu[T : 2 * T, cols].T
            gw[rows, :T] = r[:T, cols].T
        if side == 0:
            cb[...] = cu[2 * T : 2 * T + 1, :T]
            gb[:, T:] = cu[2 * T : 2 * T + 1, T : 2 * T]
            gb[:, :T] = r[T : T + 1, :T]


def finish_kernel(
    meta, order, gs_part, gx_part, rin, rout, rfwd, et_in, et_out, tfar, gx1, gx2,
    gi_out, gs_out, gs, parts,
):
    place = Place(meta)
    gs[:, :T] = gs_part[...]
    gs[:, T:] = gx_part[...]
    add_received(place, gs, rin, rout, rfwd, et_in, et_out, tfar)
    split_f32(gs[:, :T], parts, 0)
    parts[:, 3 * T : 4 * T] = gs[:, T:].astype(BF)
    parts[:, 4 * T : 5 * T] = gx1[...]
    parts[:, 5 * T :] = gx2[...]
    row = lax.broadcasted_iota(jnp.int32, (T, T), 0)
    for k in range(NT):
        put = jnp.concatenate(
            [
                (jnp.broadcast_to(order[j : j + 1, :], (T, T)) == row + k * T)
                .astype(F32)
                .astype(BF)
                for j in range(NT)
            ],
            axis=1,
        )
        rows = slice(k * T, (k + 1) * T)
        got = dot(put, parts[...])
        gs_out[rows] = got[:, :T] + got[:, T : 2 * T] + got[:, 2 * T : 3 * T]
        for t in range(3):
            gi_out[t, rows] = got[:, (3 + t) * T : (4 + t) * T].astype(BF)


SMEM = pl.BlockSpec(memory_space=pltpu.SMEM)
VMEM = pl.BlockSpec(memory_space=pltpu.VMEM)


HBM = pl.BlockSpec(memory_space=pltpu.HBM)


def run(
    kernel, name, smem, args, outs, scratch=(), specs=None, flops=10**8,
    hbm=(), smem_outs=(), sems=0,
):
    grid = (1,) if specs else ()
    specs = specs or [
        SMEM if i in smem else HBM if i in hbm else VMEM for i in range(len(args))
    ]
    out_shape = [jax.ShapeDtypeStruct(s, d) for s, d in outs]
    args = [
        pltpu.with_memory_space_constraint(x, pltpu.HBM) if i in hbm else x
        for i, x in enumerate(args)
    ]
    moved = sum(math.prod(x.shape) * x.dtype.itemsize for x in (*args, *out_shape))
    return pl.pallas_call(
        kernel,
        name=name,
        grid=grid,
        in_specs=specs,
        out_specs=[SMEM if i in smem_outs else VMEM for i in range(len(outs))],
        out_shape=out_shape,
        scratch_shapes=[pltpu.VMEM(*s) if isinstance(s, tuple) else s for s in scratch]
        + ([pltpu.SemaphoreType.DMA((sems,))] if sems else []),
        cost_estimate=pl.CostEstimate(flops=flops, bytes_accessed=moved, transcendentals=0),
        compiler_params=pltpu.CompilerParams(vmem_limit_bytes=VMEM_LIMIT),
    )(*args)


def leading(block, at):
    zeros = (0,) * (len(block) - 1)
    return pl.BlockSpec(block, lambda i: (at,) + zeros, memory_space=pltpu.VMEM)


def per_device(
    inputs, state_init, cotangent, gate_w, gate_b, cand_w, cand_b,
    tile_vals, tile_cols, tile_counts, sector_order,
):
    order = sector_order.reshape(NT, T)
    gb = gate_b.reshape(1, -1)
    cb = cand_b.reshape(1, -1)
    big = (ROWS, T)
    square = (T, T)
    flat, tall = ((T, 3 * T), BF), ((3 * T, T), BF)
    x_block = (1, ROWS, T)
    device = lax.axis_index("wide").astype(jnp.int32).reshape(1)
    meta, e_in, e_out, et_in, et_out, f_out, ft_in, x0, st, *pay = run(
        start_kernel, "start", (0,),
        (device, tile_cols.T, tile_counts, tile_vals, order, inputs, state_init),
        [((COUNTS + NT,), jnp.int32), flat, flat, tall, tall, (square, BF), (square, BF)]
        + [(big, BF), (big, F32), ((4, T, 2 * T), BF), ((3, T, 2 * T), BF)],
        [
            pltpu.SMEM((4, NT), jnp.int32), pltpu.SMEM((NT,), jnp.int32),
            ((4, T, T), BF), ((4, T, T), BF), ((NT, T), jnp.int32), (big, BF), (big, F32),
            ((ROWS, ROWS), BF), ((ROWS, 4 * T), BF),
        ],
        hbm=(1, 2, 3, 4, 5, 6), sems=7, smem_outs=(0,), flops=10**9,
    )
    vfg, vbg, vbd = run(
        operator_kernel, "operator", (0,), (meta, tile_vals),
        [((NT, T, 4 * T), BF), ((NT, T, 3 * T), BF), ((NT + 2, T, T), BF)],
    )
    x1, x2, *cots = run(
        rest_kernel, "rest", (), (order, inputs, inputs, cotangent), [(big, BF)] * 5,
        [((ROWS, ROWS), BF), ((ROWS, 5 * T), BF)],
        specs=[VMEM, leading(x_block, 1), leading(x_block, 2), VMEM],
        flops=10**9,
    )
    saved = []
    steps = inputs.shape[0]
    wide = ((NT + 2) * T, 2 * T)
    slim = ((NT + 2) * T, T)
    beside = (vfg, vbg, vbd)
    for t in range(steps):
        last = t == steps - 1
        got, beside = exchange(*pay, f_out, middle_forward, beside)
        if t == 0:
            vfg, vbg, vbd = beside
            turned = run(
                turn_kernel, "turn", (), got[:2],
                [((2, T, 2 * T), BF), ((1, T, 2 * T), BF)] + [((T, 2 * T), BF)] * 2
                + [(square, BF)],
            )
            xs, ops = (x0,), (vfg, e_in, e_out)
        feats, r, q, *pay = run(
            functools.partial(gate_kernel, first=t == 0),
            "gate",
            (0,),
            (meta, st, xs[t], *got, *ops, gate_w, gb),
            [((ROWS, 6 * T), BF), (big, F32), (big, BF)] + [((2, T, T), BF)] * 2,
            [(wide, BF)] * 2,
        )
        beside = tuple(run(
            update_kernel,
            "update",
            (),
            (feats, gate_w, gb, cand_w, cb),
            [(big, F32)] * 2,
            flops=5 * 10**8,
        ))
        if t == 0:
            beside += (x1, x2, *cots, *turned)
        got, (u, xc, *beside) = exchange(*pay, f_out, middle_forward, beside)
        if t == 0:
            xs += tuple(beside[:2])
            cots = beside[2:5]
            vin, vout, tin, tout, tfar = beside[5:]
            ops = (vfg, vin, vout, e_in, e_out)
        fq, c, *rest = run(
            functools.partial(cand_kernel, last=last),
            "cand",
            (0,),
            (meta, q, *got, *ops, cand_w, xc, u, st) + (() if last else (xs[t + 1],)),
            [((ROWS, 3 * T), BF), (big, F32)]
            + ([] if last else [(big, F32)] + [((2, T, 2 * T), BF)] * 2),
            [(slim, BF)] * 2,
        )
        saved.append((st, r, u, c, feats, fq))
        if not last:
            st, *pay = rest
            beside = ()
    ops = (vbg, vbd, tin, tout, et_in, et_out, tfar)
    gxs = [None] * steps
    carry, cu_sum, r_sum = (), (), ()
    for t in reversed(range(steps)):
        st, r, u, c, feats, fq = saved[t]
        first = t == steps - 1
        gp, ec, eu, gq, sums, *rest = run(
            functools.partial(cand_back_kernel, first=first),
            "cand_back",
            (0,),
            (meta, cots[t], u, c, st, cand_w) + ops + carry,
            [(big, F32), (big, BF), (big, BF), (big, F32), ((8, 2 * T), F32)]
            + [((2, T, T), BF)] * 2
            + ([] if first else [(big, BF)]),
            [((ROWS, 2 * T), F32), ((ROWS, 3 * T), F32), (big, BF), (slim, BF), (slim, F32)],
        )
        if not first:
            gxs[t + 1] = rest[2]
        last = t == 0
        rows, columns = 2 * T + 32, 6 * T
        args = (meta, ec, eu, sums, feats, fq, *cu_sum)
        if not last:
            cu_sum = run(
                weight_cu_kernel, "weight_cu", (0,), args, [((rows, columns), F32)],
                flops=4 * 10**8,
            )
        else:
            kept, sent = run(
                weight_cu_last_kernel, "weight_cu", (0,), args,
                [((rows, columns // 2), F32), ((rows, columns // 2), BF)],
                [((rows, columns), F32)], flops=4 * 10**8,
            )
            cu_sum = run(
                add_split_kernel, "add_split", (0,), (meta, kept, swap_in(sent)),
                [((rows // 2, columns // 2), BF)] * 2,
            )
        got, cu_sum = exchange(*rest[:2], ft_in, middle_back, cu_sum)
        gs_part, gx_part, er, sums, *rest = run(
            gate_back_kernel,
            "gate_back",
            (0,),
            (meta, gq, *got, gp, r, st, ec, eu, gate_w, cand_w) + ops,
            [(big, F32), (big, F32), (big, BF), ((8, T), F32)] + [((2, T, 2 * T), BF)] * 2,
            [
                (big, F32), ((ROWS, 2 * T), BF), (big, F32), ((ROWS, 6 * T), F32),
                ((ROWS, 2 * T), BF), (wide, BF), (wide, F32),
            ],
        )
        args = (meta, er, sums, feats, *r_sum)
        rows = T + 16
        if not last:
            r_sum = run(
                weight_r_kernel, "weight_r", (0,), args, [((rows, columns), F32)],
                flops=2 * 10**8,
            )
            got, r_sum = exchange(*rest, ft_in, middle_back, r_sum)
        else:
            kept, sent = run(
                weight_r_last_kernel, "weight_r", (0,), args,
                [((rows, columns // 2), F32), ((rows, columns // 2), BF)],
                [((rows, columns), F32)], flops=2 * 10**8,
            )
            r_part = sum_of(kept, swap_in(sent))
            got, _ = exchange(*rest, ft_in, middle_back)
        carry = (gs_part, gx_part, *got)
    cu = reduce_rows(*cu_sum)
    rr = reduce_rest(r_part, 2)
    gi, gs = run(
        finish_kernel,
        "finish",
        (0,),
        (meta, order, *carry, et_in, et_out, tfar, gxs[1], gxs[2]),
        [((steps,) + big, BF), (big, F32)],
        [((ROWS, 2 * T), F32), ((ROWS, 6 * T), BF)],
    )
    cu = (*cu, *[swap_in(x) for x in cu])
    scale = 1.0 / math.sqrt(ROWS * lax.axis_size("wide") * steps)
    gw, gb, cw, cb = run(
        functools.partial(weights_kernel, scale=scale),
        "weights",
        (0,),
        (meta, *cu, *rr),
        [((6 * T, 2 * T), F32), ((1, 2 * T), F32), ((6 * T, T), F32), ((1, T), F32)],
    )
    return gi, gs, gw, gb.reshape(-1), cw, cb.reshape(-1)


def solution(mesh):
    return jax.shard_map(
        per_device,
        mesh=mesh,
        in_specs=(
            P(None, ("parts", "wide"), None),
            P(("parts", "wide"), None),
            P(None, ("parts", "wide"), None),
            P(),
            P(),
            P(),
            P(),
            P(("parts", "wide"), None, None, None),
            P(("parts", "wide"), None),
            P(("parts", "wide")),
            P(("parts", "wide")),
        ),
        out_specs=(
            P(None, ("parts", "wide"), None),
            P(("parts", "wide"), None),
            P("parts", None),
            P("parts"),
            P("parts", None),
            P("parts"),
        ),
        check_vma=False,
    )
```

```python
import functools
import math

import jax
import jax.numpy as jnp
from jax import lax
from jax.experimental import pallas as pl
from jax.experimental.pallas import tpu as pltpu
from jax.sharding import PartitionSpec as P

BF = jnp.bfloat16
F32 = jnp.float32
T = 128
NT = 8
ROWS = NT * T
COUNTS = 34
VMEM_LIMIT = 14 * 1024 * 1024


def swap(block, start):
    count = lax.axis_size("wide")
    return lax.ppermute(
        block, "wide", [p for i in range(start, count - 1, 2) for p in ((i, i + 1), (i + 1, i))]
    )


def swap_in(block):
    return swap(block, 0)


def swap_out(block):
    return swap(block, 1)


def exchange(pay_in, pay_out, far, middle, beside=()):
    got_in = swap_in(pay_in)
    (ready,) = run(middle, "middle", (), (pay_out, got_in, far), [(pay_out.shape, BF)])
    got_out = swap_out(ready)
    got_out, beside = lax.optimization_barrier((got_out, tuple(beside)))
    return (got_in, got_out, swap_in(got_out)), beside


def dot(a, b):
    return jnp.dot(a, b, preferred_element_type=F32)


def dot_nt(a, b):
    return lax.dot_general(a, b, (((1,), (1,)), ((), ())), preferred_element_type=F32)


def dot_tn(a, b):
    return lax.dot_general(a, b, (((0,), (0,)), ((), ())), preferred_element_type=F32)


def tile(ref, i):
    start = i * T if isinstance(i, int) else pl.multiple_of(i * T, T)
    return ref.at[pl.ds(start, T)]


class Place:
    def __init__(self, meta):
        self.idx = lambda r, s: meta[4 * r + s]
        core = meta[32]
        self.core = core
        self.e_in = 7 - 7 * core
        self.n_in = 6 - 5 * core
        self.e_out = 7 * core
        self.n_out = 1 + 5 * core
        self.pos_in = 9 - 9 * core
        self.pos_out = 9 * core
        self.col_in = jnp.where(core == 0, meta[4 * 7 + 3], meta[3])
        self.col_out = jnp.where(core == 0, meta[3], meta[4 * 7 + 3])
        self.t_in = jnp.clip(self.col_in - 1, 0, NT - 1)
        self.t_out = jnp.clip(self.col_out - 1, 0, NT - 1)


def copies(sems, *pairs):
    started = [pltpu.make_async_copy(a, b, sems.at[k]) for k, (a, b) in enumerate(pairs)]
    for copy in started:
        copy.start()

    def wait():
        for copy in started:
            copy.wait()

    return wait


def start_kernel(
    device, cols_hbm, counts_hbm, vals_hbm, order_hbm, inputs_hbm, state_hbm,
    meta, e_in, e_out, et_in, et_out, f_out, ft_in, x0, st, pay_in, pay_out,
    cols, counts, first, last, order, given, state, pick, parts, sems,
):
    small = copies(sems.at[pl.ds(0, 2)], (cols_hbm, cols), (counts_hbm, counts))
    wait_order = copies(sems.at[pl.ds(2, 1)], (order_hbm, order))
    wait_rows = copies(
        sems.at[pl.ds(3, 2)], (inputs_hbm.at[0], given), (state_hbm, state)
    )
    wait_vals = copies(
        sems.at[pl.ds(5, 2)], (vals_hbm.at[0], first), (vals_hbm.at[NT - 1], last)
    )
    wait_order()
    pick_rows(order, pick)
    small()
    for r in range(NT):
        for k in range(4):
            meta[4 * r + k] = cols[k, r] - (device[0] * NT - 1)
        meta[COUNTS + r] = counts[r]
    meta[32] = lax.rem(device[0], 2)
    meta[33] = lax.rem(lax.div(device[0], 2), 2)
    place = Place(meta)
    wait_rows()
    split_f32(state[...], parts, 0)
    parts[:, 3 * T :] = given[...]
    for h in range(4):
        rows = slice(h * 256, (h + 1) * 256)
        got = dot(pick[rows], parts[...])
        st[rows] = got[:, :T] + got[:, T : 2 * T] + got[:, 2 * T : 3 * T]
        x0[rows] = got[:, 3 * T :].astype(BF)
    wait_vals()
    edge_tiles(place, meta, first, last, e_in, e_out, et_in, et_out, f_out, ft_in, pay_in, pay_out)
    write_payload(place, st, e_in, e_out, pay_in, pay_out, S_LANES)
    write_payload(place, x0, e_in, e_out, pay_in, pay_out, X_LANES)


def edge_tiles(place, meta, first, last, e_in, e_out, et_in, et_out, f_out, ft_in, pay_in, pay_out):
    zero = place.core == 0
    for low, side_row, row_far, them, far in (
        (False, place.e_in, place.col_in, place.pos_in, place.pos_out),
        (True, place.e_out, place.col_out, place.pos_out, place.pos_in),
    ):
        top = zero if low else jnp.logical_not(zero)
        vals = [jnp.where(top, first[k].astype(F32), last[k].astype(F32)) for k in range(4)]
        inside = jnp.where(top, vals[2], vals[1])
        ahead = jnp.where(top, vals[1], vals[2])
        live = meta[COUNTS + side_row] > 3

        def third(flag):
            return vals[3] * jnp.where(jnp.logical_and(live, flag), 1.0, 0.0)

        is_them, is_far = row_far == them, row_far == far
        own = third(jnp.logical_not(jnp.logical_or(is_them, is_far)))
        e_ref, et_ref = (e_out, et_out) if low else (e_in, et_in)
        for k, v in enumerate((vals[0], inside, own)):
            e_ref[:, k * T : (k + 1) * T] = v.astype(BF)
            et_ref[k * T : (k + 1) * T] = v.T.astype(BF)
        pay = pay_out if low else pay_in
        pay[2, :, :T] = ahead.astype(BF)
        pay[2, :, T:] = third(is_them).astype(BF)
        if low:
            f_out[...] = third(is_far).astype(BF)
            pay_in[3, :, T:] = third(is_far).astype(BF)
        else:
            pay_in[3, :, :T] = third(is_far).astype(BF)
            ft_in[...] = third(is_far).T.astype(BF)


def pick_rows(order, pick):
    lane = lax.broadcasted_iota(jnp.int32, (T, T), 1).astype(F32)
    for j in range(NT):
        wanted = jnp.broadcast_to(order[j : j + 1, :].astype(F32), (T, T)).T
        for k in range(NT):
            pick[j * T : (j + 1) * T, k * T : (k + 1) * T] = (
                (wanted == lane + float(k * T)).astype(F32).astype(BF)
            )


def split_f32(value, ref, start):
    for k in range(3):
        part = value.astype(BF)
        ref[:, start + k * T : start + (k + 1) * T] = part
        value = value - part.astype(F32)


def write_payload(place, own, e_in, e_out, pay_in, pay_out, lanes):
    for e_ref, pay, tiles in (
        (e_in, pay_in, (place.e_in, place.n_in, place.t_in)),
        (e_out, pay_out, (place.e_out, place.n_out, place.t_out)),
    ):
        picked = [tile(own, i)[...].astype(BF) for i in tiles]
        pay[0, :, lanes] = picked[0]
        pay[1, :, lanes] = dot(e_ref[...], jnp.concatenate(picked, axis=0)).astype(BF)


S_LANES, X_LANES = slice(0, T), slice(T, 2 * T)


def rest_kernel(order, in1, in2, cot, x1, x2, c0, c1, c2, pick, parts):
    pick_rows(order, pick)
    for k, src in enumerate((in1[0], in2[0], cot[0], cot[1], cot[2])):
        parts[:, k * T : (k + 1) * T] = src
    for h in range(4):
        rows = slice(h * 256, (h + 1) * 256)
        got = dot(pick[rows], parts[...]).astype(BF)
        for k, out in enumerate((x1, x2, c0, c1, c2)):
            out[rows] = got[:, k * T : (k + 1) * T]


def operator_kernel(meta, vals, vfg, vbg, vbd):
    for r in range(NT):
        live = jnp.where(meta[COUNTS + r] > 3, 1.0, 0.0)
        last = (vals[r, 3].astype(F32) * live).astype(BF)
        vfg[r, :, 0:T] = vals[r, 1]
        vfg[r, :, T : 2 * T] = vals[r, 0]
        vfg[r, :, 2 * T : 3 * T] = vals[r, 2]
        vfg[r, :, 3 * T :] = last
        vbg[r, :, T : 2 * T] = vals[r, 0].T
        if r > 0:
            vbg[r - 1, :, 2 * T :] = vals[r, 1].T
        else:
            vbd[8] = vals[r, 1].T
        if r < NT - 1:
            vbg[r + 1, :, 0:T] = vals[r, 2].T
        else:
            vbd[9] = vals[r, 2].T
        vbd[r] = last.T
    vbg[0, :, 0:T] = jnp.zeros((T, T), BF)
    vbg[NT - 1, :, 2 * T :] = jnp.zeros((T, T), BF)


def turn_kernel(rin, rout, vin, vout, tin, tout, tfar):
    vin[...] = rin[2:]
    vout[...] = rout[2:]
    for k in range(2):
        lanes = slice(k * T, (k + 1) * T)
        tin[:, lanes] = rin[2, :, lanes].astype(F32).T.astype(BF)
        tout[:, lanes] = rout[2, :, lanes].astype(F32).T.astype(BF)
    tfar[...] = rin[3, :, T:].astype(F32).T.astype(BF)


def middle_forward(pay, got, far, out):
    out[0] = pay[0]
    out[1] = (pay[1].astype(F32) + dot(far[...], got[0])).astype(BF)
    if pay.shape[0] > 2:
        out[2] = pay[2]


def middle_back(pay, got, far, out):
    out[0] = (pay[0].astype(F32) + dot(far[...], got[1])).astype(BF)
    out[1] = pay[1]


def forward_row(place, vfg, src, r):
    low = tile(src, place.idx(0, 1))[...] if r == 0 else tile(src, r)[...]
    high = tile(src, place.idx(7, 2))[...] if r == 7 else tile(src, r + 2)[...]
    picked = jnp.concatenate(
        [low, tile(src, r + 1)[...], high, tile(src, place.idx(r, 3))[...]], axis=0
    )
    return dot(vfg[r], picked)


def spread_kernel(meta, *rest, parts, first):
    sources, rest = rest[:parts], rest[parts:]
    if first:
        rin, rout, vfg, *rest = rest
        vin, vout = rin.at[pl.ds(2, 2)], rout.at[pl.ds(2, 1)]
    else:
        rin, rout, vfg, vin, vout, *rest = rest
    zext, d1, near = rest
    place = Place(meta)
    for k, src in enumerate(sources):
        zext[T : T + ROWS, k * T : (k + 1) * T] = src[...].astype(BF)
    tile(zext, place.pos_in)[...] = rin[0]
    tile(zext, place.pos_out)[...] = rout[0]
    for r in range(NT):
        tile(d1, r + 1)[...] = forward_row(place, vfg, zext, r).astype(BF)
    edge = tile(zext, place.e_in + 1)[...]
    near[...] = rin[1].astype(F32) + dot(vin[0], jnp.concatenate([edge, edge], axis=0))
    tile(d1, place.pos_in)[...] = jnp.zeros_like(edge)
    edge = tile(zext, place.e_out + 1)[...]
    total = rout[1].astype(F32) + dot(vout[0], jnp.concatenate([edge, edge], axis=0))
    tile(d1, place.pos_out)[...] = total.astype(BF)


def spread(meta, sources, got, vfg, boundary):
    shape = ((NT + 2) * T, len(sources) * T)
    args = (meta, *sources, *got[:2], vfg, *boundary)
    return run(
        functools.partial(spread_kernel, parts=len(sources), first=not boundary),
        "spread", (0,), args, [(shape, BF), (shape, BF), ((T, shape[1]), F32)],
    )


def complete(place, given, near, far, rfwd, d1):
    d1[...] = given[...]
    tile(d1, place.pos_in)[...] = (near[...] + dot(far, rfwd[0])).astype(BF)


def second_order(place, vfg, zext, d1, r):
    z = tile(zext, r + 1)[...].astype(F32)
    return (2.0 * forward_row(place, vfg, d1, r) - z).astype(BF)


def gate_kernel(
    meta, st, zext, given, near, rfwd, vin, vfg, e_in, e_out, gw, gb,
    feats, r_out, q_out, pay_in, pay_out, d1, *, first
):
    place = Place(meta)
    complete(place, given, near, vin[3 if first else 1, :, :T], rfwd, d1)
    for r in range(NT):
        d2 = second_order(place, vfg, zext, d1, r)
        z = tile(zext, r + 1)[...]
        one = tile(d1, r + 1)[...]
        row = jnp.concatenate(
            [z[:, T:], one[:, T:], d2[:, T:], z[:, :T], one[:, :T], d2[:, :T]], axis=1
        )
        tile(feats, r)[...] = row
    for h in range(4):
        rows = slice(h * 256, (h + 1) * 256)
        reset = jax.nn.sigmoid(dot(feats[rows], gw[:, :T]) + gb[:, :T])
        r_out[rows] = reset
        q_out[rows] = (reset * st[rows]).astype(BF)
    write_payload(place, q_out, e_in, e_out, pay_in, pay_out, S_LANES)


def update_kernel(feats, gw, gb, cw, cb, u_out, xc_out):
    for h in range(4):
        rows = slice(h * 256, (h + 1) * 256)
        f = feats[rows]
        u_out[rows] = jax.nn.sigmoid(dot(f, gw[:, T:]) + gb[:, T:])
        xc_out[rows] = dot(f[:, : 3 * T], cw[: 3 * T]) + cb[...]


def cand_kernel(
    meta, zext, given, near, rfwd, vin, vfg, e_in, e_out, cw, xc, u, st, *rest, last
):
    if last:
        fq, c_out, d1 = rest
    else:
        x_next, fq, c_out, st_out, pay_in, pay_out, d1 = rest
    place = Place(meta)
    complete(place, given, near, vin[1, :, :T], rfwd, d1)
    for r in range(NT):
        d2 = second_order(place, vfg, zext, d1, r)
        tile(fq, r)[...] = jnp.concatenate(
            [tile(zext, r + 1)[...], tile(d1, r + 1)[...], d2], axis=1
        )
    for h in range(4):
        rows = slice(h * 256, (h + 1) * 256)
        cand = jnp.tanh(dot(fq[rows], cw[3 * T :]) + xc[rows])
        c_out[rows] = cand
        if not last:
            st_out[rows] = u[rows] * st[rows] + (1.0 - u[rows]) * cand
    if not last:
        write_payload(place, st_out, e_in, e_out, pay_in, pay_out, S_LANES)
        write_payload(place, x_next, e_in, e_out, pay_in, pay_out, X_LANES)


def add_received(place, acc, rin, rout, rfwd, et_in, et_out, tfar):
    got_in = dot(et_in[...], rin[1])
    got_out = dot(et_out[...], rout[1])
    for i, block in (
        (place.e_in, got_in[:T] + rin[0].astype(F32) + dot(tfar[...], rfwd[1])),
        (place.n_in, got_in[T : 2 * T]),
        (place.t_in, got_in[2 * T :]),
        (place.e_out, got_out[:T] + rout[0].astype(F32)),
        (place.n_out, got_out[T : 2 * T]),
        (place.t_out, got_out[2 * T :]),
    ):
        tile(acc, i)[...] += block


def back_rows(place, vbg, vbd, y, acc, base):
    zero = jnp.zeros((T, acc.shape[1]), F32)
    tile(acc, 0)[...] = zero
    tile(acc, 9)[...] = zero
    for r in range(NT):
        lo, hi = max(r - 1, 0), min(r + 2, NT)
        lhs = vbg[r, :, (lo - r + 1) * T : (hi - r + 1) * T]
        tile(acc, r + 1)[...] = base(r, dot(lhs, y[lo * T : hi * T]))
    parts = [(place.idx(0, 1), 8, 0), (place.idx(7, 2), 9, 7)]
    parts += [(place.idx(r, 3), r, r) for r in range(NT)]
    for i, k, r in parts:
        tile(acc, i)[...] += dot(vbd[k], y[r * T : (r + 1) * T])


def diffuse_back(place, vbg, vbd, tin, tout, a, y, w, acc, pay_in, pay_out):
    for r in range(NT):
        rows = slice(r * T, (r + 1) * T)
        y[rows] = a(2, rows).astype(BF)
    back_rows(
        place, vbg, vbd, y, acc, lambda r, v: a(1, slice(r * T, (r + 1) * T)) * 0.5 + v
    )
    for e in range(NT + 2):
        tile(w, e)[...] = (2.0 * tile(acc, e)[...]).astype(BF)
    own = w.at[pl.ds(T, ROWS)]

    def second(r, v):
        rows = slice(r * T, (r + 1) * T)
        return a(0, rows) - a(2, rows) + v

    back_rows(place, vbg, vbd, own, acc, second)
    for pos, edge, vals, pay in (
        (place.pos_in, place.e_in, tin, pay_in),
        (place.pos_out, place.e_out, tout, pay_out),
    ):
        part = tile(w, pos)[...]
        tile(acc, edge + 1)[...] += dot(vals[...], jnp.concatenate([part, part], axis=0))
        pay[0] = tile(acc, pos)[...].astype(BF)
        pay[1] = part


def cand_back_kernel(*refs, first):
    refs = list(refs)
    take = lambda n: [refs.pop(0) for _ in range(n)]
    meta, cot, u, c, st, cw, vbg, vbd, tin, tout, et_in, et_out, tfar = take(13)
    if not first:
        gs_part, gx_part, rin, rout, rfwd = take(5)
    gp_out, ec_out, eu_out, gq_out, sums, pay_in, pay_out = take(7)
    if not first:
        (gx_out,) = take(1)
    gs, g, y, w, acc = take(5)
    place = Place(meta)
    if not first:
        gs[:, :T] = gs_part[...]
        gs[:, T:] = gx_part[...]
        add_received(place, gs, rin, rout, rfwd, et_in, et_out, tfar)
        gx_out[...] = gs[:, T:].astype(BF)
    sum_c = jnp.zeros((1, T), F32)
    sum_u = jnp.zeros((1, T), F32)
    for h in range(NT):
        rows = slice(h * T, (h + 1) * T)
        grad = cot[rows].astype(F32)
        if not first:
            grad = grad + gs[rows, :T]
        upd, cand = u[rows], c[rows]
        pre = grad * (1.0 - upd) * (1.0 - cand * cand)
        gate = grad * (st[rows] - cand) * upd * (1.0 - upd)
        gp_out[rows] = grad * upd
        ec_out[rows] = pre.astype(BF)
        eu_out[rows] = gate.astype(BF)
        sum_c = sum_c + jnp.sum(pre, axis=0, keepdims=True)
        sum_u = sum_u + jnp.sum(gate, axis=0, keepdims=True)
    sums[...] = jnp.broadcast_to(jnp.concatenate([sum_c, sum_u], axis=1), (8, 2 * T))
    g[...] = dot_nt(ec_out[...], cw[3 * T :])
    diffuse_back(
        place, vbg, vbd, tin, tout,
        lambda k, rows: g[rows, k * T : (k + 1) * T],
        y, w, acc, pay_in, pay_out,
    )
    gq_out[...] = acc[T : T + ROWS]


def gate_back_kernel(
    meta, gq_part, rin, rout, rfwd, gp, r_ref, st, ec, eu, gw, cw,
    vbg, vbd, tin, tout, et_in, et_out, tfar,
    gs_out, gx_out, er_out, sums, pay_in, pay_out, gq, eg, gps, g, y, w, acc,
):
    place = Place(meta)
    gq[...] = gq_part[...]
    add_received(place, gq, rin, rout, rfwd, et_in, et_out, tfar)
    sum_r = jnp.zeros((1, T), F32)
    for h in range(NT):
        rows = slice(h * T, (h + 1) * T)
        grad, reset = gq[rows], r_ref[rows]
        gps[rows] = gp[rows] + grad * reset
        pre = grad * st[rows] * reset * (1.0 - reset)
        eg[rows, :T] = pre.astype(BF)
        sum_r = sum_r + jnp.sum(pre, axis=0, keepdims=True)
    eg[:, T:] = eu[...]
    er_out[...] = eg[:, :T]
    sums[...] = jnp.broadcast_to(sum_r, (8, T))
    e = eg[...]
    for k in range(3):
        cols = slice(2 * k * T, (2 * k + 1) * T)
        g[:, cols] = dot_nt(e, gw[(3 + k) * T : (4 + k) * T])
        cols = slice((2 * k + 1) * T, (2 * k + 2) * T)
        g[:, cols] = dot_nt(e, gw[k * T : (k + 1) * T]) + dot_nt(
            ec[...], cw[k * T : (k + 1) * T]
        )
    diffuse_back(
        place, vbg, vbd, tin, tout,
        lambda k, rows: g[rows, 2 * k * T : 2 * (k + 1) * T],
        y, w, acc, pay_in, pay_out,
    )
    gs_out[...] = acc[T : T + ROWS, :T] + gps[...]
    gx_out[...] = acc[T : T + ROWS, T:]


def add_rows(out, value, rest, rows):
    out[rows] = value + rest[0][rows] if rest else value


def split_columns(meta, total, kept, sent):
    half = total.shape[1] // 2
    mine = meta[32] == 0
    low, high = total[:, :half], total[:, half:]
    kept[...] = jnp.where(mine, low, high)
    sent[...] = jnp.where(mine, high, low).astype(BF)


def weight_cu_kernel(meta, ec, eu, sums, feats, fq, *rest):
    *rest, out = rest
    x = feats[:, : 3 * T]
    both = jnp.concatenate([dot_tn(ec[...], x), dot_tn(ec[...], fq[...])], axis=1)
    add_rows(out, both, rest, slice(0, T))
    add_rows(out, dot_tn(eu[...], feats[...]), rest, slice(T, 2 * T))
    row = jnp.concatenate([sums[...], jnp.zeros((8, 4 * T), F32)], axis=1)
    add_rows(out, jnp.concatenate([row] * 4, axis=0), rest, slice(2 * T, 2 * T + 32))


def weight_cu_last_kernel(meta, ec, eu, sums, feats, fq, before, kept, sent, out):
    weight_cu_kernel(meta, ec, eu, sums, feats, fq, before, out)
    split_columns(meta, out, kept, sent)


def weight_r_kernel(meta, er, sums, feats, *rest):
    *rest, out = rest
    add_rows(out, dot_tn(er[...], feats[...]), rest, slice(0, T))
    row = jnp.concatenate([sums[...], jnp.zeros((8, 5 * T), F32)], axis=1)
    add_rows(out, jnp.concatenate([row, row], axis=0), rest, slice(T, T + 16))


def weight_r_last_kernel(meta, er, sums, feats, before, kept, sent, out):
    weight_r_kernel(meta, er, sums, feats, before, out)
    split_columns(meta, out, kept, sent)


def add_kernel(a, b, out):
    out[...] = (a[...].astype(F32) + b[...].astype(F32)).astype(BF)


def add_split_kernel(meta, a, b, kept, sent):
    total = (a[...].astype(F32) + b[...].astype(F32)).astype(BF)
    half = total.shape[0] // 2
    upper = meta[33] == 1
    top, bottom = total[:half].astype(F32), total[half:].astype(F32)
    kept[...] = jnp.where(upper, bottom, top).astype(BF)
    sent[...] = jnp.where(upper, top, bottom).astype(BF)


def sum_of(a, b):
    return run(add_kernel, "add", (), (a, b), [(a.shape, BF)])[0]


def reduce_step(part, step):
    count = lax.axis_size("wide")
    other = lax.ppermute(part, "wide", [(i, i ^ step) for i in range(count)])
    return sum_of(part, other)


def reduce_rows(kept, sent):
    count = lax.axis_size("wide")
    route = [(i, i ^ 2) for i in range(count)]
    part = sum_of(kept, lax.ppermute(sent, "wide", route))
    step = 4
    while step < count:
        part = reduce_step(part, step)
        step *= 2
    return part, lax.ppermute(part, "wide", route)


def reduce_rest(part, step):
    while step < lax.axis_size("wide"):
        part = reduce_step(part, step)
        step *= 2
    return part, swap_in(part)


def weights_kernel(
    meta, cu_a, cu_b, cu_a_other, cu_b_other, r_own, r_other, gw, gb, cw, cb, *, scale
):
    mine = meta[32] == 0
    upper = meta[33] == 1

    def pick(own, other, side):
        a, b = own[...].astype(F32), other[...].astype(F32)
        return jnp.where(mine, a, b) if side == 0 else jnp.where(mine, b, a)

    def rows_of(a, b):
        low, high = jnp.where(upper, b, a), jnp.where(upper, a, b)
        return jnp.concatenate([low, high], axis=0)

    for side in range(2):
        cu = rows_of(pick(cu_a, cu_a_other, side), pick(cu_b, cu_b_other, side)) * scale
        r = pick(r_own, r_other, side) * scale
        for k in range(3):
            cols = slice(k * T, (k + 1) * T)
            rows = slice((3 * side + k) * T, (3 * side + k + 1) * T)
            cw[rows] = cu[:T, cols].T
            gw[rows, T:] = cu[T : 2 * T, cols].T
            gw[rows, :T] = r[:T, cols].T
        if side == 0:
            cb[...] = cu[2 * T : 2 * T + 1, :T]
            gb[:, T:] = cu[2 * T : 2 * T + 1, T : 2 * T]
            gb[:, :T] = r[T : T + 1, :T]


def finish_kernel(
    meta, order, gs_part, gx_part, rin, rout, rfwd, et_in, et_out, tfar, gx1, gx2,
    gi_out, gs_out, gs, parts,
):
    place = Place(meta)
    gs[:, :T] = gs_part[...]
    gs[:, T:] = gx_part[...]
    add_received(place, gs, rin, rout, rfwd, et_in, et_out, tfar)
    split_f32(gs[:, :T], parts, 0)
    parts[:, 3 * T : 4 * T] = gs[:, T:].astype(BF)
    parts[:, 4 * T : 5 * T] = gx1[...]
    parts[:, 5 * T :] = gx2[...]
    row = lax.broadcasted_iota(jnp.int32, (T, T), 0)
    for k in range(NT):
        put = jnp.concatenate(
            [
                (jnp.broadcast_to(order[j : j + 1, :], (T, T)) == row + k * T)
                .astype(F32)
                .astype(BF)
                for j in range(NT)
            ],
            axis=1,
        )
        rows = slice(k * T, (k + 1) * T)
        got = dot(put, parts[...])
        gs_out[rows] = got[:, :T] + got[:, T : 2 * T] + got[:, 2 * T : 3 * T]
        for t in range(3):
            gi_out[t, rows] = got[:, (3 + t) * T : (4 + t) * T].astype(BF)


SMEM = pl.BlockSpec(memory_space=pltpu.SMEM)
VMEM = pl.BlockSpec(memory_space=pltpu.VMEM)


HBM = pl.BlockSpec(memory_space=pltpu.HBM)


def run(
    kernel, name, smem, args, outs, scratch=(), specs=None, flops=10**8,
    hbm=(), smem_outs=(), sems=0,
):
    grid = (1,) if specs else ()
    specs = specs or [
        SMEM if i in smem else HBM if i in hbm else VMEM for i in range(len(args))
    ]
    out_shape = [jax.ShapeDtypeStruct(s, d) for s, d in outs]
    args = [
        pltpu.with_memory_space_constraint(x, pltpu.HBM) if i in hbm else x
        for i, x in enumerate(args)
    ]
    moved = sum(math.prod(x.shape) * x.dtype.itemsize for x in (*args, *out_shape))
    return pl.pallas_call(
        kernel,
        name=name,
        grid=grid,
        in_specs=specs,
        out_specs=[SMEM if i in smem_outs else VMEM for i in range(len(outs))],
        out_shape=out_shape,
        scratch_shapes=[pltpu.VMEM(*s) if isinstance(s, tuple) else s for s in scratch]
        + ([pltpu.SemaphoreType.DMA((sems,))] if sems else []),
        cost_estimate=pl.CostEstimate(flops=flops, bytes_accessed=moved, transcendentals=0),
        compiler_params=pltpu.CompilerParams(vmem_limit_bytes=VMEM_LIMIT),
    )(*args)


def leading(block, at):
    zeros = (0,) * (len(block) - 1)
    return pl.BlockSpec(block, lambda i: (at,) + zeros, memory_space=pltpu.VMEM)


def per_device(
    inputs, state_init, cotangent, gate_w, gate_b, cand_w, cand_b,
    tile_vals, tile_cols, tile_counts, sector_order,
):
    order = sector_order.reshape(NT, T)
    gb = gate_b.reshape(1, -1)
    cb = cand_b.reshape(1, -1)
    big = (ROWS, T)
    square = (T, T)
    flat, tall = ((T, 3 * T), BF), ((3 * T, T), BF)
    x_block = (1, ROWS, T)
    device = lax.axis_index("wide").astype(jnp.int32).reshape(1)
    meta, e_in, e_out, et_in, et_out, f_out, ft_in, x0, st, *pay = run(
        start_kernel, "start", (0,),
        (device, tile_cols.T, tile_counts, tile_vals, order, inputs, state_init),
        [((COUNTS + NT,), jnp.int32), flat, flat, tall, tall, (square, BF), (square, BF)]
        + [(big, BF), (big, F32), ((4, T, 2 * T), BF), ((3, T, 2 * T), BF)],
        [
            pltpu.SMEM((4, NT), jnp.int32), pltpu.SMEM((NT,), jnp.int32),
            ((4, T, T), BF), ((4, T, T), BF), ((NT, T), jnp.int32), (big, BF), (big, F32),
            ((ROWS, ROWS), BF), ((ROWS, 4 * T), BF),
        ],
        hbm=(1, 2, 3, 4, 5, 6), sems=7, smem_outs=(0,), flops=10**9,
    )
    vfg, vbg, vbd = run(
        operator_kernel, "operator", (0,), (meta, tile_vals),
        [((NT, T, 4 * T), BF), ((NT, T, 3 * T), BF), ((NT + 2, T, T), BF)],
    )
    x1, x2, *cots = run(
        rest_kernel, "rest", (), (order, inputs, inputs, cotangent), [(big, BF)] * 5,
        [((ROWS, ROWS), BF), ((ROWS, 5 * T), BF)],
        specs=[VMEM, leading(x_block, 1), leading(x_block, 2), VMEM],
        flops=10**9,
    )
    saved = []
    steps = inputs.shape[0]
    wide = ((NT + 2) * T, 2 * T)
    slim = ((NT + 2) * T, T)
    beside = (vfg, vbg, vbd)
    for t in range(steps):
        last = t == steps - 1
        got, beside = exchange(*pay, f_out, middle_forward, beside)
        if t == 0:
            vfg, vbg, vbd = beside
            turned = run(
                turn_kernel, "turn", (), got[:2],
                [((2, T, 2 * T), BF), ((1, T, 2 * T), BF)] + [((T, 2 * T), BF)] * 2
                + [(square, BF)],
            )
            xs = (x0,)
        boundary = () if t == 0 else (vin, vout)
        terms = spread(meta, (st, xs[t]), got, vfg, boundary)
        feats, r, q, *pay = run(
            functools.partial(gate_kernel, first=t == 0),
            "gate",
            (0,),
            (meta, st, *terms, got[2], got[0] if t == 0 else vin, vfg, e_in, e_out, gate_w, gb),
            [((ROWS, 6 * T), BF), (big, F32), (big, BF)] + [((2, T, T), BF)] * 2,
            [(wide, BF)],
        )
        beside = tuple(run(
            update_kernel,
            "update",
            (),
            (feats, gate_w, gb, cand_w, cb),
            [(big, F32)] * 2,
            flops=5 * 10**8,
        ))
        if t == 0:
            beside += (x1, x2, *cots, *turned)
        got, (u, xc, *beside) = exchange(*pay, f_out, middle_forward, beside)
        if t == 0:
            xs += tuple(beside[:2])
            cots = beside[2:5]
            vin, vout, tin, tout, tfar = beside[5:]
        terms = spread(meta, (q,), got, vfg, (vin, vout))
        fq, c, *rest = run(
            functools.partial(cand_kernel, last=last),
            "cand",
            (0,),
            (meta, *terms, got[2], vin, vfg, e_in, e_out, cand_w, xc, u, st) + (() if last else (xs[t + 1],)),
            [((ROWS, 3 * T), BF), (big, F32)]
            + ([] if last else [(big, F32)] + [((2, T, 2 * T), BF)] * 2),
            [(slim, BF)],
        )
        saved.append((st, r, u, c, feats, fq))
        if not last:
            st, *pay = rest
            beside = ()
    ops = (vbg, vbd, tin, tout, et_in, et_out, tfar)
    gxs = [None] * steps
    carry, cu_sum, r_sum = (), (), ()
    for t in reversed(range(steps)):
        st, r, u, c, feats, fq = saved[t]
        first = t == steps - 1
        gp, ec, eu, gq, sums, *rest = run(
            functools.partial(cand_back_kernel, first=first),
            "cand_back",
            (0,),
            (meta, cots[t], u, c, st, cand_w) + ops + carry,
            [(big, F32), (big, BF), (big, BF), (big, F32), ((8, 2 * T), F32)]
            + [((2, T, T), BF)] * 2
            + ([] if first else [(big, BF)]),
            [((ROWS, 2 * T), F32), ((ROWS, 3 * T), F32), (big, BF), (slim, BF), (slim, F32)],
        )
        if not first:
            gxs[t + 1] = rest[2]
        last = t == 0
        rows, columns = 2 * T + 32, 6 * T
        args = (meta, ec, eu, sums, feats, fq, *cu_sum)
        if not last:
            cu_sum = run(
                weight_cu_kernel, "weight_cu", (0,), args, [((rows, columns), F32)],
                flops=4 * 10**8,
            )
        else:
            kept, sent = run(
                weight_cu_last_kernel, "weight_cu", (0,), args,
                [((rows, columns // 2), F32), ((rows, columns // 2), BF)],
                [((rows, columns), F32)], flops=4 * 10**8,
            )
            cu_sum = run(
                add_split_kernel, "add_split", (0,), (meta, kept, swap_in(sent)),
                [((rows // 2, columns // 2), BF)] * 2,
            )
        got, cu_sum = exchange(*rest[:2], ft_in, middle_back, cu_sum)
        gs_part, gx_part, er, sums, *rest = run(
            gate_back_kernel,
            "gate_back",
            (0,),
            (meta, gq, *got, gp, r, st, ec, eu, gate_w, cand_w) + ops,
            [(big, F32), (big, F32), (big, BF), ((8, T), F32)] + [((2, T, 2 * T), BF)] * 2,
            [
                (big, F32), ((ROWS, 2 * T), BF), (big, F32), ((ROWS, 6 * T), F32),
                ((ROWS, 2 * T), BF), (wide, BF), (wide, F32),
            ],
        )
        args = (meta, er, sums, feats, *r_sum)
        rows = T + 16
        if not last:
            r_sum = run(
                weight_r_kernel, "weight_r", (0,), args, [((rows, columns), F32)],
                flops=2 * 10**8,
            )
            got, r_sum = exchange(*rest, ft_in, middle_back, r_sum)
        else:
            kept, sent = run(
                weight_r_last_kernel, "weight_r", (0,), args,
                [((rows, columns // 2), F32), ((rows, columns // 2), BF)],
                [((rows, columns), F32)], flops=2 * 10**8,
            )
            r_part = sum_of(kept, swap_in(sent))
            got, _ = exchange(*rest, ft_in, middle_back)
        carry = (gs_part, gx_part, *got)
    cu = reduce_rows(*cu_sum)
    rr = reduce_rest(r_part, 2)
    gi, gs = run(
        finish_kernel,
        "finish",
        (0,),
        (meta, order, *carry, et_in, et_out, tfar, gxs[1], gxs[2]),
        [((steps,) + big, BF), (big, F32)],
        [((ROWS, 2 * T), F32), ((ROWS, 6 * T), BF)],
    )
    gi, gs, cu = lax.optimization_barrier((gi, gs, cu))
    cu = (*cu, *[swap_in(x) for x in cu])
    scale = 1.0 / math.sqrt(ROWS * lax.axis_size("wide") * steps)
    gw, gb, cw, cb = run(
        functools.partial(weights_kernel, scale=scale),
        "weights",
        (0,),
        (meta, *cu, *rr),
        [((6 * T, 2 * T), F32), ((1, 2 * T), F32), ((6 * T, T), F32), ((1, T), F32)],
    )
    return gi, gs, gw, gb.reshape(-1), cw, cb.reshape(-1)


def solution(mesh):
    return jax.shard_map(
        per_device,
        mesh=mesh,
        in_specs=(
            P(None, ("parts", "wide"), None),
            P(("parts", "wide"), None),
            P(None, ("parts", "wide"), None),
            P(),
            P(),
            P(),
            P(),
            P(("parts", "wide"), None, None, None),
            P(("parts", "wide"), None),
            P(("parts", "wide")),
            P(("parts", "wide")),
        ),
        out_specs=(
            P(None, ("parts", "wide"), None),
            P(("parts", "wide"), None),
            P("parts", None),
            P("parts"),
            P("parts", None),
            P("parts"),
        ),
        check_vma=False,
    )
```

```python
import functools
import math

import jax
import jax.numpy as jnp
from jax import lax
from jax.experimental import pallas as pl
from jax.experimental.pallas import tpu as pltpu
from jax.sharding import PartitionSpec as P

BF = jnp.bfloat16
F32 = jnp.float32
T = 128
NT = 8
ROWS = NT * T
COUNTS = 34
VMEM_LIMIT = 14 * 1024 * 1024


def swap(block, start):
    count = lax.axis_size("wide")
    return lax.ppermute(
        block, "wide", [p for i in range(start, count - 1, 2) for p in ((i, i + 1), (i + 1, i))]
    )


def swap_in(block):
    return swap(block, 0)


def swap_out(block):
    return swap(block, 1)


def exchange(pay_in, pay_out, far, middle, beside=()):
    got_in = swap_in(pay_in)
    (ready,) = run(middle, "middle", (), (pay_out, got_in, far), [(pay_out.shape, BF)])
    got_out = swap_out(ready)
    got_out, beside = lax.optimization_barrier((got_out, tuple(beside)))
    return (got_in, got_out, swap_in(got_out)), beside


def dot(a, b):
    return jnp.dot(a, b, preferred_element_type=F32)


def dot_nt(a, b):
    return lax.dot_general(a, b, (((1,), (1,)), ((), ())), preferred_element_type=F32)


def dot_tn(a, b):
    return lax.dot_general(a, b, (((0,), (0,)), ((), ())), preferred_element_type=F32)


def tile(ref, i):
    start = i * T if isinstance(i, int) else pl.multiple_of(i * T, T)
    return ref.at[pl.ds(start, T)]


class Place:
    def __init__(self, meta):
        self.idx = lambda r, s: meta[4 * r + s]
        core = meta[32]
        self.core = core
        self.e_in = 7 - 7 * core
        self.n_in = 6 - 5 * core
        self.e_out = 7 * core
        self.n_out = 1 + 5 * core
        self.pos_in = 9 - 9 * core
        self.pos_out = 9 * core
        self.col_in = jnp.where(core == 0, meta[4 * 7 + 3], meta[3])
        self.col_out = jnp.where(core == 0, meta[3], meta[4 * 7 + 3])
        self.t_in = jnp.clip(self.col_in - 1, 0, NT - 1)
        self.t_out = jnp.clip(self.col_out - 1, 0, NT - 1)


def copies(sems, *pairs):
    started = [pltpu.make_async_copy(a, b, sems.at[k]) for k, (a, b) in enumerate(pairs)]
    for copy in started:
        copy.start()

    def wait():
        for copy in started:
            copy.wait()

    return wait


def start_kernel(
    device, cols_hbm, counts_hbm, vals_hbm, order_hbm, inputs_hbm, state_hbm,
    meta, e_in, e_out, et_in, et_out, f_out, ft_in, x0, st, pay_in, pay_out,
    cols, counts, first, last, order, given, state, pick, parts, sems,
):
    small = copies(sems.at[pl.ds(0, 2)], (cols_hbm, cols), (counts_hbm, counts))
    wait_order = copies(sems.at[pl.ds(2, 1)], (order_hbm, order))
    wait_rows = copies(
        sems.at[pl.ds(3, 2)], (inputs_hbm.at[0], given), (state_hbm, state)
    )
    wait_vals = copies(
        sems.at[pl.ds(5, 2)], (vals_hbm.at[0], first), (vals_hbm.at[NT - 1], last)
    )
    wait_order()
    pick_rows(order, pick)
    small()
    for r in range(NT):
        for k in range(4):
            meta[4 * r + k] = cols[k, r] - (device[0] * NT - 1)
        meta[COUNTS + r] = counts[r]
    meta[32] = lax.rem(device[0], 2)
    meta[33] = lax.rem(lax.div(device[0], 2), 2)
    place = Place(meta)
    wait_rows()
    split_f32(state[...], parts, 0)
    parts[:, 3 * T :] = given[...]
    for h in range(4):
        rows = slice(h * 256, (h + 1) * 256)
        got = dot(pick[rows], parts[...])
        st[rows] = got[:, :T] + got[:, T : 2 * T] + got[:, 2 * T : 3 * T]
        x0[rows] = got[:, 3 * T :].astype(BF)
    wait_vals()
    edge_tiles(place, meta, first, last, e_in, e_out, et_in, et_out, f_out, ft_in, pay_in, pay_out)
    write_payload(place, st, e_in, e_out, pay_in, pay_out, S_LANES)
    write_payload(place, x0, e_in, e_out, pay_in, pay_out, X_LANES)


def edge_tiles(place, meta, first, last, e_in, e_out, et_in, et_out, f_out, ft_in, pay_in, pay_out):
    zero = place.core == 0
    for low, side_row, row_far, them, far in (
        (False, place.e_in, place.col_in, place.pos_in, place.pos_out),
        (True, place.e_out, place.col_out, place.pos_out, place.pos_in),
    ):
        top = zero if low else jnp.logical_not(zero)
        vals = [jnp.where(top, first[k].astype(F32), last[k].astype(F32)) for k in range(4)]
        inside = jnp.where(top, vals[2], vals[1])
        ahead = jnp.where(top, vals[1], vals[2])
        live = meta[COUNTS + side_row] > 3

        def third(flag):
            return vals[3] * jnp.where(jnp.logical_and(live, flag), 1.0, 0.0)

        is_them, is_far = row_far == them, row_far == far
        own = third(jnp.logical_not(jnp.logical_or(is_them, is_far)))
        e_ref, et_ref = (e_out, et_out) if low else (e_in, et_in)
        for k, v in enumerate((vals[0], inside, own)):
            e_ref[:, k * T : (k + 1) * T] = v.astype(BF)
            et_ref[k * T : (k + 1) * T] = v.T.astype(BF)
        pay = pay_out if low else pay_in
        pay[2, :, :T] = ahead.astype(BF)
        pay[2, :, T:] = third(is_them).astype(BF)
        if low:
            f_out[...] = third(is_far).astype(BF)
            pay_in[3, :, T:] = third(is_far).astype(BF)
        else:
            pay_in[3, :, :T] = third(is_far).astype(BF)
            ft_in[...] = third(is_far).T.astype(BF)


def pick_rows(order, pick):
    lane = lax.broadcasted_iota(jnp.int32, (T, T), 1).astype(F32)
    for j in range(NT):
        wanted = jnp.broadcast_to(order[j : j + 1, :].astype(F32), (T, T)).T
        for k in range(NT):
            pick[j * T : (j + 1) * T, k * T : (k + 1) * T] = (
                (wanted == lane + float(k * T)).astype(F32).astype(BF)
            )


def split_f32(value, ref, start):
    for k in range(3):
        part = value.astype(BF)
        ref[:, start + k * T : start + (k + 1) * T] = part
        value = value - part.astype(F32)


def write_payload(place, own, e_in, e_out, pay_in, pay_out, lanes):
    for e_ref, pay, tiles in (
        (e_in, pay_in, (place.e_in, place.n_in, place.t_in)),
        (e_out, pay_out, (place.e_out, place.n_out, place.t_out)),
    ):
        picked = [tile(own, i)[...].astype(BF) for i in tiles]
        pay[0, :, lanes] = picked[0]
        pay[1, :, lanes] = dot(e_ref[...], jnp.concatenate(picked, axis=0)).astype(BF)


S_LANES, X_LANES = slice(0, T), slice(T, 2 * T)


def rest_kernel(order, in1, in2, cot, x1, x2, c0, c1, c2, pick, parts):
    pick_rows(order, pick)
    for k, src in enumerate((in1[0], in2[0], cot[0], cot[1], cot[2])):
        parts[:, k * T : (k + 1) * T] = src
    for h in range(4):
        rows = slice(h * 256, (h + 1) * 256)
        got = dot(pick[rows], parts[...]).astype(BF)
        for k, out in enumerate((x1, x2, c0, c1, c2)):
            out[rows] = got[:, k * T : (k + 1) * T]


def operator_kernel(meta, vals, vfg, vbg, vbd):
    for r in range(NT):
        live = jnp.where(meta[COUNTS + r] > 3, 1.0, 0.0)
        last = (vals[r, 3].astype(F32) * live).astype(BF)
        vfg[r, :, 0:T] = vals[r, 1]
        vfg[r, :, T : 2 * T] = vals[r, 0]
        vfg[r, :, 2 * T : 3 * T] = vals[r, 2]
        vfg[r, :, 3 * T :] = last
        vbg[r, :, T : 2 * T] = vals[r, 0].T
        if r > 0:
            vbg[r - 1, :, 2 * T :] = vals[r, 1].T
        else:
            vbd[8] = vals[r, 1].T
        if r < NT - 1:
            vbg[r + 1, :, 0:T] = vals[r, 2].T
        else:
            vbd[9] = vals[r, 2].T
        vbd[r] = last.T
    vbg[0, :, 0:T] = jnp.zeros((T, T), BF)
    vbg[NT - 1, :, 2 * T :] = jnp.zeros((T, T), BF)


def turn_kernel(rin, rout, vin, vout, tin, tout, tfar):
    vin[...] = rin[2:]
    vout[...] = rout[2:]
    for k in range(2):
        lanes = slice(k * T, (k + 1) * T)
        tin[:, lanes] = rin[2, :, lanes].astype(F32).T.astype(BF)
        tout[:, lanes] = rout[2, :, lanes].astype(F32).T.astype(BF)
    tfar[...] = rin[3, :, T:].astype(F32).T.astype(BF)


def middle_forward(pay, got, far, out):
    out[0] = pay[0]
    out[1] = (pay[1].astype(F32) + dot(far[...], got[0])).astype(BF)
    if pay.shape[0] > 2:
        out[2] = pay[2]


def middle_back(pay, got, far, out):
    out[0] = (pay[0].astype(F32) + dot(far[...], got[1])).astype(BF)
    out[1] = pay[1]


def forward_row(place, vfg, src, r):
    low = tile(src, place.idx(0, 1))[...] if r == 0 else tile(src, r)[...]
    high = tile(src, place.idx(7, 2))[...] if r == 7 else tile(src, r + 2)[...]
    picked = jnp.concatenate(
        [low, tile(src, r + 1)[...], high, tile(src, place.idx(r, 3))[...]], axis=0
    )
    return dot(vfg[r], picked)


def spread_kernel(meta, *rest, parts, first):
    sources, rest = rest[:parts], rest[parts:]
    if first:
        rin, rout, vfg, *rest = rest
        vin, vout = rin.at[pl.ds(2, 2)], rout.at[pl.ds(2, 1)]
    else:
        rin, rout, vfg, vin, vout, *rest = rest
    zext, d1, near = rest
    place = Place(meta)
    for k, src in enumerate(sources):
        zext[T : T + ROWS, k * T : (k + 1) * T] = src[...].astype(BF)
    tile(zext, place.pos_in)[...] = rin[0]
    tile(zext, place.pos_out)[...] = rout[0]
    for r in range(NT):
        tile(d1, r + 1)[...] = forward_row(place, vfg, zext, r).astype(BF)
    edge = tile(zext, place.e_in + 1)[...]
    near[...] = rin[1].astype(F32) + dot(vin[0], jnp.concatenate([edge, edge], axis=0))
    tile(d1, place.pos_in)[...] = jnp.zeros_like(edge)
    edge = tile(zext, place.e_out + 1)[...]
    total = rout[1].astype(F32) + dot(vout[0], jnp.concatenate([edge, edge], axis=0))
    tile(d1, place.pos_out)[...] = total.astype(BF)


def spread(meta, sources, got, vfg, boundary):
    shape = ((NT + 2) * T, len(sources) * T)
    args = (meta, *sources, *got[:2], vfg, *boundary)
    return run(
        functools.partial(spread_kernel, parts=len(sources), first=not boundary),
        "spread", (0,), args, [(shape, BF), (shape, BF), ((T, shape[1]), F32)],
    )


def complete(place, given, near, far, rfwd, d1):
    d1[...] = given[...]
    tile(d1, place.pos_in)[...] = (near[...] + dot(far, rfwd[0])).astype(BF)


def second_order(place, vfg, zext, d1, r):
    z = tile(zext, r + 1)[...].astype(F32)
    return (2.0 * forward_row(place, vfg, d1, r) - z).astype(BF)


def gate_kernel(
    meta, st, zext, given, near, rfwd, vin, vfg, e_in, e_out, gw, gb,
    feats, r_out, q_out, pay_in, pay_out, d1, *, first
):
    place = Place(meta)
    complete(place, given, near, vin[3 if first else 1, :, :T], rfwd, d1)
    for r in range(NT):
        d2 = second_order(place, vfg, zext, d1, r)
        z = tile(zext, r + 1)[...]
        one = tile(d1, r + 1)[...]
        row = jnp.concatenate(
            [z[:, T:], one[:, T:], d2[:, T:], z[:, :T], one[:, :T], d2[:, :T]], axis=1
        )
        tile(feats, r)[...] = row
    for h in range(4):
        rows = slice(h * 256, (h + 1) * 256)
        reset = jax.nn.sigmoid(dot(feats[rows], gw[:, :T]) + gb[:, :T])
        r_out[rows] = reset
        q_out[rows] = (reset * st[rows]).astype(BF)
    write_payload(place, q_out, e_in, e_out, pay_in, pay_out, S_LANES)


def update_kernel(feats, gw, gb, cw, cb, u_out, xc_out):
    for h in range(4):
        rows = slice(h * 256, (h + 1) * 256)
        f = feats[rows]
        u_out[rows] = jax.nn.sigmoid(dot(f, gw[:, T:]) + gb[:, T:])
        xc_out[rows] = dot(f[:, : 3 * T], cw[: 3 * T]) + cb[...]


def cand_kernel(
    meta, zext, given, near, rfwd, vin, vfg, e_in, e_out, cw, xc, u, st, *rest, last
):
    if last:
        fq, c_out, d1 = rest
    else:
        x_next, fq, c_out, st_out, pay_in, pay_out, d1 = rest
    place = Place(meta)
    complete(place, given, near, vin[1, :, :T], rfwd, d1)
    for r in range(NT):
        d2 = second_order(place, vfg, zext, d1, r)
        tile(fq, r)[...] = jnp.concatenate(
            [tile(zext, r + 1)[...], tile(d1, r + 1)[...], d2], axis=1
        )
    for h in range(4):
        rows = slice(h * 256, (h + 1) * 256)
        cand = jnp.tanh(dot(fq[rows], cw[3 * T :]) + xc[rows])
        c_out[rows] = cand
        if not last:
            st_out[rows] = u[rows] * st[rows] + (1.0 - u[rows]) * cand
    if not last:
        write_payload(place, st_out, e_in, e_out, pay_in, pay_out, S_LANES)
        write_payload(place, x_next, e_in, e_out, pay_in, pay_out, X_LANES)


def collect_kernel(meta, *rest, parts):
    sources, (rin, rout, et_in, et_out, acc) = rest[:parts], rest[parts:]
    place = Place(meta)
    for k, src in enumerate(sources):
        acc[:, k * T : (k + 1) * T] = src[...]
    got_in = dot(et_in[...], rin[1])
    got_out = dot(et_out[...], rout[1])
    for i, block in (
        (place.e_in, got_in[:T] + rin[0].astype(F32)),
        (place.n_in, got_in[T : 2 * T]),
        (place.t_in, got_in[2 * T :]),
        (place.e_out, got_out[:T] + rout[0].astype(F32)),
        (place.n_out, got_out[T : 2 * T]),
        (place.t_out, got_out[2 * T :]),
    ):
        tile(acc, i)[...] += block


def collect(meta, sources, got, et_in, et_out):
    return run(
        functools.partial(collect_kernel, parts=len(sources)), "collect", (0,),
        (meta, *sources, *got[:2], et_in, et_out), [((ROWS, len(sources) * T), F32)],
    )[0]


def add_far(place, acc, given, rfwd, tfar):
    acc[...] = given[...]
    tile(acc, place.e_in)[...] += dot(tfar[...], rfwd[1])


def back_rows(place, vbg, vbd, y, acc, base):
    zero = jnp.zeros((T, acc.shape[1]), F32)
    tile(acc, 0)[...] = zero
    tile(acc, 9)[...] = zero
    for r in range(NT):
        lo, hi = max(r - 1, 0), min(r + 2, NT)
        lhs = vbg[r, :, (lo - r + 1) * T : (hi - r + 1) * T]
        tile(acc, r + 1)[...] = base(r, dot(lhs, y[lo * T : hi * T]))
    parts = [(place.idx(0, 1), 8, 0), (place.idx(7, 2), 9, 7)]
    parts += [(place.idx(r, 3), r, r) for r in range(NT)]
    for i, k, r in parts:
        tile(acc, i)[...] += dot(vbd[k], y[r * T : (r + 1) * T])


def diffuse_back(place, vbg, vbd, tin, tout, a, y, w, acc, pay_in, pay_out):
    for r in range(NT):
        rows = slice(r * T, (r + 1) * T)
        y[rows] = a(2, rows).astype(BF)
    back_rows(
        place, vbg, vbd, y, acc, lambda r, v: a(1, slice(r * T, (r + 1) * T)) * 0.5 + v
    )
    for e in range(NT + 2):
        tile(w, e)[...] = (2.0 * tile(acc, e)[...]).astype(BF)
    own = w.at[pl.ds(T, ROWS)]

    def second(r, v):
        rows = slice(r * T, (r + 1) * T)
        return a(0, rows) - a(2, rows) + v

    back_rows(place, vbg, vbd, own, acc, second)
    for pos, edge, vals, pay in (
        (place.pos_in, place.e_in, tin, pay_in),
        (place.pos_out, place.e_out, tout, pay_out),
    ):
        part = tile(w, pos)[...]
        tile(acc, edge + 1)[...] += dot(vals[...], jnp.concatenate([part, part], axis=0))
        pay[0] = tile(acc, pos)[...].astype(BF)
        pay[1] = part


def cand_back_kernel(*refs, first):
    refs = list(refs)
    take = lambda n: [refs.pop(0) for _ in range(n)]
    meta, cot, u, c, st, cw, vbg, vbd, tin, tout, tfar = take(11)
    if not first:
        given, rfwd = take(2)
    gp_out, ec_out, eu_out, gq_out, sums, pay_in, pay_out = take(7)
    if not first:
        (gx_out,) = take(1)
    gs, g, y, w, acc = take(5)
    place = Place(meta)
    if not first:
        add_far(place, gs, given, rfwd, tfar)
        gx_out[...] = gs[:, T:].astype(BF)
    sum_c = jnp.zeros((1, T), F32)
    sum_u = jnp.zeros((1, T), F32)
    for h in range(NT):
        rows = slice(h * T, (h + 1) * T)
        grad = cot[rows].astype(F32)
        if not first:
            grad = grad + gs[rows, :T]
        upd, cand = u[rows], c[rows]
        pre = grad * (1.0 - upd) * (1.0 - cand * cand)
        gate = grad * (st[rows] - cand) * upd * (1.0 - upd)
        gp_out[rows] = grad * upd
        ec_out[rows] = pre.astype(BF)
        eu_out[rows] = gate.astype(BF)
        sum_c = sum_c + jnp.sum(pre, axis=0, keepdims=True)
        sum_u = sum_u + jnp.sum(gate, axis=0, keepdims=True)
    sums[...] = jnp.broadcast_to(jnp.concatenate([sum_c, sum_u], axis=1), (8, 2 * T))
    g[...] = dot_nt(ec_out[...], cw[3 * T :])
    diffuse_back(
        place, vbg, vbd, tin, tout,
        lambda k, rows: g[rows, k * T : (k + 1) * T],
        y, w, acc, pay_in, pay_out,
    )
    gq_out[...] = acc[T : T + ROWS]


def gate_back_kernel(
    meta, given, rfwd, gp, r_ref, st, ec, eu, gw, cw, vbg, vbd, tin, tout, tfar,
    gs_out, gx_out, er_out, sums, pay_in, pay_out, gq, eg, gps, g, y, w, acc,
):
    place = Place(meta)
    add_far(place, gq, given, rfwd, tfar)
    sum_r = jnp.zeros((1, T), F32)
    for h in range(NT):
        rows = slice(h * T, (h + 1) * T)
        grad, reset = gq[rows], r_ref[rows]
        gps[rows] = gp[rows] + grad * reset
        pre = grad * st[rows] * reset * (1.0 - reset)
        eg[rows, :T] = pre.astype(BF)
        sum_r = sum_r + jnp.sum(pre, axis=0, keepdims=True)
    eg[:, T:] = eu[...]
    er_out[...] = eg[:, :T]
    sums[...] = jnp.broadcast_to(sum_r, (8, T))
    e = eg[...]
    for k in range(3):
        cols = slice(2 * k * T, (2 * k + 1) * T)
        g[:, cols] = dot_nt(e, gw[(3 + k) * T : (4 + k) * T])
        cols = slice((2 * k + 1) * T, (2 * k + 2) * T)
        g[:, cols] = dot_nt(e, gw[k * T : (k + 1) * T]) + dot_nt(
            ec[...], cw[k * T : (k + 1) * T]
        )
    diffuse_back(
        place, vbg, vbd, tin, tout,
        lambda k, rows: g[rows, 2 * k * T : 2 * (k + 1) * T],
        y, w, acc, pay_in, pay_out,
    )
    gs_out[...] = acc[T : T + ROWS, :T] + gps[...]
    gx_out[...] = acc[T : T + ROWS, T:]


def add_rows(out, value, rest, rows):
    out[rows] = value + rest[0][rows] if rest else value


def split_columns(meta, total, kept, sent):
    half = total.shape[1] // 2
    mine = meta[32] == 0
    low, high = total[:, :half], total[:, half:]
    kept[...] = jnp.where(mine, low, high)
    sent[...] = jnp.where(mine, high, low).astype(BF)


def weight_cu_kernel(meta, ec, eu, sums, feats, fq, *rest):
    *rest, out = rest
    x = feats[:, : 3 * T]
    both = jnp.concatenate([dot_tn(ec[...], x), dot_tn(ec[...], fq[...])], axis=1)
    add_rows(out, both, rest, slice(0, T))
    add_rows(out, dot_tn(eu[...], feats[...]), rest, slice(T, 2 * T))
    row = jnp.concatenate([sums[...], jnp.zeros((8, 4 * T), F32)], axis=1)
    add_rows(out, jnp.concatenate([row] * 4, axis=0), rest, slice(2 * T, 2 * T + 32))


def weight_cu_last_kernel(meta, ec, eu, sums, feats, fq, before, kept, sent, out):
    weight_cu_kernel(meta, ec, eu, sums, feats, fq, before, out)
    split_columns(meta, out, kept, sent)


def weight_r_kernel(meta, er, sums, feats, *rest):
    *rest, out = rest
    add_rows(out, dot_tn(er[...], feats[...]), rest, slice(0, T))
    row = jnp.concatenate([sums[...], jnp.zeros((8, 5 * T), F32)], axis=1)
    add_rows(out, jnp.concatenate([row, row], axis=0), rest, slice(T, T + 16))


def weight_r_last_kernel(meta, er, sums, feats, before, kept, sent, out):
    weight_r_kernel(meta, er, sums, feats, before, out)
    split_columns(meta, out, kept, sent)


def add_kernel(a, b, out):
    out[...] = (a[...].astype(F32) + b[...].astype(F32)).astype(BF)


def add_split_kernel(meta, a, b, kept, sent):
    total = (a[...].astype(F32) + b[...].astype(F32)).astype(BF)
    half = total.shape[0] // 2
    upper = meta[33] == 1
    top, bottom = total[:half].astype(F32), total[half:].astype(F32)
    kept[...] = jnp.where(upper, bottom, top).astype(BF)
    sent[...] = jnp.where(upper, top, bottom).astype(BF)


def sum_of(a, b):
    return run(add_kernel, "add", (), (a, b), [(a.shape, BF)])[0]


def reduce_step(part, step):
    count = lax.axis_size("wide")
    other = lax.ppermute(part, "wide", [(i, i ^ step) for i in range(count)])
    return sum_of(part, other)


def reduce_rows(kept, sent):
    count = lax.axis_size("wide")
    route = [(i, i ^ 2) for i in range(count)]
    part = sum_of(kept, lax.ppermute(sent, "wide", route))
    step = 4
    while step < count:
        part = reduce_step(part, step)
        step *= 2
    return part, lax.ppermute(part, "wide", route)


def reduce_rest(part, step):
    while step < lax.axis_size("wide"):
        part = reduce_step(part, step)
        step *= 2
    return part, swap_in(part)


def weights_kernel(
    meta, cu_a, cu_b, cu_a_other, cu_b_other, r_own, r_other, gw, gb, cw, cb, *, scale
):
    mine = meta[32] == 0
    upper = meta[33] == 1

    def pick(own, other, side):
        a, b = own[...].astype(F32), other[...].astype(F32)
        return jnp.where(mine, a, b) if side == 0 else jnp.where(mine, b, a)

    def rows_of(a, b):
        low, high = jnp.where(upper, b, a), jnp.where(upper, a, b)
        return jnp.concatenate([low, high], axis=0)

    for side in range(2):
        cu = rows_of(pick(cu_a, cu_a_other, side), pick(cu_b, cu_b_other, side)) * scale
        r = pick(r_own, r_other, side) * scale
        for k in range(3):
            cols = slice(k * T, (k + 1) * T)
            rows = slice((3 * side + k) * T, (3 * side + k + 1) * T)
            cw[rows] = cu[:T, cols].T
            gw[rows, T:] = cu[T : 2 * T, cols].T
            gw[rows, :T] = r[:T, cols].T
        if side == 0:
            cb[...] = cu[2 * T : 2 * T + 1, :T]
            gb[:, T:] = cu[2 * T : 2 * T + 1, T : 2 * T]
            gb[:, :T] = r[T : T + 1, :T]


def finish_kernel(
    meta, order, given, rfwd, tfar, gx1, gx2,
    gi_out, gs_out, gs, parts,
):
    place = Place(meta)
    add_far(place, gs, given, rfwd, tfar)
    split_f32(gs[:, :T], parts, 0)
    parts[:, 3 * T : 4 * T] = gs[:, T:].astype(BF)
    parts[:, 4 * T : 5 * T] = gx1[...]
    parts[:, 5 * T :] = gx2[...]
    row = lax.broadcasted_iota(jnp.int32, (T, T), 0)
    for k in range(NT):
        put = jnp.concatenate(
            [
                (jnp.broadcast_to(order[j : j + 1, :], (T, T)) == row + k * T)
                .astype(F32)
                .astype(BF)
                for j in range(NT)
            ],
            axis=1,
        )
        rows = slice(k * T, (k + 1) * T)
        got = dot(put, parts[...])
        gs_out[rows] = got[:, :T] + got[:, T : 2 * T] + got[:, 2 * T : 3 * T]
        for t in range(3):
            gi_out[t, rows] = got[:, (3 + t) * T : (4 + t) * T].astype(BF)


SMEM = pl.BlockSpec(memory_space=pltpu.SMEM)
VMEM = pl.BlockSpec(memory_space=pltpu.VMEM)


HBM = pl.BlockSpec(memory_space=pltpu.HBM)


def run(
    kernel, name, smem, args, outs, scratch=(), specs=None, flops=10**8,
    hbm=(), smem_outs=(), sems=0,
):
    grid = (1,) if specs else ()
    specs = specs or [
        SMEM if i in smem else HBM if i in hbm else VMEM for i in range(len(args))
    ]
    out_shape = [jax.ShapeDtypeStruct(s, d) for s, d in outs]
    args = [
        pltpu.with_memory_space_constraint(x, pltpu.HBM) if i in hbm else x
        for i, x in enumerate(args)
    ]
    moved = sum(math.prod(x.shape) * x.dtype.itemsize for x in (*args, *out_shape))
    return pl.pallas_call(
        kernel,
        name=name,
        grid=grid,
        in_specs=specs,
        out_specs=[SMEM if i in smem_outs else VMEM for i in range(len(outs))],
        out_shape=out_shape,
        scratch_shapes=[pltpu.VMEM(*s) if isinstance(s, tuple) else s for s in scratch]
        + ([pltpu.SemaphoreType.DMA((sems,))] if sems else []),
        cost_estimate=pl.CostEstimate(flops=flops, bytes_accessed=moved, transcendentals=0),
        compiler_params=pltpu.CompilerParams(vmem_limit_bytes=VMEM_LIMIT),
    )(*args)


def leading(block, at):
    zeros = (0,) * (len(block) - 1)
    return pl.BlockSpec(block, lambda i: (at,) + zeros, memory_space=pltpu.VMEM)


def per_device(
    inputs, state_init, cotangent, gate_w, gate_b, cand_w, cand_b,
    tile_vals, tile_cols, tile_counts, sector_order,
):
    order = sector_order.reshape(NT, T)
    gb = gate_b.reshape(1, -1)
    cb = cand_b.reshape(1, -1)
    big = (ROWS, T)
    square = (T, T)
    flat, tall = ((T, 3 * T), BF), ((3 * T, T), BF)
    x_block = (1, ROWS, T)
    device = lax.axis_index("wide").astype(jnp.int32).reshape(1)
    meta, e_in, e_out, et_in, et_out, f_out, ft_in, x0, st, *pay = run(
        start_kernel, "start", (0,),
        (device, tile_cols.T, tile_counts, tile_vals, order, inputs, state_init),
        [((COUNTS + NT,), jnp.int32), flat, flat, tall, tall, (square, BF), (square, BF)]
        + [(big, BF), (big, F32), ((4, T, 2 * T), BF), ((3, T, 2 * T), BF)],
        [
            pltpu.SMEM((4, NT), jnp.int32), pltpu.SMEM((NT,), jnp.int32),
            ((4, T, T), BF), ((4, T, T), BF), ((NT, T), jnp.int32), (big, BF), (big, F32),
            ((ROWS, ROWS), BF), ((ROWS, 4 * T), BF),
        ],
        hbm=(1, 2, 3, 4, 5, 6), sems=7, smem_outs=(0,), flops=10**9,
    )
    vfg, vbg, vbd = run(
        operator_kernel, "operator", (0,), (meta, tile_vals),
        [((NT, T, 4 * T), BF), ((NT, T, 3 * T), BF), ((NT + 2, T, T), BF)],
    )
    x1, x2, *cots = run(
        rest_kernel, "rest", (), (order, inputs, inputs, cotangent), [(big, BF)] * 5,
        [((ROWS, ROWS), BF), ((ROWS, 5 * T), BF)],
        specs=[VMEM, leading(x_block, 1), leading(x_block, 2), VMEM],
        flops=10**9,
    )
    saved = []
    steps = inputs.shape[0]
    wide = ((NT + 2) * T, 2 * T)
    slim = ((NT + 2) * T, T)
    beside = (vfg, vbg, vbd)
    for t in range(steps):
        last = t == steps - 1
        got, beside = exchange(*pay, f_out, middle_forward, beside)
        if t == 0:
            vfg, vbg, vbd = beside
            turned = run(
                turn_kernel, "turn", (), got[:2],
                [((2, T, 2 * T), BF), ((1, T, 2 * T), BF)] + [((T, 2 * T), BF)] * 2
                + [(square, BF)],
            )
            xs = (x0,)
        boundary = () if t == 0 else (vin, vout)
        terms = spread(meta, (st, xs[t]), got, vfg, boundary)
        feats, r, q, *pay = run(
            functools.partial(gate_kernel, first=t == 0),
            "gate",
            (0,),
            (meta, st, *terms, got[2], got[0] if t == 0 else vin, vfg, e_in, e_out, gate_w, gb),
            [((ROWS, 6 * T), BF), (big, F32), (big, BF)] + [((2, T, T), BF)] * 2,
            [(wide, BF)],
        )
        beside = tuple(run(
            update_kernel,
            "update",
            (),
            (feats, gate_w, gb, cand_w, cb),
            [(big, F32)] * 2,
            flops=5 * 10**8,
        ))
        if t == 0:
            beside += (x1, x2, *cots, *turned)
        got, (u, xc, *beside) = exchange(*pay, f_out, middle_forward, beside)
        if t == 0:
            xs += tuple(beside[:2])
            cots = beside[2:5]
            vin, vout, tin, tout, tfar = beside[5:]
        terms = spread(meta, (q,), got, vfg, (vin, vout))
        fq, c, *rest = run(
            functools.partial(cand_kernel, last=last),
            "cand",
            (0,),
            (meta, *terms, got[2], vin, vfg, e_in, e_out, cand_w, xc, u, st) + (() if last else (xs[t + 1],)),
            [((ROWS, 3 * T), BF), (big, F32)]
            + ([] if last else [(big, F32)] + [((2, T, 2 * T), BF)] * 2),
            [(slim, BF)],
        )
        saved.append((st, r, u, c, feats, fq))
        if not last:
            st, *pay = rest
            beside = ()
    ops = (vbg, vbd, tin, tout, tfar)
    gxs = [None] * steps
    carry, cu_sum, r_sum = (), (), ()
    for t in reversed(range(steps)):
        st, r, u, c, feats, fq = saved[t]
        first = t == steps - 1
        gp, ec, eu, gq, sums, *rest = run(
            functools.partial(cand_back_kernel, first=first),
            "cand_back",
            (0,),
            (meta, cots[t], u, c, st, cand_w) + ops + carry,
            [(big, F32), (big, BF), (big, BF), (big, F32), ((8, 2 * T), F32)]
            + [((2, T, T), BF)] * 2
            + ([] if first else [(big, BF)]),
            [((ROWS, 2 * T), F32), ((ROWS, 3 * T), F32), (big, BF), (slim, BF), (slim, F32)],
        )
        if not first:
            gxs[t + 1] = rest[2]
        last = t == 0
        rows, columns = 2 * T + 32, 6 * T
        args = (meta, ec, eu, sums, feats, fq, *cu_sum)
        if not last:
            cu_sum = run(
                weight_cu_kernel, "weight_cu", (0,), args, [((rows, columns), F32)],
                flops=4 * 10**8,
            )
        else:
            kept, sent = run(
                weight_cu_last_kernel, "weight_cu", (0,), args,
                [((rows, columns // 2), F32), ((rows, columns // 2), BF)],
                [((rows, columns), F32)], flops=4 * 10**8,
            )
            cu_sum = run(
                add_split_kernel, "add_split", (0,), (meta, kept, swap_in(sent)),
                [((rows // 2, columns // 2), BF)] * 2,
            )
        got, cu_sum = exchange(*rest[:2], ft_in, middle_back, cu_sum)
        gs_part, gx_part, er, sums, *rest = run(
            gate_back_kernel,
            "gate_back",
            (0,),
            (meta, collect(meta, (gq,), got, et_in, et_out), got[2], gp, r, st, ec, eu, gate_w, cand_w) + ops,
            [(big, F32), (big, F32), (big, BF), ((8, T), F32)] + [((2, T, 2 * T), BF)] * 2,
            [
                (big, F32), ((ROWS, 2 * T), BF), (big, F32), ((ROWS, 6 * T), F32),
                ((ROWS, 2 * T), BF), (wide, BF), (wide, F32),
            ],
        )
        args = (meta, er, sums, feats, *r_sum)
        rows = T + 16
        if not last:
            r_sum = run(
                weight_r_kernel, "weight_r", (0,), args, [((rows, columns), F32)],
                flops=2 * 10**8,
            )
            got, r_sum = exchange(*rest, ft_in, middle_back, r_sum)
        else:
            kept, sent = run(
                weight_r_last_kernel, "weight_r", (0,), args,
                [((rows, columns // 2), F32), ((rows, columns // 2), BF)],
                [((rows, columns), F32)], flops=2 * 10**8,
            )
            r_part = sum_of(kept, swap_in(sent))
            got, _ = exchange(*rest, ft_in, middle_back)
        carry = (collect(meta, (gs_part, gx_part), got, et_in, et_out), got[2])
    cu = reduce_rows(*cu_sum)
    rr = reduce_rest(r_part, 2)
    gi, gs = run(
        finish_kernel,
        "finish",
        (0,),
        (meta, order, *carry, tfar, gxs[1], gxs[2]),
        [((steps,) + big, BF), (big, F32)],
        [((ROWS, 2 * T), F32), ((ROWS, 6 * T), BF)],
    )
    gi, gs, cu = lax.optimization_barrier((gi, gs, cu))
    cu = (*cu, *[swap_in(x) for x in cu])
    scale = 1.0 / math.sqrt(ROWS * lax.axis_size("wide") * steps)
    gw, gb, cw, cb = run(
        functools.partial(weights_kernel, scale=scale),
        "weights",
        (0,),
        (meta, *cu, *rr),
        [((6 * T, 2 * T), F32), ((1, 2 * T), F32), ((6 * T, T), F32), ((1, T), F32)],
    )
    return gi, gs, gw, gb.reshape(-1), cw, cb.reshape(-1)


def solution(mesh):
    return jax.shard_map(
        per_device,
        mesh=mesh,
        in_specs=(
            P(None, ("parts", "wide"), None),
            P(("parts", "wide"), None),
            P(None, ("parts", "wide"), None),
            P(),
            P(),
            P(),
            P(),
            P(("parts", "wide"), None, None, None),
            P(("parts", "wide"), None),
            P(("parts", "wide")),
            P(("parts", "wide")),
        ),
        out_specs=(
            P(None, ("parts", "wide"), None),
            P(("parts", "wide"), None),
            P("parts", None),
            P("parts"),
            P("parts", None),
            P("parts"),
        ),
        check_vma=False,
    )
```

```python
import functools
import math

import jax
import jax.numpy as jnp
from jax import lax
from jax.experimental import pallas as pl
from jax.experimental.pallas import tpu as pltpu
from jax.sharding import PartitionSpec as P

BF = jnp.bfloat16
F32 = jnp.float32
T = 128
NT = 8
ROWS = NT * T
COUNTS = 34
VMEM_LIMIT = 14 * 1024 * 1024


def swap(block, start):
    count = lax.axis_size("wide")
    return lax.ppermute(
        block, "wide", [p for i in range(start, count - 1, 2) for p in ((i, i + 1), (i + 1, i))]
    )


def swap_in(block):
    return swap(block, 0)


def swap_out(block):
    return swap(block, 1)


def exchange(pay_in, pay_out, far, middle, beside=()):
    got_in = swap_in(pay_in)
    (ready,) = run(middle, "middle", (), (pay_out, got_in, far), [(pay_out.shape, BF)])
    got_out = swap_out(ready)
    got_out, beside = lax.optimization_barrier((got_out, tuple(beside)))
    return (got_in, got_out, swap_in(got_out)), beside


def dot(a, b):
    return jnp.dot(a, b, preferred_element_type=F32)


def dot_nt(a, b):
    return lax.dot_general(a, b, (((1,), (1,)), ((), ())), preferred_element_type=F32)


def dot_tn(a, b):
    return lax.dot_general(a, b, (((0,), (0,)), ((), ())), preferred_element_type=F32)


def tile(ref, i):
    start = i * T if isinstance(i, int) else pl.multiple_of(i * T, T)
    return ref.at[pl.ds(start, T)]


class Place:
    def __init__(self, meta):
        self.idx = lambda r, s: meta[4 * r + s]
        core = meta[32]
        self.core = core
        self.e_in = 7 - 7 * core
        self.n_in = 6 - 5 * core
        self.e_out = 7 * core
        self.n_out = 1 + 5 * core
        self.pos_in = 9 - 9 * core
        self.pos_out = 9 * core
        self.col_in = jnp.where(core == 0, meta[4 * 7 + 3], meta[3])
        self.col_out = jnp.where(core == 0, meta[3], meta[4 * 7 + 3])
        self.t_in = jnp.clip(self.col_in - 1, 0, NT - 1)
        self.t_out = jnp.clip(self.col_out - 1, 0, NT - 1)


def copies(sems, *pairs):
    started = [pltpu.make_async_copy(a, b, sems.at[k]) for k, (a, b) in enumerate(pairs)]
    for copy in started:
        copy.start()

    def wait():
        for copy in started:
            copy.wait()

    return wait


def start_kernel(
    device, cols_hbm, counts_hbm, vals_hbm, order_hbm, inputs_hbm, state_hbm,
    meta, e_in, e_out, et_in, et_out, f_out, ft_in, x0, st, pay_in, pay_out,
    cols, counts, first, last, order, given, state, pick, parts, sems,
):
    small = copies(sems.at[pl.ds(0, 2)], (cols_hbm, cols), (counts_hbm, counts))
    wait_order = copies(sems.at[pl.ds(2, 1)], (order_hbm, order))
    wait_rows = copies(
        sems.at[pl.ds(3, 2)], (inputs_hbm.at[0], given), (state_hbm, state)
    )
    wait_vals = copies(
        sems.at[pl.ds(5, 2)], (vals_hbm.at[0], first), (vals_hbm.at[NT - 1], last)
    )
    wait_order()
    pick_rows(order, pick)
    small()
    for r in range(NT):
        for k in range(4):
            meta[4 * r + k] = cols[k, r] - (device[0] * NT - 1)
        meta[COUNTS + r] = counts[r]
    meta[32] = lax.rem(device[0], 2)
    meta[33] = lax.rem(lax.div(device[0], 2), 2)
    place = Place(meta)
    wait_rows()
    split_f32(state[...], parts, 0)
    parts[:, 3 * T :] = given[...]
    for h in range(4):
        rows = slice(h * 256, (h + 1) * 256)
        got = dot(pick[rows], parts[...])
        st[rows] = got[:, :T] + got[:, T : 2 * T] + got[:, 2 * T : 3 * T]
        x0[rows] = got[:, 3 * T :].astype(BF)
    wait_vals()
    edge_tiles(place, meta, first, last, e_in, e_out, et_in, et_out, f_out, ft_in, pay_in, pay_out)
    write_payload(place, st, e_in, e_out, pay_in, pay_out, S_LANES)
    write_payload(place, x0, e_in, e_out, pay_in, pay_out, X_LANES)


def edge_tiles(place, meta, first, last, e_in, e_out, et_in, et_out, f_out, ft_in, pay_in, pay_out):
    zero = place.core == 0
    for low, side_row, row_far, them, far in (
        (False, place.e_in, place.col_in, place.pos_in, place.pos_out),
        (True, place.e_out, place.col_out, place.pos_out, place.pos_in),
    ):
        top = zero if low else jnp.logical_not(zero)
        vals = [jnp.where(top, first[k].astype(F32), last[k].astype(F32)) for k in range(4)]
        inside = jnp.where(top, vals[2], vals[1])
        ahead = jnp.where(top, vals[1], vals[2])
        live = meta[COUNTS + side_row] > 3

        def third(flag):
            return vals[3] * jnp.where(jnp.logical_and(live, flag), 1.0, 0.0)

        is_them, is_far = row_far == them, row_far == far
        own = third(jnp.logical_not(jnp.logical_or(is_them, is_far)))
        e_ref, et_ref = (e_out, et_out) if low else (e_in, et_in)
        for k, v in enumerate((vals[0], inside, own)):
            e_ref[:, k * T : (k + 1) * T] = v.astype(BF)
            et_ref[k * T : (k + 1) * T] = v.T.astype(BF)
        pay = pay_out if low else pay_in
        pay[2, :, :T] = ahead.astype(BF)
        pay[2, :, T:] = third(is_them).astype(BF)
        if low:
            f_out[...] = third(is_far).astype(BF)
            pay_in[3, :, T:] = third(is_far).astype(BF)
        else:
            pay_in[3, :, :T] = third(is_far).astype(BF)
            ft_in[...] = third(is_far).T.astype(BF)


def pick_rows(order, pick):
    lane = lax.broadcasted_iota(jnp.int32, (T, T), 1).astype(F32)
    for j in range(NT):
        wanted = jnp.broadcast_to(order[j : j + 1, :].astype(F32), (T, T)).T
        for k in range(NT):
            pick[j * T : (j + 1) * T, k * T : (k + 1) * T] = (
                (wanted == lane + float(k * T)).astype(F32).astype(BF)
            )


def split_f32(value, ref, start):
    for k in range(3):
        part = value.astype(BF)
        ref[:, start + k * T : start + (k + 1) * T] = part
        value = value - part.astype(F32)


def write_payload(place, own, e_in, e_out, pay_in, pay_out, lanes):
    for e_ref, pay, tiles in (
        (e_in, pay_in, (place.e_in, place.n_in, place.t_in)),
        (e_out, pay_out, (place.e_out, place.n_out, place.t_out)),
    ):
        picked = [tile(own, i)[...].astype(BF) for i in tiles]
        pay[0, :, lanes] = picked[0]
        pay[1, :, lanes] = dot(e_ref[...], jnp.concatenate(picked, axis=0)).astype(BF)


S_LANES, X_LANES = slice(0, T), slice(T, 2 * T)


def rest_kernel(order, in1, in2, cot, x1, x2, c0, c1, c2, pick, parts):
    pick_rows(order, pick)
    for k, src in enumerate((in1[0], in2[0], cot[0], cot[1], cot[2])):
        parts[:, k * T : (k + 1) * T] = src
    for h in range(4):
        rows = slice(h * 256, (h + 1) * 256)
        got = dot(pick[rows], parts[...]).astype(BF)
        for k, out in enumerate((x1, x2, c0, c1, c2)):
            out[rows] = got[:, k * T : (k + 1) * T]


def operator_kernel(meta, vals, vfg, vbg, vbd):
    for r in range(NT):
        live = jnp.where(meta[COUNTS + r] > 3, 1.0, 0.0)
        last = (vals[r, 3].astype(F32) * live).astype(BF)
        vfg[r, :, 0:T] = vals[r, 1]
        vfg[r, :, T : 2 * T] = vals[r, 0]
        vfg[r, :, 2 * T : 3 * T] = vals[r, 2]
        vfg[r, :, 3 * T :] = last
        vbg[r, :, T : 2 * T] = vals[r, 0].T
        if r > 0:
            vbg[r - 1, :, 2 * T :] = vals[r, 1].T
        else:
            vbd[8] = vals[r, 1].T
        if r < NT - 1:
            vbg[r + 1, :, 0:T] = vals[r, 2].T
        else:
            vbd[9] = vals[r, 2].T
        vbd[r] = last.T
    vbg[0, :, 0:T] = jnp.zeros((T, T), BF)
    vbg[NT - 1, :, 2 * T :] = jnp.zeros((T, T), BF)


def turn_kernel(rin, rout, vin, vout, tin, tout, tfar):
    vin[...] = rin[2:]
    vout[...] = rout[2:]
    for k in range(2):
        lanes = slice(k * T, (k + 1) * T)
        tin[:, lanes] = rin[2, :, lanes].astype(F32).T.astype(BF)
        tout[:, lanes] = rout[2, :, lanes].astype(F32).T.astype(BF)
    tfar[...] = rin[3, :, T:].astype(F32).T.astype(BF)


def middle_forward(pay, got, far, out):
    out[0] = pay[0]
    out[1] = (pay[1].astype(F32) + dot(far[...], got[0])).astype(BF)
    if pay.shape[0] > 2:
        out[2] = pay[2]


def middle_back(pay, got, far, out):
    out[0] = (pay[0].astype(F32) + dot(far[...], got[1])).astype(BF)
    out[1] = pay[1]


def forward_row(place, vfg, src, r):
    low = tile(src, place.idx(0, 1))[...] if r == 0 else tile(src, r)[...]
    high = tile(src, place.idx(7, 2))[...] if r == 7 else tile(src, r + 2)[...]
    picked = jnp.concatenate(
        [low, tile(src, r + 1)[...], high, tile(src, place.idx(r, 3))[...]], axis=0
    )
    return dot(vfg[r], picked)


def spread_kernel(meta, *rest, parts, first):
    sources, rest = rest[:parts], rest[parts:]
    if first:
        rin, rout, vfg, *rest = rest
        vin, vout = rin.at[pl.ds(2, 2)], rout.at[pl.ds(2, 1)]
    else:
        rin, rout, vfg, vin, vout, *rest = rest
    zext, d1, near = rest
    place = Place(meta)
    for k, src in enumerate(sources):
        zext[T : T + ROWS, k * T : (k + 1) * T] = src[...].astype(BF)
    tile(zext, place.pos_in)[...] = rin[0]
    tile(zext, place.pos_out)[...] = rout[0]
    for r in range(NT):
        tile(d1, r + 1)[...] = forward_row(place, vfg, zext, r).astype(BF)
    edge = tile(zext, place.e_in + 1)[...]
    near[...] = rin[1].astype(F32) + dot(vin[0], jnp.concatenate([edge, edge], axis=0))
    tile(d1, place.pos_in)[...] = jnp.zeros_like(edge)
    edge = tile(zext, place.e_out + 1)[...]
    total = rout[1].astype(F32) + dot(vout[0], jnp.concatenate([edge, edge], axis=0))
    tile(d1, place.pos_out)[...] = total.astype(BF)


def spread(meta, sources, got, vfg, boundary):
    shape = ((NT + 2) * T, len(sources) * T)
    args = (meta, *sources, *got[:2], vfg, *boundary)
    return run(
        functools.partial(spread_kernel, parts=len(sources), first=not boundary),
        "spread", (0,), args, [(shape, BF), (shape, BF), ((T, shape[1]), F32)],
    )


def complete(place, given, near, far, rfwd, d1):
    d1[...] = given[...]
    tile(d1, place.pos_in)[...] = (near[...] + dot(far, rfwd[0])).astype(BF)


def second_order(place, vfg, zext, d1, r):
    z = tile(zext, r + 1)[...].astype(F32)
    return (2.0 * forward_row(place, vfg, d1, r) - z).astype(BF)


def gate_kernel(
    meta, st, zext, given, near, rfwd, vin, vfg, e_in, e_out, gw, gb,
    feats, r_out, q_out, pay_in, pay_out, d1, *, first
):
    place = Place(meta)
    complete(place, given, near, vin[3 if first else 1, :, :T], rfwd, d1)
    for r in range(NT):
        d2 = second_order(place, vfg, zext, d1, r)
        z = tile(zext, r + 1)[...]
        one = tile(d1, r + 1)[...]
        row = jnp.concatenate(
            [z[:, T:], one[:, T:], d2[:, T:], z[:, :T], one[:, :T], d2[:, :T]], axis=1
        )
        tile(feats, r)[...] = row
    for h in range(4):
        rows = slice(h * 256, (h + 1) * 256)
        reset = jax.nn.sigmoid(dot(feats[rows], gw[:, :T]) + gb[:, :T])
        r_out[rows] = reset
        q_out[rows] = (reset * st[rows]).astype(BF)
    write_payload(place, q_out, e_in, e_out, pay_in, pay_out, S_LANES)


def update_kernel(feats, gw, gb, cw, cb, u_out, xc_out):
    for h in range(4):
        rows = slice(h * 256, (h + 1) * 256)
        f = feats[rows]
        u_out[rows] = jax.nn.sigmoid(dot(f, gw[:, T:]) + gb[:, T:])
        xc_out[rows] = dot(f[:, : 3 * T], cw[: 3 * T]) + cb[...]


def cand_kernel(
    meta, zext, given, near, rfwd, vin, vfg, e_in, e_out, cw, xc, u, st, *rest, last
):
    if last:
        fq, c_out, d1 = rest
    else:
        x_next, fq, c_out, st_out, pay_in, pay_out, d1 = rest
    place = Place(meta)
    complete(place, given, near, vin[1, :, :T], rfwd, d1)
    for r in range(NT):
        d2 = second_order(place, vfg, zext, d1, r)
        tile(fq, r)[...] = jnp.concatenate(
            [tile(zext, r + 1)[...], tile(d1, r + 1)[...], d2], axis=1
        )
    for h in range(4):
        rows = slice(h * 256, (h + 1) * 256)
        cand = jnp.tanh(dot(fq[rows], cw[3 * T :]) + xc[rows])
        c_out[rows] = cand
        if not last:
            st_out[rows] = u[rows] * st[rows] + (1.0 - u[rows]) * cand
    if not last:
        write_payload(place, st_out, e_in, e_out, pay_in, pay_out, S_LANES)
        write_payload(place, x_next, e_in, e_out, pay_in, pay_out, X_LANES)


def collect_kernel(meta, *rest, parts):
    sources, (rin, rout, et_in, et_out, acc) = rest[:parts], rest[parts:]
    place = Place(meta)
    for k, src in enumerate(sources):
        acc[:, k * T : (k + 1) * T] = src[...]
    got_in = dot(et_in[...], rin[1])
    got_out = dot(et_out[...], rout[1])
    for i, block in (
        (place.e_in, got_in[:T] + rin[0].astype(F32)),
        (place.n_in, got_in[T : 2 * T]),
        (place.t_in, got_in[2 * T :]),
        (place.e_out, got_out[:T] + rout[0].astype(F32)),
        (place.n_out, got_out[T : 2 * T]),
        (place.t_out, got_out[2 * T :]),
    ):
        tile(acc, i)[...] += block


def collect(meta, sources, got, et_in, et_out):
    return run(
        functools.partial(collect_kernel, parts=len(sources)), "collect", (0,),
        (meta, *sources, *got[:2], et_in, et_out), [((ROWS, len(sources) * T), F32)],
    )[0]


def add_far(place, acc, given, rfwd, tfar):
    acc[...] = given[...]
    tile(acc, place.e_in)[...] += dot(tfar[...], rfwd[1])


def back_rows(place, vbg, vbd, y, acc, base):
    zero = jnp.zeros((T, acc.shape[1]), F32)
    tile(acc, 0)[...] = zero
    tile(acc, 9)[...] = zero
    for r in range(NT):
        lo, hi = max(r - 1, 0), min(r + 2, NT)
        lhs = vbg[r, :, (lo - r + 1) * T : (hi - r + 1) * T]
        tile(acc, r + 1)[...] = base(r, dot(lhs, y[lo * T : hi * T]))
    parts = [(place.idx(0, 1), 8, 0), (place.idx(7, 2), 9, 7)]
    parts += [(place.idx(r, 3), r, r) for r in range(NT)]
    for i, k, r in parts:
        tile(acc, i)[...] += dot(vbd[k], y[r * T : (r + 1) * T])


def diffuse_back(place, vbg, vbd, tin, tout, a, y, w, acc, pay_in, pay_out):
    for r in range(NT):
        rows = slice(r * T, (r + 1) * T)
        y[rows] = a(2, rows).astype(BF)
    back_rows(
        place, vbg, vbd, y, acc, lambda r, v: a(1, slice(r * T, (r + 1) * T)) * 0.5 + v
    )
    for e in range(NT + 2):
        tile(w, e)[...] = (2.0 * tile(acc, e)[...]).astype(BF)
    own = w.at[pl.ds(T, ROWS)]

    def second(r, v):
        rows = slice(r * T, (r + 1) * T)
        return a(0, rows) - a(2, rows) + v

    back_rows(place, vbg, vbd, own, acc, second)
    for pos, edge, vals, pay in (
        (place.pos_in, place.e_in, tin, pay_in),
        (place.pos_out, place.e_out, tout, pay_out),
    ):
        part = tile(w, pos)[...]
        tile(acc, edge + 1)[...] += dot(vals[...], jnp.concatenate([part, part], axis=0))
        pay[0] = tile(acc, pos)[...].astype(BF)
        pay[1] = part


def cand_back_kernel(*refs, first):
    refs = list(refs)
    take = lambda n: [refs.pop(0) for _ in range(n)]
    meta, cot, u, c, st, cw, vbg, vbd, tin, tout, tfar = take(11)
    if not first:
        given, rfwd = take(2)
    gp_out, ec_out, eu_out, gq_out, sums, pay_in, pay_out = take(7)
    if not first:
        (gx_out,) = take(1)
    gs, g, y, w, acc = take(5)
    place = Place(meta)
    if not first:
        add_far(place, gs, given, rfwd, tfar)
        gx_out[...] = gs[:, T:].astype(BF)
    sum_c = jnp.zeros((1, T), F32)
    sum_u = jnp.zeros((1, T), F32)
    for h in range(NT):
        rows = slice(h * T, (h + 1) * T)
        grad = cot[rows].astype(F32)
        if not first:
            grad = grad + gs[rows, :T]
        upd, cand = u[rows], c[rows]
        pre = grad * (1.0 - upd) * (1.0 - cand * cand)
        gate = grad * (st[rows] - cand) * upd * (1.0 - upd)
        gp_out[rows] = grad * upd
        ec_out[rows] = pre.astype(BF)
        eu_out[rows] = gate.astype(BF)
        sum_c = sum_c + jnp.sum(pre, axis=0, keepdims=True)
        sum_u = sum_u + jnp.sum(gate, axis=0, keepdims=True)
    sums[...] = jnp.broadcast_to(jnp.concatenate([sum_c, sum_u], axis=1), (8, 2 * T))
    g[...] = dot_nt(ec_out[...], cw[3 * T :])
    diffuse_back(
        place, vbg, vbd, tin, tout,
        lambda k, rows: g[rows, k * T : (k + 1) * T],
        y, w, acc, pay_in, pay_out,
    )
    gq_out[...] = acc[T : T + ROWS]


def gate_back_kernel(
    meta, given, rfwd, gp, r_ref, st, ec, eu, gw, cw, vbg, vbd, tin, tout, tfar,
    gs_out, gx_out, er_out, sums, pay_in, pay_out, gq, eg, gps, g, y, w, acc,
):
    place = Place(meta)
    add_far(place, gq, given, rfwd, tfar)
    sum_r = jnp.zeros((1, T), F32)
    for h in range(NT):
        rows = slice(h * T, (h + 1) * T)
        grad, reset = gq[rows], r_ref[rows]
        gps[rows] = gp[rows] + grad * reset
        pre = grad * st[rows] * reset * (1.0 - reset)
        eg[rows, :T] = pre.astype(BF)
        sum_r = sum_r + jnp.sum(pre, axis=0, keepdims=True)
    eg[:, T:] = eu[...]
    er_out[...] = eg[:, :T]
    sums[...] = jnp.broadcast_to(sum_r, (8, T))
    e = eg[...]
    for k in range(3):
        cols = slice(2 * k * T, (2 * k + 1) * T)
        g[:, cols] = dot_nt(e, gw[(3 + k) * T : (4 + k) * T])
        cols = slice((2 * k + 1) * T, (2 * k + 2) * T)
        g[:, cols] = dot_nt(e, gw[k * T : (k + 1) * T]) + dot_nt(
            ec[...], cw[k * T : (k + 1) * T]
        )
    diffuse_back(
        place, vbg, vbd, tin, tout,
        lambda k, rows: g[rows, 2 * k * T : 2 * (k + 1) * T],
        y, w, acc, pay_in, pay_out,
    )
    gs_out[...] = acc[T : T + ROWS, :T] + gps[...]
    gx_out[...] = acc[T : T + ROWS, T:]


def add_rows(out, value, rest, rows):
    out[rows] = value + rest[0][rows] if rest else value


def split_columns(meta, total, kept, sent):
    half = total.shape[1] // 2
    mine = meta[32] == 0
    low, high = total[:, :half], total[:, half:]
    kept[...] = jnp.where(mine, low, high)
    sent[...] = jnp.where(mine, high, low).astype(BF)


def weight_cu_kernel(meta, ec, eu, sums, feats, fq, *rest):
    *rest, out = rest
    x = feats[:, : 3 * T]
    both = jnp.concatenate([dot_tn(ec[...], x), dot_tn(ec[...], fq[...])], axis=1)
    add_rows(out, both, rest, slice(0, T))
    add_rows(out, dot_tn(eu[...], feats[...]), rest, slice(T, 2 * T))
    row = jnp.concatenate([sums[...], jnp.zeros((8, 4 * T), F32)], axis=1)
    add_rows(out, jnp.concatenate([row] * 4, axis=0), rest, slice(2 * T, 2 * T + 32))


def weight_cu_last_kernel(meta, ec, eu, sums, feats, fq, before, kept, sent, out):
    weight_cu_kernel(meta, ec, eu, sums, feats, fq, before, out)
    split_columns(meta, out, kept, sent)


def weight_r_kernel(meta, er, sums, feats, *rest):
    *rest, out = rest
    add_rows(out, dot_tn(er[...], feats[...]), rest, slice(0, T))
    row = jnp.concatenate([sums[...], jnp.zeros((8, 5 * T), F32)], axis=1)
    add_rows(out, jnp.concatenate([row, row], axis=0), rest, slice(T, T + 16))


def weight_r_last_kernel(meta, er, sums, feats, before, kept, sent, out):
    weight_r_kernel(meta, er, sums, feats, before, out)
    split_columns(meta, out, kept, sent)


def add_kernel(a, b, out):
    out[...] = (a[...].astype(F32) + b[...].astype(F32)).astype(BF)


def add_split_kernel(meta, a, b, kept, sent):
    total = (a[...].astype(F32) + b[...].astype(F32)).astype(BF)
    half = total.shape[0] // 2
    upper = meta[33] == 1
    top, bottom = total[:half].astype(F32), total[half:].astype(F32)
    kept[...] = jnp.where(upper, bottom, top).astype(BF)
    sent[...] = jnp.where(upper, top, bottom).astype(BF)


def sum_of(a, b):
    return run(add_kernel, "add", (), (a, b), [(a.shape, BF)])[0]


def reduce_step(part, step):
    count = lax.axis_size("wide")
    other = lax.ppermute(part, "wide", [(i, i ^ step) for i in range(count)])
    return sum_of(part, other)


def reduce_rows(kept, sent):
    count = lax.axis_size("wide")
    route = [(i, i ^ 2) for i in range(count)]
    part = sum_of(kept, lax.ppermute(sent, "wide", route))
    step = 4
    while step < count:
        part = reduce_step(part, step)
        step *= 2
    return part, lax.ppermute(part, "wide", route)


def reduce_rest(part, step):
    while step < lax.axis_size("wide"):
        part = reduce_step(part, step)
        step *= 2
    return part, swap_in(part)


def weights_kernel(
    meta, cu_a, cu_b, cu_a_other, cu_b_other, r_own, r_other, gw, gb, cw, cb, *, scale
):
    mine = meta[32] == 0
    upper = meta[33] == 1

    def pick(own, other, side):
        a, b = own[...].astype(F32), other[...].astype(F32)
        return jnp.where(mine, a, b) if side == 0 else jnp.where(mine, b, a)

    def rows_of(a, b):
        low, high = jnp.where(upper, b, a), jnp.where(upper, a, b)
        return jnp.concatenate([low, high], axis=0)

    for side in range(2):
        cu = rows_of(pick(cu_a, cu_a_other, side), pick(cu_b, cu_b_other, side)) * scale
        r = pick(r_own, r_other, side) * scale
        for k in range(3):
            cols = slice(k * T, (k + 1) * T)
            rows = slice((3 * side + k) * T, (3 * side + k + 1) * T)
            cw[rows] = cu[:T, cols].T
            gw[rows, T:] = cu[T : 2 * T, cols].T
            gw[rows, :T] = r[:T, cols].T
        if side == 0:
            cb[...] = cu[2 * T : 2 * T + 1, :T]
            gb[:, T:] = cu[2 * T : 2 * T + 1, T : 2 * T]
            gb[:, :T] = r[T : T + 1, :T]


def finish_kernel(
    meta, order, given, rfwd, tfar, gx1, gx2,
    gi_out, gs_out, gs, parts,
):
    place = Place(meta)
    add_far(place, gs, given, rfwd, tfar)
    split_f32(gs[:, :T], parts, 0)
    parts[:, 3 * T : 4 * T] = gs[:, T:].astype(BF)
    parts[:, 4 * T : 5 * T] = gx1[...]
    parts[:, 5 * T :] = gx2[...]
    row = lax.broadcasted_iota(jnp.int32, (T, T), 0)
    for k in range(NT):
        put = jnp.concatenate(
            [
                (jnp.broadcast_to(order[j : j + 1, :], (T, T)) == row + k * T)
                .astype(F32)
                .astype(BF)
                for j in range(NT)
            ],
            axis=1,
        )
        rows = slice(k * T, (k + 1) * T)
        got = dot(put, parts[...])
        gs_out[rows] = got[:, :T] + got[:, T : 2 * T] + got[:, 2 * T : 3 * T]
        for t in range(3):
            gi_out[t, rows] = got[:, (3 + t) * T : (4 + t) * T].astype(BF)


SMEM = pl.BlockSpec(memory_space=pltpu.SMEM)
VMEM = pl.BlockSpec(memory_space=pltpu.VMEM)


HBM = pl.BlockSpec(memory_space=pltpu.HBM)


def run(
    kernel, name, smem, args, outs, scratch=(), specs=None, flops=10**8,
    hbm=(), smem_outs=(), sems=0,
):
    grid = (1,) if specs else ()
    specs = specs or [
        SMEM if i in smem else HBM if i in hbm else VMEM for i in range(len(args))
    ]
    out_shape = [jax.ShapeDtypeStruct(s, d) for s, d in outs]
    args = [
        pltpu.with_memory_space_constraint(x, pltpu.HBM) if i in hbm else x
        for i, x in enumerate(args)
    ]
    moved = sum(math.prod(x.shape) * x.dtype.itemsize for x in (*args, *out_shape))
    return pl.pallas_call(
        kernel,
        name=name,
        grid=grid,
        in_specs=specs,
        out_specs=[SMEM if i in smem_outs else VMEM for i in range(len(outs))],
        out_shape=out_shape,
        scratch_shapes=[pltpu.VMEM(*s) if isinstance(s, tuple) else s for s in scratch]
        + ([pltpu.SemaphoreType.DMA((sems,))] if sems else []),
        cost_estimate=pl.CostEstimate(flops=flops, bytes_accessed=moved, transcendentals=0),
        compiler_params=pltpu.CompilerParams(vmem_limit_bytes=VMEM_LIMIT),
    )(*args)


def leading(block, at):
    zeros = (0,) * (len(block) - 1)
    return pl.BlockSpec(block, lambda i: (at,) + zeros, memory_space=pltpu.VMEM)


def per_device(
    inputs, state_init, cotangent, gate_w, gate_b, cand_w, cand_b,
    tile_vals, tile_cols, tile_counts, sector_order,
):
    order = sector_order.reshape(NT, T)
    gb = gate_b.reshape(1, -1)
    cb = cand_b.reshape(1, -1)
    big = (ROWS, T)
    square = (T, T)
    flat, tall = ((T, 3 * T), BF), ((3 * T, T), BF)
    x_block = (1, ROWS, T)
    device = lax.axis_index("wide").astype(jnp.int32).reshape(1)
    meta, e_in, e_out, et_in, et_out, f_out, ft_in, x0, st, *pay = run(
        start_kernel, "start", (0,),
        (device, tile_cols.T, tile_counts, tile_vals, order, inputs, state_init),
        [((COUNTS + NT,), jnp.int32), flat, flat, tall, tall, (square, BF), (square, BF)]
        + [(big, BF), (big, F32), ((4, T, 2 * T), BF), ((3, T, 2 * T), BF)],
        [
            pltpu.SMEM((4, NT), jnp.int32), pltpu.SMEM((NT,), jnp.int32),
            ((4, T, T), BF), ((4, T, T), BF), ((NT, T), jnp.int32), (big, BF), (big, F32),
            ((ROWS, ROWS), BF), ((ROWS, 4 * T), BF),
        ],
        hbm=(1, 2, 3, 4, 5, 6), sems=7, smem_outs=(0,), flops=10**9,
    )
    vfg, vbg, vbd = run(
        operator_kernel, "operator", (0,), (meta, tile_vals),
        [((NT, T, 4 * T), BF), ((NT, T, 3 * T), BF), ((NT + 2, T, T), BF)],
    )
    x1, x2, *cots = run(
        rest_kernel, "rest", (), (order, inputs, inputs, cotangent), [(big, BF)] * 5,
        [((ROWS, ROWS), BF), ((ROWS, 5 * T), BF)],
        specs=[VMEM, leading(x_block, 1), leading(x_block, 2), VMEM],
        flops=10**9,
    )
    saved = []
    steps = inputs.shape[0]
    wide = ((NT + 2) * T, 2 * T)
    slim = ((NT + 2) * T, T)
    beside = (vfg, vbg, vbd)
    for t in range(steps):
        last = t == steps - 1
        got, beside = exchange(*pay, f_out, middle_forward, beside)
        if t == 0:
            vfg, vbg, vbd = beside
            turned = run(
                turn_kernel, "turn", (), got[:2],
                [((2, T, 2 * T), BF), ((1, T, 2 * T), BF)] + [((T, 2 * T), BF)] * 2
                + [(square, BF)],
            )
            xs = (x0,)
        boundary = () if t == 0 else (vin, vout)
        terms = spread(meta, (st, xs[t]), got, vfg, boundary)
        feats, r, q, *pay = run(
            functools.partial(gate_kernel, first=t == 0),
            "gate",
            (0,),
            (meta, st, *terms, got[2], got[0] if t == 0 else vin, vfg, e_in, e_out, gate_w, gb),
            [((ROWS, 6 * T), BF), (big, F32), (big, BF)] + [((2, T, T), BF)] * 2,
            [(wide, BF)],
        )
        beside = tuple(run(
            update_kernel,
            "update",
            (),
            (feats, gate_w, gb, cand_w, cb),
            [(big, F32)] * 2,
            flops=5 * 10**8,
        ))
        if t == 0:
            beside += (x1, x2, *cots, *turned)
        got, (u, xc, *beside) = exchange(*pay, f_out, middle_forward, beside)
        if t == 0:
            xs += tuple(beside[:2])
            cots = beside[2:5]
            vin, vout, tin, tout, tfar = beside[5:]
        terms = spread(meta, (q,), got, vfg, (vin, vout))
        fq, c, *rest = run(
            functools.partial(cand_kernel, last=last),
            "cand",
            (0,),
            (meta, *terms, got[2], vin, vfg, e_in, e_out, cand_w, xc, u, st) + (() if last else (xs[t + 1],)),
            [((ROWS, 3 * T), BF), (big, F32)]
            + ([] if last else [(big, F32)] + [((2, T, 2 * T), BF)] * 2),
            [(slim, BF)],
        )
        saved.append((st, r, u, c, feats, fq))
        if not last:
            st, *pay = rest
            beside = ()
    ops = (vbg, vbd, tin, tout, tfar)
    gxs = [None] * steps
    carry, cu_sum, r_sum = (), (), ()
    for t in reversed(range(steps)):
        st, r, u, c, feats, fq = saved[t]
        first = t == steps - 1
        gp, ec, eu, gq, sums, *rest = run(
            functools.partial(cand_back_kernel, first=first),
            "cand_back",
            (0,),
            (meta, cots[t], u, c, st, cand_w) + ops + carry,
            [(big, F32), (big, BF), (big, BF), (big, F32), ((8, 2 * T), F32)]
            + [((2, T, T), BF)] * 2
            + ([] if first else [(big, BF)]),
            [((ROWS, 2 * T), F32), ((ROWS, 3 * T), F32), (big, BF), (slim, BF), (slim, F32)],
        )
        if not first:
            gxs[t + 1] = rest[2]
        last = t == 0
        rows, columns = 2 * T + 32, 6 * T
        args = (meta, ec, eu, sums, feats, fq, *cu_sum)
        if not last:
            cu_sum = run(
                weight_cu_kernel, "weight_cu", (0,), args, [((rows, columns), F32)],
                flops=4 * 10**8,
            )
        else:
            kept, sent = run(
                weight_cu_last_kernel, "weight_cu", (0,), args,
                [((rows, columns // 2), F32), ((rows, columns // 2), BF)],
                [((rows, columns), F32)], flops=4 * 10**8,
            )
            cu_sum = run(
                add_split_kernel, "add_split", (0,), (meta, kept, swap_in(sent)),
                [((rows // 2, columns // 2), BF)] * 2,
            )
        got, cu_sum = exchange(*rest[:2], ft_in, middle_back, cu_sum)
        gs_part, gx_part, er, sums, *rest = run(
            gate_back_kernel,
            "gate_back",
            (0,),
            (meta, collect(meta, (gq,), got, et_in, et_out), got[2], gp, r, st, ec, eu, gate_w, cand_w) + ops,
            [(big, F32), (big, F32), (big, BF), ((8, T), F32)] + [((2, T, 2 * T), BF)] * 2,
            [
                (big, F32), ((ROWS, 2 * T), BF), (big, F32), ((ROWS, 6 * T), F32),
                ((ROWS, 2 * T), BF), (wide, BF), (wide, F32),
            ],
        )
        args = (meta, er, sums, feats, *r_sum)
        rows = T + 16
        if not last:
            r_sum = run(
                weight_r_kernel, "weight_r", (0,), args, [((rows, columns), F32)],
                flops=2 * 10**8,
            )
            got, r_sum = exchange(*rest, ft_in, middle_back, r_sum)
        else:
            kept, sent = run(
                weight_r_last_kernel, "weight_r", (0,), args,
                [((rows, columns // 2), F32), ((rows, columns // 2), BF)],
                [((rows, columns), F32)], flops=2 * 10**8,
            )
            r_part = sum_of(kept, swap_in(sent))
            rest, r_part = lax.optimization_barrier((rest, r_part))
            got, _ = exchange(*rest, ft_in, middle_back)
        carry = (collect(meta, (gs_part, gx_part), got, et_in, et_out), got[2])
    cu = reduce_rows(*cu_sum)
    rr = reduce_rest(r_part, 2)
    gi, gs = run(
        finish_kernel,
        "finish",
        (0,),
        (meta, order, *carry, tfar, gxs[1], gxs[2]),
        [((steps,) + big, BF), (big, F32)],
        [((ROWS, 2 * T), F32), ((ROWS, 6 * T), BF)],
    )
    gi, gs, cu = lax.optimization_barrier((gi, gs, cu))
    cu = (*cu, *[swap_in(x) for x in cu])
    scale = 1.0 / math.sqrt(ROWS * lax.axis_size("wide") * steps)
    gw, gb, cw, cb = run(
        functools.partial(weights_kernel, scale=scale),
        "weights",
        (0,),
        (meta, *cu, *rr),
        [((6 * T, 2 * T), F32), ((1, 2 * T), F32), ((6 * T, T), F32), ((1, T), F32)],
    )
    return gi, gs, gw, gb.reshape(-1), cw, cb.reshape(-1)


def solution(mesh):
    return jax.shard_map(
        per_device,
        mesh=mesh,
        in_specs=(
            P(None, ("parts", "wide"), None),
            P(("parts", "wide"), None),
            P(None, ("parts", "wide"), None),
            P(),
            P(),
            P(),
            P(),
            P(("parts", "wide"), None, None, None),
            P(("parts", "wide"), None),
            P(("parts", "wide")),
            P(("parts", "wide")),
        ),
        out_specs=(
            P(None, ("parts", "wide"), None),
            P(("parts", "wide"), None),
            P("parts", None),
            P("parts"),
            P("parts", None),
            P("parts"),
        ),
        check_vma=False,
    )
```
